32 devices in a mesh: group: 2 (over y), gx: 4 (over z), gz: 2 (over x), col: 2 (over core).
Axes of the slice: x: 2, y: 2, z: 4, core: 2. Of those that a mesh axis runs over, the one named last changes fastest.
Arguments:
- features: bfloat16 [32, 64, 16, 256], P(None, 'col', ('group', 'gx'), 'gz'), parts along dimension 2, may hold values from -6 to 6
- labels: int32 [64, 16, 256], P(None, ('group', 'gx'), 'gz'), parts along dimension 1, may hold values from 0 to 3
- grid_index: int32 [64], replicated, may hold values from 0 to 15
- stretch: float32 [16, 9], replicated, may hold values from 0.5 to 2
- tile_filter: float32 [32, 25], replicated, may hold values from -1.25 to 1.25
- wall_filter: float32 [32, 9], replicated, may hold values from -2 to 2
- class_weight: float32 [4, 32], replicated, may hold values from -1 to 1
Outputs:
- grad_features: bfloat16 [32, 64, 16, 256], P(None, 'col', ('group', 'gx'), 'gz'), parts along dimension 2
- grad_tile_filter: float32 [64, 25], P('group'), parts along dimension 0
- grad_wall_filter: float32 [64, 9], P('group'), parts along dimension 0
- grad_class_weight: float32 [8, 32], P('group'), parts along dimension 0
The draws below stay inside these ranges and needn't reach their ends.
There are 2 independent parts, one for each index of `group`. The reference program is written for one: setup_inputs(seed, part) draws one part's arguments, and reference() takes and returns one part's arrays. A program takes and returns all parts, laid end to end along the dimension named above; an argument that names none is the same for every part. Nothing has to cross between parts.
All inputs are finite; a program needn't handle non-finite values.
Results may differ from the reference program's by a relative error of at most 0.0064.
Values may be sent and summed in bfloat16 or wider, within the bound.
No kernel may reach another device: no remote copies, remote signals or barrier semaphores. Data moves between devices by JAX's collectives and lax.ppermute only.
A program may use at most 64 MiB of HBM per device.

```python
import math
import jax
import jax.numpy as jnp
from jax import lax

C = 32
K = 4
L = 16
NY = 64
NX = 8
NZ = 256


def with_ends(entries, own_key, low, largest):
    longest = entries.shape.index(max(entries.shape))
    spots = []
    for shift in (0, 1):
        where = [jax.random.randint(jax.random.fold_in(own_key, axis), (), 0, length) for axis, length in enumerate(entries.shape)]
        where[longest] = (where[longest] + shift) % entries.shape[longest]
        spots.append(tuple(where))
    return entries.at[spots[0]].set(low).at[spots[1]].set(largest)


def block_levels(own_key, shape, shards, low, high):
    loudness, own = 1.0, jax.random.fold_in(own_key, 6)
    for position, parts in shards:
        draws = jnp.exp(jax.random.uniform(jax.random.fold_in(own, position), (parts,), jnp.float32, low / len(shards), high / len(shards)))
        loudness = loudness * jnp.repeat(draws, shape[position] // parts).reshape([-1 if axis == position else 1 for axis in range(len(shape))])
    return loudness


def centred(stream_key, shape, deviation, reach, cuts=(), kind=jnp.bfloat16):
    level = block_levels(stream_key, shape, cuts, -0.22, 0.18) if cuts else 1.0
    values = jax.random.normal(stream_key, shape, jnp.float32) * deviation * level
    return jnp.minimum(jnp.maximum(values, -reach), reach).astype(kind)


def setup_inputs(seed: int = 0, part: int = 0) -> dict:
    splits = jax.random.split(jax.random.key(seed), 8)
    part_splits = jax.random.split(jax.random.fold_in(splits[7], part), 8)
    features = centred(part_splits[0], (C, NY, NX, NZ), 1.0, 6.0, ((1, 2), (2, 4), (3, 2)))
    labels = with_ends(jax.random.randint(part_splits[1], (NY, NX, NZ), 0, K), jax.random.fold_in(part_splits[1], 1), 0, K - 1).astype(jnp.int32)
    grid_index = with_ends(jax.random.randint(splits[2], (NY,), 0, L), jax.random.fold_in(splits[2], 1), 0, L - 1).astype(jnp.int32)
    stretch = jnp.clip(jnp.exp(jax.random.uniform(splits[3], (L, 9), jnp.float32, math.log(0.5), math.log(2.0))), 0.5, 2.0)
    tile_filter = centred(splits[4], (C, 25), 25 ** -0.5, 1.25, (), jnp.float32)
    wall_filter = centred(splits[5], (C, 9), 9 ** -0.5, 2.0, (), jnp.float32)
    class_weight = centred(splits[6], (K, C), C ** -0.5, 1.0, (), jnp.float32)
    return dict(features=features, labels=labels, grid_index=grid_index, stretch=stretch, tile_filter=tile_filter, wall_filter=wall_filter, class_weight=class_weight)


def band_table(grid_index, stretch):
    levels = stretch.shape[0]
    onehot = (grid_index[:, None] == jnp.arange(levels, dtype=jnp.int32)[None, :]).astype(jnp.float32)
    return jnp.dot(onehot, stretch, precision=lax.Precision.HIGHEST)


def channel_forward(field, tile_row, wall_row, bands):
    rows = field.shape[0]
    values = field.astype(jnp.float32)
    smooth = jnp.zeros(values.shape, jnp.float32)
    for i in range(5):
        for j in range(5):
            smooth = smooth + tile_row[5 * i + j] * jnp.roll(values, (2 - i, 2 - j), axis=(1, 2))
    smoothed = smooth.astype(jnp.bfloat16)
    padded = jnp.pad(smoothed.astype(jnp.float32), ((4, 4), (0, 0), (0, 0)))
    wall_out = jnp.zeros(values.shape, jnp.float32)
    for k in range(9):
        tap = wall_row[k] * bands[:, k]
        wall_out = wall_out + tap[:, None, None] * padded[k:k + rows]
    return values, padded, wall_out


def reference(features, labels, grid_index, stretch, tile_filter, wall_filter, class_weight):
    classes = class_weight.shape[0]
    rows = features.shape[1]
    volume = features.shape[1] * features.shape[2] * features.shape[3]
    bands = band_table(grid_index, stretch)
    bands_pad = jnp.pad(bands, ((4, 4), (0, 0)))

    def forward_step(total, items):
        field, tile_row, wall_row, class_col = items
        values, padded, wall_out = channel_forward(field, tile_row, wall_row, bands)
        hidden = wall_out * jax.nn.sigmoid(wall_out)
        return total + class_col[:, None, None, None] * hidden[None], None

    start = jnp.zeros((classes,) + features.shape[1:], jnp.float32)
    scores, unused = lax.scan(forward_step, start, (features, tile_filter, wall_filter, class_weight.T))
    targets = (labels[None] == jnp.arange(classes, dtype=jnp.int32)[:, None, None, None]).astype(jnp.float32)
    errors = scores - targets

    def backward_step(carry, items):
        field, tile_row, wall_row, class_col = items
        values, padded, wall_out = channel_forward(field, tile_row, wall_row, bands)
        sig = jax.nn.sigmoid(wall_out)
        hidden = wall_out * sig
        grad_hidden = jnp.einsum('k,kyxz->yxz', class_col, errors, precision=lax.Precision.HIGHEST)
        grad_wall = (grad_hidden * sig * (1.0 + wall_out * (1.0 - sig))).astype(jnp.bfloat16)
        class_grad = jnp.einsum('kyxz,yxz->k', errors, hidden, precision=lax.Precision.HIGHEST)
        wall_vals = grad_wall.astype(jnp.float32)
        wall_grad = jnp.stack([jnp.sum(wall_vals * bands[:, k][:, None, None] * padded[k:k + rows]) for k in range(9)])
        wall_pad = jnp.pad(wall_vals, ((4, 4), (0, 0), (0, 0)))
        back = jnp.zeros(values.shape, jnp.float32)
        for k in range(9):
            first = 8 - k
            tap = wall_row[k] * bands_pad[first:first + rows, k]
            back = back + tap[:, None, None] * wall_pad[first:first + rows]
        grad_smooth = back.astype(jnp.bfloat16).astype(jnp.float32)
        grad_field = jnp.zeros(values.shape, jnp.float32)
        tile_grad = []
        for i in range(5):
            for j in range(5):
                grad_field = grad_field + tile_row[5 * i + j] * jnp.roll(grad_smooth, (i - 2, j - 2), axis=(1, 2))
                tile_grad.append(jnp.sum(jnp.roll(values, (2 - i, 2 - j), axis=(1, 2)) * grad_smooth))
        return carry, (grad_field.astype(jnp.bfloat16), jnp.stack(tile_grad), wall_grad, class_grad)

    unused, outs = lax.scan(backward_step, jnp.zeros((), jnp.float32), (features, tile_filter, wall_filter, class_weight.T))
    grad_features, tile_grads, wall_grads, class_grads = outs
    return grad_features, tile_grads / volume, wall_grads / volume, class_grads.T / volume
```

```python
import functools

import jax
import jax.numpy as jnp
from jax import lax
from jax.experimental import pallas as pl
from jax.experimental.pallas import tpu as pltpu
from jax.sharding import PartitionSpec as P

LANES = 128
TAPS = 5
REACH = 2
EDGE = 4
WALL = 9
WALL_HALO = 8
ROW_WALL = TAPS * TAPS
ROW_CLASS = ROW_WALL + WALL
CENTRE = ROW_WALL // 2
F32, BF16 = jnp.float32, jnp.bfloat16


class Plan:
    def __init__(self, ring, chans, rows, cells_x, cells_z, classes):
        self.ring, self.chans, self.rows, self.cells_x = ring, chans, rows, cells_x
        self.classes = classes
        self.window = cells_z // ring
        self.block = self.window + 2 * EDGE
        self.per = LANES // self.block
        self.slots = chans + 1
        self.groups = self.slots // self.per
        self.xs = ring * cells_x
        self.packs = chans // ring
        self.reach_rows = rows + 2 * (WALL_HALO // 2)
        self.edge_slots = LANES // (2 * EDGE)
        self.edge_groups = -(-self.slots // self.edge_slots)
        self.table_rows = -(-(ROW_CLASS + classes) // 8) * 8


def fits(ring, gz, col, chans, rows, cells_x, cells_z, classes):
    if cells_z != LANES or cells_x != 2 or col != 2 or ring < 2 or ring > 4 or LANES % ring:
        return False
    block = LANES // ring + 2 * EDGE
    per = LANES // block
    return (chans + 1) % per == 0 and chans % ring == 0 and rows % 16 == 0 and ring * cells_x >= TAPS


def vmem(count):
    return [pl.BlockSpec(memory_space=pltpu.VMEM)] * count


def call(body, outs, args, scratch=()):
    return pl.pallas_call(
        body,
        out_shape=outs,
        in_specs=vmem(len(args)),
        out_specs=vmem(len(outs)),
        scratch_shapes=list(scratch),
        compiler_params=pltpu.CompilerParams(vmem_limit_bytes=40 * 2**20),
    )(*args)


def lane_of(rows):
    return lax.broadcasted_iota(jnp.int32, (rows, LANES), 1)


def edge_body(p, field, labels, out):
    core = lax.axis_index("col")
    tall = p.rows * p.cells_x
    lane = lane_of(tall)

    def group(g, count, fetch):
        total = jnp.zeros((tall, LANES), F32)
        for e in range(count):
            moved = pltpu.roll(fetch(g * p.edge_slots + e), (2 * EDGE * e + EDGE) % LANES, 1)
            total = jnp.where(lane // (2 * EDGE) == e, moved, total)
        out[g] = total.astype(BF16)

    def step(g, carry):
        group(g, p.edge_slots, lambda c: field[c].astype(F32))
        return carry

    full = p.chans // p.edge_slots
    lax.fori_loop(0, full, step, 0)
    own = labels[pl.ds(pl.multiple_of(core * tall, 8), tall), :].astype(F32)
    group(full, p.slots - full * p.edge_slots, lambda c: own)


def pack_body(p, cuts, field, labels, left, right, *refs):
    outs, stage = refs[:-1], refs[-1]
    ring = p.ring
    me, core = lax.axis_index("gx"), lax.axis_index("col")
    tall = p.rows * p.cells_x
    lane = lane_of(tall)
    takes = [lax.rem(me + d, ring) for d in range(ring)]
    fixes = [
        ((lane >= LANES - EDGE) & (k == 0)) | ((lane < EDGE) & (k == ring - 1)) for k in takes
    ]
    older = lane % (2 * EDGE) < EDGE

    def edges(c):
        g, e = c // p.edge_slots, c % p.edge_slots
        both = jnp.where(older, left[g].astype(F32), right[g].astype(F32))
        return pltpu.roll(both, LANES - EDGE - 2 * EDGE * e, 1)

    def group(cg, fetch, chunk, first):
        values = [fetch(cg * p.per + b) for b in range(p.per)]
        rims = [edges(cg * p.per + b) for b in range(p.per)]
        for d in range(ring):
            total = jnp.zeros((tall, LANES), F32)
            for b in range(p.per):
                shift = lax.rem(2 * LANES + p.block * b + EDGE - p.window * takes[d], LANES)
                moved = pltpu.roll(jnp.where(fixes[d], rims[b], values[b]), shift, 1)
                total = jnp.where(lane // p.block == b, moved, total)
            stage[d] = total
            for xp in range(p.cells_x):
                outs[chunk * ring + d][cg - first, xp] = stage[
                    d, pl.ds(xp, p.rows, stride=p.cells_x), :
                ].astype(BF16)

    own = labels[pl.ds(pl.multiple_of(core * tall, 8), tall), :].astype(F32)
    for chunk, (first, last) in enumerate(cuts):
        tail = last == p.groups

        def step(cg, carry, chunk=chunk, first=first):
            group(cg, lambda c: field[c].astype(F32), chunk, first)
            return carry

        lax.fori_loop(first, last - 1 if tail else last, step, 0)
        if tail:
            group(last - 1, lambda c: field[c].astype(F32) if c < p.chans else own, chunk, first)


def cell_of(p, d, xp):
    return (xp - p.cells_x * d) % p.xs


def conv_body(p, first, count, table, *refs):
    pieces, smooth, rim = refs[: p.ring], refs[p.ring], refs[p.ring + 1]
    core = lax.axis_index("col")

    def step(g, carry):
        weights = [table[first + g, pl.ds(t, 1), :] for t in range(ROW_WALL)]
        tops, lows = {}, {}
        for part in range(p.rows // 16):
            cells = {}
            for d in range(p.ring):
                for xp in range(p.cells_x):
                    cells[cell_of(p, d, xp)] = pieces[d][g, xp, pl.ds(16 * part, 16), :].astype(F32)
            for x in range(p.xs):
                total = None
                for j in range(TAPS):
                    line = None
                    for i in range(TAPS):
                        term = weights[TAPS * i + j] * cells[(x + i - REACH) % p.xs]
                        line = term if line is None else line + term
                    if j != REACH:
                        line = pltpu.roll(line, (REACH - j) % LANES, 1)
                    total = line if total is None else total + line
                smooth[g, x, pl.ds(16 * part, 16), :] = total.astype(BF16)
                if part == 0:
                    tops[x] = total[:8]
                if part == p.rows // 16 - 1:
                    lows[x] = total[8:]
        for pair in range(p.xs // 2):
            top = jnp.concatenate([tops[2 * pair], tops[2 * pair + 1]], axis=0)
            low = jnp.concatenate([lows[2 * pair], lows[2 * pair + 1]], axis=0)
            rim[g, pair] = jnp.where(core == 0, low, top).astype(BF16)
        return carry

    lax.fori_loop(0, count, step, 0)


def fill_column(p, core, smooth, rim, g, x, store):
    store(WALL_HALO, p.rows, smooth[g, x].astype(F32))
    near = rim[g, x // 2].astype(F32)[8 * (x % 2) : 8 * (x % 2) + 8]
    store(0, WALL_HALO, jnp.where(core == 0, 0.0, near))
    store(WALL_HALO + p.rows, WALL_HALO, jnp.where(core == 0, near, 0.0))


def own_lanes(p, rows):
    lane = lane_of(rows)
    place = lane % p.block
    return (place >= EDGE) & (place < EDGE + p.window) & (lane < p.per * p.block)


def spread(p, value, lane):
    total = value
    for b in range(p.per - 1):
        moved = pltpu.roll(value, LANES - p.block * (p.per - 1 - b), 1)
        total = jnp.where(lane // p.block == b, moved, total)
    return total


def wall_body(p, cuts, table, bands, *refs):
    count = len(cuts)
    smooths, rims = refs[:count], refs[count : 2 * count]
    refs = refs[2 * count :]
    results = refs[: p.ring]
    grad_smooth, grad_wall, hidden_out, errors_out = refs[p.ring : p.ring + 4]
    column, hidden, slope, score, wall, field = refs[p.ring + 4 :]
    core, me = lax.axis_index("col"), lax.axis_index("gx")
    blocks = p.reach_rows // 8
    lane = lane_of(8)
    half = WALL // 2
    all_rows = 2 * p.rows

    for chunk, (first, last) in enumerate(cuts):

        def fill(g, carry, chunk=chunk, first=first):
            for x in range(p.xs):

                def store(start, length, value, x=x):
                    column[first + g, x, pl.ds(start, length), :] = value

                fill_column(p, core, smooths[chunk], rims[chunk], g, x, store)
            return carry

        lax.fori_loop(0, last - first, fill, 0)

    score[...] = jnp.zeros_like(score)

    def forward(cg, carry):
        taps = [table[cg, pl.ds(ROW_WALL + k, 1), :] for k in range(WALL)]
        classes = [table[cg, pl.ds(ROW_CLASS + k, 1), :] for k in range(p.classes)]
        for blk in range(blocks):
            rows = pl.ds(8 * blk, 8)
            sums = [None] * p.xs
            for k in range(WALL):
                tap = taps[k] * bands[k, rows, :]
                for x in range(p.xs):
                    term = tap * column[cg, x, pl.ds(8 * blk + k, 8), :]
                    sums[x] = term if k == 0 else sums[x] + term
            for x in range(p.xs):
                value = sums[x]
                sig = 0.5 * jnp.tanh(0.5 * value) + 0.5
                act = value * sig
                hidden[cg, x, rows, :] = act
                slope[cg, x, rows, :] = sig + act * (1.0 - sig)
                for k in range(p.classes):
                    score[k, x, rows, :] += classes[k] * act
        return carry

    lax.fori_loop(0, p.groups, forward, 0)

    def judge(blk, carry):
        rows = pl.ds(pl.multiple_of(8 * blk, 8), 8)
        place = core * p.rows - half + 8 * blk + lax.broadcasted_iota(jnp.int32, (8, LANES), 0)
        inside = (place >= 0) & (place < all_rows)
        for x in range(p.xs):
            label = spread(p, column[p.groups - 1, x, pl.ds(8 * blk + half, 8), :], lane)
            for k in range(p.classes):
                value = score[k, x, rows, :]
                total = value
                for b in range(1, p.per):
                    total = total + pltpu.roll(value, p.block * b, 1)
                error = spread(p, total, lane) - jnp.where(label == k, 1.0, 0.0)
                score[k, x, rows, :] = jnp.where(inside, error, 0.0)
        return carry

    lax.fori_loop(0, blocks, judge, 0)
    own = own_lanes(p, p.rows)
    for k in range(p.classes):
        for x in range(p.xs):
            errors_out[k, x] = jnp.where(own, score[k, x, pl.ds(half, p.rows), :], 0.0)

    def backward(cg, carry):
        taps = [table[cg, pl.ds(ROW_WALL + k, 1), :] for k in range(WALL)]
        classes = [table[cg, pl.ds(ROW_CLASS + k, 1), :] for k in range(p.classes)]
        for blk in range(blocks):
            rows = pl.ds(8 * blk, 8)
            for x in range(p.xs):
                grad = classes[0] * score[0, x, rows, :]
                for k in range(1, p.classes):
                    grad = grad + classes[k] * score[k, x, rows, :]
                wall[x, rows, :] = (grad * slope[cg, x, rows, :]).astype(BF16).astype(F32)
        for x in range(p.xs):
            grad_wall[cg, x] = jnp.where(own, wall[x, pl.ds(half, p.rows), :], 0.0).astype(BF16)
            hidden_out[cg, x] = hidden[cg, x, pl.ds(half, p.rows), :].astype(BF16)
        for part in range(p.rows // 16):
            sums = [None] * p.xs
            for k in range(WALL):
                rows = pl.ds(16 * part + WALL - 1 - k, 16)
                tap = taps[k] * bands[k, rows, :]
                for x in range(p.xs):
                    term = tap * wall[x, rows, :]
                    sums[x] = term if k == 0 else sums[x] + term
            for x in range(p.xs):
                grad_smooth[cg, x, pl.ds(16 * part, 16), :] = sums[x].astype(BF16)
        weights = [table[cg, pl.ds(t, 1), :] for t in range(ROW_WALL)]
        for part in range(p.rows // 16):
            rows = pl.ds(16 * part, 16)
            cells = [grad_smooth[cg, x, rows, :].astype(F32) for x in range(p.xs)]
            for x in range(p.xs):
                total = None
                for j in range(TAPS):
                    line = None
                    for i in range(TAPS):
                        term = weights[TAPS * i + j] * cells[(x - i + REACH) % p.xs]
                        line = term if line is None else line + term
                    if j != REACH:
                        line = pltpu.roll(line, (j - REACH) % LANES, 1)
                    total = line if total is None else total + line
                field[cg, x, rows, :] = total
        return carry

    lax.fori_loop(0, p.groups, backward, 0)

    wide = lane_of(p.rows)

    def ship(pack, carry):
        for b in range(p.ring):
            c = pack * p.ring + b
            cg, at = c // p.per, c % p.per
            spot = lax.rem(b + me, p.ring)
            shift = lax.rem(2 * LANES + p.window * spot - p.block * at - EDGE, LANES)
            for d in range(p.ring):
                for xp in range(p.cells_x):
                    moved = pltpu.roll(field[cg, cell_of(p, d, xp)], shift, 1)
                    held = column[0, cell_of(p, d, xp), pl.ds(0, p.rows), :]
                    column[0, cell_of(p, d, xp), pl.ds(0, p.rows), :] = jnp.where(
                        wide // p.window == spot, moved, held
                    )
        for d in range(p.ring):
            for xp in range(p.cells_x):
                results[d][pack, xp] = column[0, cell_of(p, d, xp), pl.ds(0, p.rows), :].astype(
                    BF16
                )
        return carry

    lax.fori_loop(0, p.packs, ship, 0)


def weight_body(p, cuts, bands, grad_smooth, grad_wall, hidden, errors, *refs):
    count = len(cuts)
    smooths, rims = refs[:count], refs[count : 2 * count]
    refs = refs[2 * count :]
    pieces = [refs[i * p.ring : (i + 1) * p.ring] for i in range(count)]
    out, column, lines = refs[count * p.ring :]
    core = lax.axis_index("col")
    half = WALL // 2
    own = own_lanes(p, 16)
    out[...] = jnp.zeros_like(out)
    lines[...] = jnp.zeros_like(lines)
    lane = lane_of(LANES)
    channel = lax.broadcasted_iota(jnp.int32, (LANES, LANES), 0)

    def fold(value):
        total = value[:8]
        for r in range(8, value.shape[0], 8):
            total = total + value[r : r + 8]
        return jnp.sum(total, axis=0, keepdims=True)

    for chunk, (first, last) in enumerate(cuts):

        def step(g, carry, chunk=chunk, first=first):
            cg = first + g
            sums = [None] * ROW_WALL
            for part in range(p.rows // 16):
                rows = pl.ds(16 * part, 16)
                cells = {}
                for d in range(p.ring):
                    for xp in range(p.cells_x):
                        cells[cell_of(p, d, xp)] = pieces[chunk][d][g, xp, rows, :].astype(F32)
                for x in range(p.xs):
                    grad = jnp.where(own, grad_smooth[cg, x, rows, :].astype(F32), 0.0)
                    for j in range(TAPS):
                        moved = grad if j == REACH else pltpu.roll(grad, (j - REACH) % LANES, 1)
                        for i in range(TAPS):
                            t = TAPS * i + j
                            term = cells[(x + i - REACH) % p.xs] * moved
                            term = term[:8] + term[8:]
                            sums[t] = term if sums[t] is None else sums[t] + term
            for t in range(ROW_WALL):
                lines[pl.ds(t, 1), :] = fold(sums[t])
            for x in range(p.xs):

                def store(start, length, value, x=x):
                    column[x, pl.ds(start, length), :] = value

                fill_column(p, core, smooths[chunk], rims[chunk], g, x, store)
            grads = [grad_wall[cg, x].astype(F32) for x in range(p.xs)]
            for k in range(WALL):
                total = None
                for x in range(p.xs):
                    term = grads[x] * column[x, pl.ds(half + k, p.rows), :]
                    total = term if total is None else total + term
                lines[pl.ds(ROW_WALL + k, 1), :] = fold(total * bands[k, pl.ds(half, p.rows), :])
            for k in range(p.classes):
                total = None
                for x in range(p.xs):
                    term = errors[k, x] * hidden[cg, x].astype(F32)
                    total = term if total is None else total + term
                lines[pl.ds(ROW_CLASS + k, 1), :] = fold(total)
            pick = (lane // p.block + cg * p.per == channel) & (lane < p.per * p.block)
            out[...] += lax.dot_general(
                lines[...],
                jnp.where(pick, 1.0, 0.0),
                (((1,), (1,)), ((), ())),
                precision=lax.Precision.HIGHEST,
                preferred_element_type=F32,
            )
            return carry

        lax.fori_loop(0, last - first, step, 0)


def unpack_body(p, *refs):
    pieces, out, stage = refs[: p.ring], refs[p.ring], refs[p.ring + 1]
    me = lax.axis_index("gx")
    spot = lane_of(p.rows) // p.window

    def step(pack, carry):
        for xp in range(p.cells_x):
            values = [pieces[d][pack, xp].astype(F32) for d in range(p.ring)]
            for b in range(p.ring):
                total = values[0]
                for d in range(1, p.ring):
                    total = jnp.where(spot == lax.rem(b + me + d, p.ring), values[d], total)
                total = pltpu.roll(total, (LANES - p.window * b) % LANES, 1) if b else total
                stage[b, pl.ds(xp, p.rows, stride=p.cells_x), :] = total
        for b in range(p.ring):
            out[pack * p.ring + b] = stage[b].astype(BF16)
        return carry

    lax.fori_loop(0, p.packs, step, 0)


def rotation(size, by):
    return [(i, (i + by) % size) for i in range(size)]


def sum_over(value, axis):
    size = lax.axis_size(axis)
    return sum((lax.ppermute(value, axis, rotation(size, d)) for d in range(1, size)), value)


def band_rows(grid_index, stretch):
    levels = stretch.shape[0]
    onehot = (grid_index[:, None] == jnp.arange(levels, dtype=jnp.int32)[None, :]).astype(F32)
    return jnp.dot(onehot, stretch, precision=lax.Precision.HIGHEST)


def by_windows(features, labels, grid_index, stretch, tile_filter, wall_filter, class_weight):
    chans, rows, cells_x, cells_z = features.shape
    classes = class_weight.shape[0]
    ring, gz = lax.axis_size("gx"), lax.axis_size("gz")
    p = Plan(ring, chans, rows, cells_x, cells_z, classes)
    volume = labels.shape[0] * cells_x * ring * cells_z * gz
    tall = rows * cells_x
    middle = p.groups // 2
    cuts = ((0, middle), (middle, p.groups))

    field = features.reshape(chans, tall, cells_z)
    marks = labels.reshape(labels.shape[0] * cells_x, cells_z)
    (edge,) = call(
        functools.partial(edge_body, p),
        [jax.ShapeDtypeStruct((p.edge_groups, tall, LANES), BF16)],
        (field, marks),
    )
    left = lax.ppermute(edge, "gz", rotation(gz, 1))
    right = left if gz == 2 else lax.ppermute(edge, "gz", rotation(gz, -1))

    windows = call(
        functools.partial(pack_body, p, cuts),
        [
            jax.ShapeDtypeStruct((last - first, cells_x, rows, LANES), BF16)
            for first, last in cuts
            for d in range(ring)
        ],
        (field, marks, left, right),
        [pltpu.VMEM((ring, tall, LANES), F32)],
    )

    bands = band_rows(grid_index, stretch)
    half = WALL // 2
    near = lax.dynamic_slice_in_dim(
        jnp.pad(bands, ((half, half), (0, 0))), lax.axis_index("col") * rows, p.reach_rows, 0
    )
    near = jnp.broadcast_to(near.T[:, :, None], (WALL, p.reach_rows, LANES))
    params = jnp.concatenate([tile_filter.T, wall_filter.T, class_weight], axis=0)
    extra = (jnp.arange(params.shape[0]) == CENTRE).astype(F32)[:, None]
    params = jnp.concatenate([params, extra], axis=1).reshape(-1, p.groups, p.per, 1)
    table = jnp.broadcast_to(params, params.shape[:3] + (p.block,))
    table = table.reshape(params.shape[0], p.groups, p.per * p.block)
    table = jnp.pad(
        table,
        ((0, p.table_rows - table.shape[0]), (0, 0), (0, LANES - p.per * p.block)),
    ).transpose(1, 0, 2)

    smooths, rims, pieces = [], [], []
    for chunk, (first, last) in enumerate(cuts):
        sent = windows[chunk * ring : (chunk + 1) * ring]
        got = [sent[0]] + [
            lax.ppermute(sent[d], "gx", rotation(ring, d)) for d in range(1, ring)
        ]
        smooth, rim = call(
            functools.partial(conv_body, p, first, last - first),
            [
                jax.ShapeDtypeStruct((last - first, p.xs, rows, LANES), BF16),
                jax.ShapeDtypeStruct((last - first, p.xs // 2, 16, LANES), BF16),
            ],
            (table, *got),
        )
        smooths.append(smooth)
        rims.append(lax.ppermute(rim, "col", rotation(2, 1)))
        pieces += got

    out_shapes = [jax.ShapeDtypeStruct((p.packs, cells_x, rows, LANES), BF16)] * ring + [
        jax.ShapeDtypeStruct((p.groups, p.xs, rows, LANES), BF16),
        jax.ShapeDtypeStruct((p.groups, p.xs, rows, LANES), BF16),
        jax.ShapeDtypeStruct((p.groups, p.xs, rows, LANES), BF16),
        jax.ShapeDtypeStruct((classes, p.xs, rows, LANES), F32),
    ]
    solved = call(
        functools.partial(wall_body, p, cuts),
        out_shapes,
        (table, near, *smooths, *rims),
        [
            pltpu.VMEM((p.groups, p.xs, rows + 2 * WALL_HALO, LANES), F32),
            pltpu.VMEM((p.groups, p.xs, p.reach_rows, LANES), F32),
            pltpu.VMEM((p.groups, p.xs, p.reach_rows, LANES), F32),
            pltpu.VMEM((classes, p.xs, p.reach_rows, LANES), F32),
            pltpu.VMEM((p.xs, p.reach_rows, LANES), F32),
            pltpu.VMEM((p.groups, p.xs, rows, LANES), F32),
        ],
    )
    results, (grad_smooth, grad_wall, hidden, errors) = solved[:ring], solved[ring:]
    back = [results[0]] + [
        lax.ppermute(results[d], "gx", rotation(ring, -d)) for d in range(1, ring)
    ]
    (sums,) = call(
        functools.partial(weight_body, p, cuts),
        [jax.ShapeDtypeStruct((p.table_rows, LANES), F32)],
        (near, grad_smooth, grad_wall, hidden, errors, *smooths, *rims, *pieces),
        [
            pltpu.VMEM((p.xs, rows + 2 * WALL_HALO, LANES), F32),
            pltpu.VMEM((p.table_rows, LANES), F32),
        ],
    )
    for axis in ("col", "gz", "gx"):
        sums = sum_over(sums, axis)
    sums = sums / volume
    (grad_field,) = call(
        functools.partial(unpack_body, p),
        [jax.ShapeDtypeStruct((chans, tall, cells_z), BF16)],
        back,
        [pltpu.VMEM((ring, tall, LANES), F32)],
    )
    return (
        grad_field.reshape(features.shape),
        sums[:ROW_WALL, :chans].T,
        sums[ROW_WALL:ROW_CLASS, :chans].T,
        sums[ROW_CLASS : ROW_CLASS + classes, :chans],
    )


def with_halo(value, sides, width):
    for axis, dim in sides:
        size, length = (lax.axis_size(axis), value.shape[dim])
        up = [(i, (i + 1) % size) for i in range(size)]
        down = [(j, i) for i, j in up]
        last = lax.slice_in_dim(value, length - width, length, axis=dim)
        leading = lax.slice_in_dim(value, 0, width, axis=dim)
        before = lax.ppermute(last, axis, up)
        after = lax.ppermute(leading, axis, down)
        value = jnp.concatenate([before, value, after], axis=dim)
    return value


def rim_tiles(field):
    return with_halo(field, (("gx", 2), ("gz", 3)), 2)


def wall_forward(smooth_ext, wall_rows, band_rows):
    rows = band_rows.shape[0]
    total = jnp.zeros((smooth_ext.shape[0], rows) + smooth_ext.shape[2:], jnp.float32)
    for k in range(9):
        tap = wall_rows[:, k][:, None] * band_rows[:, k][None, :]
        total = total + tap[:, :, None, None] * smooth_ext[:, k : k + rows].astype(jnp.float32)
    return total


def wall_backward(grad_ext, wall_rows, band_ext, rows):
    total = jnp.zeros((grad_ext.shape[0], rows) + grad_ext.shape[2:], jnp.float32)
    for k in range(9):
        first = 8 - k
        tap = wall_rows[:, k][:, None] * band_ext[first : first + rows, k][None, :]
        total = total + tap[:, :, None, None] * grad_ext[:, first : first + rows].astype(
            jnp.float32
        )
    return total


def by_halos(features, labels, grid_index, stretch, tile_filter, wall_filter, class_weight):
    chans, half_rows, cells_x, cells_z = features.shape
    all_rows = labels.shape[0]
    classes = class_weight.shape[0]
    volume = all_rows * cells_x * lax.axis_size("gx") * cells_z * lax.axis_size("gz")
    widened = rim_tiles(features)
    smooth = jnp.zeros(features.shape, jnp.float32)
    for i in range(5):
        for j in range(5):
            weight = tile_filter[:, 5 * i + j][:, None, None, None]
            smooth = smooth + weight * widened[:, :, i : i + cells_x, j : j + cells_z].astype(
                jnp.float32
            )
    smoothed = smooth.astype(jnp.bfloat16)
    bands = band_rows(grid_index, stretch)
    bands_pad = jnp.pad(bands, ((4, 4), (0, 0)))
    place = lax.axis_index("col")
    share = chans // lax.axis_size("col")
    first_chan = place * share
    pencil = lax.all_to_all(smoothed, "col", split_axis=0, concat_axis=1, tiled=True)
    smooth_ext = jnp.pad(pencil, ((0, 0), (4, 4), (0, 0), (0, 0)))
    wall_rows = lax.dynamic_slice_in_dim(wall_filter, first_chan, share, 0)
    class_rows = lax.dynamic_slice_in_dim(class_weight, first_chan, share, 1)
    wall_out = wall_forward(smooth_ext, wall_rows, bands)
    sig = jax.nn.sigmoid(wall_out)
    hidden = wall_out * sig
    partial_scores = jnp.einsum(
        "kc,cyxz->kyxz", class_rows, hidden, precision=lax.Precision.HIGHEST
    )
    scores = lax.psum(partial_scores, "col")
    targets = (labels[None] == jnp.arange(classes, dtype=jnp.int32)[:, None, None, None]).astype(
        jnp.float32
    )
    errors = scores - targets
    grad_hidden = jnp.einsum("kc,kyxz->cyxz", class_rows, errors, precision=lax.Precision.HIGHEST)
    grad_wall = (grad_hidden * sig * (1.0 + wall_out * (1.0 - sig))).astype(jnp.bfloat16)
    class_part = jnp.einsum("kyxz,cyxz->kc", errors, hidden, precision=lax.Precision.HIGHEST)
    grad_vals = grad_wall.astype(jnp.float32)
    wall_part = jnp.stack(
        [
            jnp.sum(
                grad_vals
                * bands[:, k][None, :, None, None]
                * smooth_ext[:, k : k + all_rows].astype(jnp.float32),
                axis=(1, 2, 3),
            )
            for k in range(9)
        ],
        axis=1,
    )
    grad_ext = jnp.pad(grad_wall, ((0, 0), (4, 4), (0, 0), (0, 0)))
    grad_smooth = wall_backward(grad_ext, wall_rows, bands_pad, all_rows).astype(jnp.bfloat16)
    grad_tile = lax.all_to_all(grad_smooth, "col", split_axis=1, concat_axis=0, tiled=True)
    wall_full = lax.dynamic_update_slice_in_dim(
        jnp.zeros((chans, 9), jnp.float32), wall_part, first_chan, 0
    )
    class_full = lax.dynamic_update_slice_in_dim(
        jnp.zeros((classes, chans), jnp.float32), class_part, first_chan, 1
    )
    grad_widened = rim_tiles(grad_tile)
    grad_tile_vals = grad_tile.astype(jnp.float32)
    grad_field = jnp.zeros(features.shape, jnp.float32)
    tile_terms = []
    for i in range(5):
        for j in range(5):
            weight = tile_filter[:, 5 * i + j][:, None, None, None]
            grad_field = grad_field + weight * grad_widened[
                :, :, 4 - i : 4 - i + cells_x, 4 - j : 4 - j + cells_z
            ].astype(jnp.float32)
            shifted = widened[:, :, i : i + cells_x, j : j + cells_z].astype(jnp.float32)
            tile_terms.append(jnp.sum(shifted * grad_tile_vals, axis=(1, 2, 3)))
    tile_part = jnp.stack(tile_terms, axis=1)
    totals = lax.psum((tile_part, wall_full, class_full), ("gx", "gz", "col"))
    return (
        grad_field.astype(jnp.bfloat16),
        totals[0] / volume,
        totals[1] / volume,
        totals[2] / volume,
    )


def shards(features, labels, grid_index, stretch, tile_filter, wall_filter, class_weight):
    sizes = [lax.axis_size(axis) for axis in ("gx", "gz", "col")]
    plan = by_windows if fits(*sizes, *features.shape, class_weight.shape[0]) else by_halos
    return plan(features, labels, grid_index, stretch, tile_filter, wall_filter, class_weight)


def solution(mesh):
    return jax.shard_map(
        shards,
        mesh=mesh,
        in_specs=(
            P(None, "col", ("group", "gx"), "gz"),
            P(None, ("group", "gx"), "gz"),
            P(),
            P(),
            P(),
            P(),
            P(),
        ),
        out_specs=(
            P(None, "col", ("group", "gx"), "gz"),
            P("group", None),
            P("group", None),
            P("group", None),
        ),
        check_vma=False,
    )
```

```python
import functools
import math

import jax
import jax.numpy as jnp
from jax import lax
from jax.experimental import pallas as pl
from jax.experimental.pallas import tpu as pltpu
from jax.sharding import PartitionSpec as P

LANES = 128
TAPS = 5
REACH = 2
EDGE = 4
WALL = 9
WALL_HALO = 8
ROW_WALL = TAPS * TAPS
ROW_CLASS = ROW_WALL + WALL
CENTRE = ROW_WALL // 2
F32, BF16 = jnp.float32, jnp.bfloat16


class Plan:
    def __init__(self, ring, chans, rows, cells_x, cells_z, classes):
        self.ring, self.chans, self.rows, self.cells_x = ring, chans, rows, cells_x
        self.classes = classes
        self.window = cells_z // ring
        self.block = self.window + 2 * EDGE
        self.per = LANES // self.block
        self.slots = chans + 1
        self.groups = self.slots // self.per
        self.xs = ring * cells_x
        self.packs = chans // ring
        self.reach_rows = rows + 2 * (WALL_HALO // 2)
        self.edge_slots = LANES // (2 * EDGE)
        self.edge_groups = -(-self.slots // self.edge_slots)
        self.table_rows = -(-(ROW_CLASS + classes) // 8) * 8


    def cuts(self):
        unit = math.lcm(self.per, self.ring)
        step = unit // self.per
        firsts = list(range(0, self.groups, step))
        if len(firsts) > 3:
            firsts = [firsts[0], firsts[len(firsts) // 3], firsts[len(firsts) * 2 // 3]]
        cuts = tuple(zip(firsts, firsts[1:] + [self.groups]))
        early = cuts[-1][0] * self.per // self.ring
        return cuts, (early, self.packs - early)


def fits(ring, gz, col, chans, rows, cells_x, cells_z, classes):
    if cells_z != LANES or cells_x != 2 or col != 2 or ring < 2 or ring > 4 or LANES % ring:
        return False
    block = LANES // ring + 2 * EDGE
    per = LANES // block
    return (chans + 1) % per == 0 and chans % ring == 0 and rows % 16 == 0 and ring * cells_x >= TAPS


def vmem(count):
    return [pl.BlockSpec(memory_space=pltpu.VMEM)] * count


def call(body, outs, args, scratch=(), micros=1.0, unread=0):
    return pl.pallas_call(
        body,
        out_shape=outs,
        in_specs=vmem(len(args) - unread) + [pl.BlockSpec(memory_space=pl.ANY)] * unread,
        cost_estimate=pl.CostEstimate(
            flops=0, bytes_accessed=int(3.0e6 * micros), transcendentals=0
        ),
        out_specs=vmem(len(outs)),
        scratch_shapes=list(scratch),
        compiler_params=pltpu.CompilerParams(vmem_limit_bytes=40 * 2**20),
    )(*args)


def lane_of(rows):
    return lax.broadcasted_iota(jnp.int32, (rows, LANES), 1)


def edge_body(p, field, labels, out):
    core = lax.axis_index("col")
    tall = p.rows * p.cells_x
    lane = lane_of(tall)

    def group(g, count, fetch):
        total = jnp.zeros((tall, LANES), F32)
        for e in range(count):
            moved = pltpu.roll(fetch(g * p.edge_slots + e), (2 * EDGE * e + EDGE) % LANES, 1)
            total = jnp.where(lane // (2 * EDGE) == e, moved, total)
        out[g] = total.astype(BF16)

    def step(g, carry):
        group(g, p.edge_slots, lambda c: field[c].astype(F32))
        return carry

    full = p.chans // p.edge_slots
    lax.fori_loop(0, full, step, 0)
    own = labels[pl.ds(pl.multiple_of(core * tall, 8), tall), :].astype(F32)
    group(full, p.slots - full * p.edge_slots, lambda c: own)


def pack_body(p, cuts, field, labels, left, right, *refs):
    outs, stage = refs[:-1], refs[-1]
    ring = p.ring
    me, core = lax.axis_index("gx"), lax.axis_index("col")
    tall = p.rows * p.cells_x
    lane = lane_of(tall)
    takes = [lax.rem(me + d, ring) for d in range(ring)]
    fixes = [
        ((lane >= LANES - EDGE) & (k == 0)) | ((lane < EDGE) & (k == ring - 1)) for k in takes
    ]
    older = lane % (2 * EDGE) < EDGE

    def edges(c):
        g, e = c // p.edge_slots, c % p.edge_slots
        both = jnp.where(older, left[g].astype(F32), right[g].astype(F32))
        return pltpu.roll(both, LANES - EDGE - 2 * EDGE * e, 1)

    def group(cg, fetch, chunk, first):
        values = [fetch(cg * p.per + b) for b in range(p.per)]
        rims = [edges(cg * p.per + b) for b in range(p.per)]
        for d in range(ring):
            total = jnp.zeros((tall, LANES), F32)
            for b in range(p.per):
                shift = lax.rem(2 * LANES + p.block * b + EDGE - p.window * takes[d], LANES)
                moved = pltpu.roll(jnp.where(fixes[d], rims[b], values[b]), shift, 1)
                total = jnp.where(lane // p.block == b, moved, total)
            stage[d] = total
            for xp in range(p.cells_x):
                outs[chunk * ring + d][cg - first, xp] = stage[
                    d, pl.ds(xp, p.rows, stride=p.cells_x), :
                ].astype(BF16)

    own = labels[pl.ds(pl.multiple_of(core * tall, 8), tall), :].astype(F32)
    for chunk, (first, last) in enumerate(cuts):
        tail = last == p.groups

        def step(cg, carry, chunk=chunk, first=first):
            group(cg, lambda c: field[c].astype(F32), chunk, first)
            return carry

        lax.fori_loop(first, last - 1 if tail else last, step, 0)
        if tail:
            group(last - 1, lambda c: field[c].astype(F32) if c < p.chans else own, chunk, first)


def cell_of(p, d, xp):
    return (xp - p.cells_x * d) % p.xs


def smooth_group(p, table, cg, pieces, g, store):
    weights = [table[cg, pl.ds(t, 1), :] for t in range(ROW_WALL)]
    for part in range(p.rows // 16):
        cells = {}
        for d in range(p.ring):
            for xp in range(p.cells_x):
                cells[cell_of(p, d, xp)] = pieces[d][g, xp, pl.ds(16 * part, 16), :].astype(F32)
        for x in range(p.xs):
            total = None
            for j in range(TAPS):
                line = None
                for i in range(TAPS):
                    term = weights[TAPS * i + j] * cells[(x + i - REACH) % p.xs]
                    line = term if line is None else line + term
                if j != REACH:
                    line = pltpu.roll(line, (REACH - j) % LANES, 1)
                total = line if total is None else total + line
            store(x, 16 * part, total.astype(BF16))


def activate(value):
    sig = 0.5 * jnp.tanh(0.5 * value) + 0.5
    act = value * sig
    return act, sig + act * (1.0 - sig)


def forward_body(p, first, count, last, table, bands, *refs):
    refs = list(refs)

    def take(number):
        taken = refs[:number]
        del refs[:number]
        return taken

    pieces = take(p.ring)
    before = take(1 if first else 0)
    rims = take(len(refs) - 6 if last else 0)
    smooth, hidden, slope, score, rim, column = refs
    core = lax.axis_index("col")
    blocks = p.reach_rows // 8
    score[...] = before[0][...] if first else jnp.zeros_like(score)
    for x in range(p.xs):
        column[x, pl.ds(0, WALL_HALO), :] = jnp.zeros((WALL_HALO, LANES), F32)
        column[x, pl.ds(WALL_HALO + p.rows, WALL_HALO), :] = jnp.zeros((WALL_HALO, LANES), F32)
    base = 0
    for other in rims:
        rim[pl.ds(base, other.shape[0])] = other[...]
        base += other.shape[0]

    def step(g, carry):
        cg = first + g

        def store(x, row, value):
            smooth[g, x, pl.ds(row, 16), :] = value
            column[x, pl.ds(WALL_HALO + row, 16), :] = value.astype(F32)

        smooth_group(p, table, cg, pieces, g, store)
        for pair in range(p.xs // 2):
            cells = (2 * pair, 2 * pair + 1)
            tops = [column[x, pl.ds(WALL_HALO, 8), :] for x in cells]
            lows = [column[x, pl.ds(p.rows, 8), :] for x in cells]
            rim[base + g, pair] = jnp.where(
                core == 0, jnp.concatenate(lows, axis=0), jnp.concatenate(tops, axis=0)
            ).astype(BF16)
        taps = [table[cg, pl.ds(ROW_WALL + k, 1), :] for k in range(WALL)]
        classes = [table[cg, pl.ds(ROW_CLASS + k, 1), :] for k in range(p.classes)]
        for blk in range(blocks):
            rows = pl.ds(8 * blk, 8)
            sums = [None] * p.xs
            for k in range(WALL):
                tap = taps[k] * bands[k, rows, :]
                for x in range(p.xs):
                    term = tap * column[x, pl.ds(8 * blk + k, 8), :]
                    sums[x] = term if k == 0 else sums[x] + term
            for x in range(p.xs):
                hidden[g, x, rows, :], slope[g, x, rows, :] = act, _ = activate(sums[x])
                for k in range(p.classes):
                    score[k, x, rows, :] += classes[k] * act
        return carry

    lax.fori_loop(0, count, step, 0)


def fill_column(p, core, smooth, rim, g, cg, x, store):
    store(WALL_HALO, p.rows, smooth[g, x].astype(F32))
    near = rim[cg, x // 2].astype(F32)[8 * (x % 2) : 8 * (x % 2) + 8]
    store(0, WALL_HALO, jnp.where(core == 0, 0.0, near))
    store(WALL_HALO + p.rows, WALL_HALO, jnp.where(core == 0, near, 0.0))


def own_lanes(p, rows):
    lane = lane_of(rows)
    place = lane % p.block
    return (place >= EDGE) & (place < EDGE + p.window) & (lane < p.per * p.block)


def spread(p, value, lane):
    total = value
    for b in range(p.per - 1):
        moved = pltpu.roll(value, LANES - p.block * (p.per - 1 - b), 1)
        total = jnp.where(lane // p.block == b, moved, total)
    return total


def near_block(p, core):
    return pl.multiple_of(jnp.where(core == 0, p.reach_rows - 8, 0), 8)


def edge_rows(p, core, cuts, table, bands, smooths, rim, score, hidden_near, slope_near):
    base = near_block(p, core)
    rows = pl.ds(base, 8)
    for k in range(p.classes):
        for x in range(p.xs):
            score[k, x, rows, :] = jnp.zeros((8, LANES), F32)

    for chunk, (first, last) in enumerate(cuts):

        def step(g, carry, chunk=chunk, first=first):
            cg = first + g
            taps = [
                table[cg, pl.ds(ROW_WALL + k, 1), :] * bands[k, rows, :] for k in range(WALL)
            ]
            classes = [table[cg, pl.ds(ROW_CLASS + k, 1), :] for k in range(p.classes)]
            for x in range(p.xs):
                near = rim[cg, x // 2].astype(F32)[8 * (x % 2) : 8 * (x % 2) + 8]
                low = smooths[chunk][g, x, pl.ds(p.rows - 16, 16), :].astype(F32)[8:]
                top = smooths[chunk][g, x, pl.ds(0, 16), :].astype(F32)[:8]
                hidden_near[cg, x] = jnp.where(core == 0, low, near)
                slope_near[cg, x] = jnp.where(core == 0, near, top)
            sums = []
            for x in range(p.xs):
                both = jnp.concatenate([hidden_near[cg, x], slope_near[cg, x]], axis=0)
                total = taps[0] * both[:8]
                for k in range(1, WALL):
                    total = total + taps[k] * both[k : k + 8]
                sums.append(total)
            for x in range(p.xs):
                act, bend = activate(sums[x])
                hidden_near[cg, x], slope_near[cg, x] = act, bend
                for k in range(p.classes):
                    score[k, x, rows, :] += classes[k] * act
            return carry

        lax.fori_loop(0, last - first, step, 0)


def judge(p, core, smooth, rim, score, errors, column):
    lane = lane_of(8)
    half = WALL // 2
    for x in range(p.xs):

        def store(start, length, value, x=x):
            column[x, pl.ds(start, length), :] = value

        fill_column(p, core, smooth, rim, smooth.shape[0] - 1, p.groups - 1, x, store)

    def step(blk, carry):
        rows = pl.ds(pl.multiple_of(8 * blk, 8), 8)
        place = core * p.rows - half + 8 * blk + lax.broadcasted_iota(jnp.int32, (8, LANES), 0)
        inside = (place >= 0) & (place < 2 * p.rows)
        for x in range(p.xs):
            label = spread(p, column[x, pl.ds(8 * blk + half, 8), :], lane)
            for k in range(p.classes):
                value = score[k, x, rows, :]
                total = value
                for b in range(1, p.per):
                    total = total + pltpu.roll(value, p.block * b, 1)
                error = spread(p, total, lane) - jnp.where(label == k, 1.0, 0.0)
                score[k, x, rows, :] = jnp.where(inside, error, 0.0)
        return carry

    lax.fori_loop(0, p.reach_rows // 8, step, 0)
    own = own_lanes(p, p.rows)
    for k in range(p.classes):
        for x in range(p.xs):
            errors[k, x] = jnp.where(own, score[k, x, pl.ds(half, p.rows), :], 0.0)


def with_near(p, core, blk, value, near):
    if blk == 0:
        return jnp.where(core == 0, value, near)
    if blk == p.reach_rows // 8 - 1:
        return jnp.where(core == 0, near, value)
    return value


def backward_groups(
    p, first, count, table, bands, score, slope, slope_near, grad_smooth, grad_wall, wall, field
):
    core = lax.axis_index("col")
    half = WALL // 2
    own = own_lanes(p, p.rows)

    def step(g, carry):
        cg = first + g
        taps = [table[cg, pl.ds(ROW_WALL + k, 1), :] for k in range(WALL)]
        classes = [table[cg, pl.ds(ROW_CLASS + k, 1), :] for k in range(p.classes)]
        for blk in range(p.reach_rows // 8):
            rows = pl.ds(8 * blk, 8)
            for x in range(p.xs):
                grad = classes[0] * score[0, x, rows, :]
                for k in range(1, p.classes):
                    grad = grad + classes[k] * score[k, x, rows, :]
                bend = with_near(p, core, blk, slope[g, x, rows, :], slope_near[cg, x])
                wall[x, rows, :] = (grad * bend).astype(BF16).astype(F32)
        for x in range(p.xs):
            grad_wall[g, x] = jnp.where(own, wall[x, pl.ds(half, p.rows), :], 0.0).astype(BF16)
        for part in range(p.rows // 16):
            sums = [None] * p.xs
            for k in range(WALL):
                rows = pl.ds(16 * part + WALL - 1 - k, 16)
                tap = taps[k] * bands[k, rows, :]
                for x in range(p.xs):
                    term = tap * wall[x, rows, :]
                    sums[x] = term if k == 0 else sums[x] + term
            for x in range(p.xs):
                grad_smooth[g, x, pl.ds(16 * part, 16), :] = sums[x].astype(BF16)
        weights = [table[cg, pl.ds(t, 1), :] for t in range(ROW_WALL)]
        for part in range(p.rows // 16):
            rows = pl.ds(16 * part, 16)
            cells = [grad_smooth[g, x, rows, :].astype(F32) for x in range(p.xs)]
            for x in range(p.xs):
                total = None
                for j in range(TAPS):
                    line = None
                    for i in range(TAPS):
                        term = weights[TAPS * i + j] * cells[(x - i + REACH) % p.xs]
                        line = term if line is None else line + term
                    if j != REACH:
                        line = pltpu.roll(line, (j - REACH) % LANES, 1)
                    total = line if total is None else total + line
                field[g, x, rows, :] = total
        return carry

    lax.fori_loop(0, count, step, 0)


def ship(p, packs, field, results):
    me = lax.axis_index("gx")
    wide = lane_of(p.rows) // p.window

    def step(pack, carry):
        totals = [jnp.zeros((p.rows, LANES), F32)] * p.xs
        for b in range(p.ring):
            c = pack * p.ring + b
            spot = lax.rem(b + me, p.ring)
            shift = lax.rem(2 * LANES + p.window * spot - p.block * (c % p.per) - EDGE, LANES)
            for x in range(p.xs):
                moved = pltpu.roll(field[c // p.per, x], shift, 1)
                totals[x] = jnp.where(wide == spot, moved, totals[x])
        for d in range(p.ring):
            for xp in range(p.cells_x):
                results[d][pack, xp] = totals[cell_of(p, d, xp)].astype(BF16)
        return carry

    lax.fori_loop(0, packs, step, 0)


def backward_body(p, cuts, packs, table, bands, score_in, rim, *refs):
    count = len(cuts)
    smooths, slopes, refs = refs[:count], refs[count : 2 * count - 1], refs[2 * count - 1 :]
    results, refs = refs[: p.ring], refs[p.ring :]
    score, errors, hidden_near, slope_near = refs[:4]
    grads = refs[4:-3]
    wall, field, column = refs[-3:]
    core = lax.axis_index("col")
    score[...] = score_in[...]
    edge_rows(p, core, cuts, table, bands, smooths, rim, score, hidden_near, slope_near)
    judge(p, core, smooths[-1], rim, score, errors, column)
    for i, (first, last) in enumerate(cuts[:-1]):
        backward_groups(
            p, first, last - first, table, bands, score, slopes[i], slope_near,
            grads[i], grads[count - 1 + i], wall, field.at[pl.ds(first, last - first)],
        )
    ship(p, packs, field, results)


def finish_body(
    p, cuts, packs, table, bands, score, errors, hidden_near, slope_near, rim, slope, *refs
):
    count = len(cuts)
    refs = list(refs)

    def take(number):
        taken = refs[:number]
        del refs[:number]
        return taken

    hiddens, smooths = take(count), take(count)
    pieces = [take(p.ring) for i in range(count)]
    grad_smooths, grad_walls = take(count - 1), take(count - 1)
    results = take(p.ring)
    out, wall, field, last_smooth, last_wall, column, lines = refs
    first, last = cuts[-1]
    backward_groups(
        p, first, last - first, table, bands, score, slope, slope_near, last_smooth, last_wall,
        wall, field,
    )
    ship(p, packs, field, results)
    grad_smooths, grad_walls = grad_smooths + [last_smooth], grad_walls + [last_wall]

    core = lax.axis_index("col")
    half = WALL // 2
    own = own_lanes(p, 16)
    lines[...] = jnp.zeros_like(lines)

    def fold(value):
        total = value[:8]
        for r in range(8, value.shape[0], 8):
            total = total + value[r : r + 8]
        return jnp.sum(total, axis=0, keepdims=True)

    for chunk, (first, last) in enumerate(cuts):

        def step(g, carry, chunk=chunk, first=first):
            cg = first + g
            sums = [None] * ROW_WALL
            for part in range(p.rows // 16):
                rows = pl.ds(16 * part, 16)
                cells = {}
                for d in range(p.ring):
                    for xp in range(p.cells_x):
                        cells[cell_of(p, d, xp)] = pieces[chunk][d][g, xp, rows, :].astype(F32)
                for x in range(p.xs):
                    grad = jnp.where(own, grad_smooths[chunk][g, x, rows, :].astype(F32), 0.0)
                    for j in range(TAPS):
                        moved = grad if j == REACH else pltpu.roll(grad, (j - REACH) % LANES, 1)
                        for i in range(TAPS):
                            t = TAPS * i + j
                            term = cells[(x + i - REACH) % p.xs] * moved
                            term = term[:8] + term[8:]
                            sums[t] = term if sums[t] is None else sums[t] + term
            for t in range(ROW_WALL):
                lines[cg, pl.ds(t, 1), :] = fold(sums[t])
            for x in range(p.xs):

                def store(start, length, value, x=x):
                    column[x, pl.ds(start, length), :] = value

                fill_column(p, core, smooths[chunk], rim, g, cg, x, store)
            grads = [grad_walls[chunk][g, x].astype(F32) for x in range(p.xs)]
            for k in range(WALL):
                total = None
                for x in range(p.xs):
                    term = grads[x] * column[x, pl.ds(half + k, p.rows), :]
                    total = term if total is None else total + term
                lines[cg, pl.ds(ROW_WALL + k, 1), :] = fold(
                    total * bands[k, pl.ds(half, p.rows), :]
                )
            for x in range(p.xs):
                for blk in range(p.reach_rows // 8):
                    rows = pl.ds(8 * blk, 8)
                    wall[x, rows, :] = with_near(
                        p, core, blk, hiddens[chunk][g, x, rows, :], hidden_near[cg, x]
                    )
            for k in range(p.classes):
                total = None
                for x in range(p.xs):
                    term = errors[k, x] * wall[x, pl.ds(half, p.rows), :]
                    total = term if total is None else total + term
                lines[cg, pl.ds(ROW_CLASS + k, 1), :] = fold(total)
            return carry

        lax.fori_loop(0, last - first, step, 0)

    lane = lane_of(LANES)
    channel = lax.broadcasted_iota(jnp.int32, (LANES, LANES), 0)
    total = jnp.zeros((p.table_rows, LANES), F32)
    for cg in range(p.groups):
        pick = (lane // p.block + cg * p.per == channel) & (lane < p.per * p.block)
        total = total + lax.dot_general(
            lines[cg],
            jnp.where(pick, 1.0, 0.0),
            (((1,), (1,)), ((), ())),
            precision=lax.Precision.HIGHEST,
            preferred_element_type=F32,
        )
    out[...] = total


def pass_body(value, *refs):
    refs[-1][...] = value[...]


def unpack_body(p, *refs):
    out, stage = refs[-2:]
    me = lax.axis_index("gx")
    spot = lane_of(p.rows) // p.window

    def step(pack, carry, pieces, base):
        for xp in range(p.cells_x):
            values = [pieces[d][pack, xp].astype(F32) for d in range(p.ring)]
            for b in range(p.ring):
                total = values[0]
                for d in range(1, p.ring):
                    total = jnp.where(spot == lax.rem(b + me + d, p.ring), values[d], total)
                total = pltpu.roll(total, (LANES - p.window * b) % LANES, 1) if b else total
                stage[b, pl.ds(xp, p.rows, stride=p.cells_x), :] = total
        for b in range(p.ring):
            out[(base + pack) * p.ring + b] = stage[b].astype(BF16)
        return carry

    base = 0
    for i in range(0, len(refs) - 2, p.ring):
        pieces = refs[i : i + p.ring]
        size = pieces[0].shape[0]
        lax.fori_loop(0, size, functools.partial(step, pieces=pieces, base=base), 0)
        base += size


def rotation(size, by):
    return [(i, (i + by) % size) for i in range(size)]


def sum_over(value, axis):
    size = lax.axis_size(axis)
    return sum((lax.ppermute(value, axis, rotation(size, d)) for d in range(1, size)), value)


def sum_near(value):
    col, gz = lax.axis_size("col"), lax.axis_size("gz")
    total = value
    for d in range(1, col * gz):
        pairs = [
            (i * col + j, (i + d // col) % gz * col + (j + d) % col)
            for i in range(gz)
            for j in range(col)
        ]
        total = total + lax.ppermute(value, ("gz", "col"), pairs)
    return total


def band_rows(grid_index, stretch):
    levels = stretch.shape[0]
    onehot = (grid_index[:, None] == jnp.arange(levels, dtype=jnp.int32)[None, :]).astype(F32)
    return jnp.dot(onehot, stretch, precision=lax.Precision.HIGHEST)


def by_windows(features, labels, grid_index, stretch, tile_filter, wall_filter, class_weight):
    chans, rows, cells_x, cells_z = features.shape
    classes = class_weight.shape[0]
    ring, gz = lax.axis_size("gx"), lax.axis_size("gz")
    p = Plan(ring, chans, rows, cells_x, cells_z, classes)
    volume = labels.shape[0] * cells_x * ring * cells_z * gz
    tall = rows * cells_x
    cuts, packs = p.cuts()

    field = features.reshape(chans, tall, cells_z)
    marks = labels.reshape(labels.shape[0] * cells_x, cells_z)
    (edge,) = call(
        functools.partial(edge_body, p),
        [jax.ShapeDtypeStruct((p.edge_groups, tall, LANES), BF16)],
        (field, marks),
    )
    left = lax.ppermute(edge, "gz", rotation(gz, 1))
    right = left if gz == 2 else lax.ppermute(edge, "gz", rotation(gz, -1))

    windows = call(
        functools.partial(pack_body, p, cuts),
        [
            jax.ShapeDtypeStruct((last - first, cells_x, rows, LANES), BF16)
            for first, last in cuts
            for d in range(ring)
        ],
        (field, marks, left, right),
        [pltpu.VMEM((ring, tall, LANES), F32)],
    )

    bands = band_rows(grid_index, stretch)
    half = WALL // 2
    near = lax.dynamic_slice_in_dim(
        jnp.pad(bands, ((half, half), (0, 0))), lax.axis_index("col") * rows, p.reach_rows, 0
    )
    near = jnp.broadcast_to(near.T[:, :, None], (WALL, p.reach_rows, LANES))
    params = jnp.concatenate([tile_filter.T, wall_filter.T, class_weight], axis=0)
    extra = (jnp.arange(params.shape[0]) == CENTRE).astype(F32)[:, None]
    params = jnp.concatenate([params, extra], axis=1).reshape(-1, p.groups, p.per, 1)
    table = jnp.broadcast_to(params, params.shape[:3] + (p.block,))
    table = table.reshape(params.shape[0], p.groups, p.per * p.block)
    table = jnp.pad(
        table,
        ((0, p.table_rows - table.shape[0]), (0, 0), (0, LANES - p.per * p.block)),
    ).transpose(1, 0, 2)

    def shape(*sizes, kind=BF16):
        return jax.ShapeDtypeStruct(sizes, kind)

    column = pltpu.VMEM((p.xs, rows + 2 * WALL_HALO, LANES), F32)
    wall = pltpu.VMEM((p.xs, p.reach_rows, LANES), F32)
    smooths, rims, pieces, hiddens, slopes, score = [], [], [], [], [], ()
    for chunk, (first, last) in enumerate(cuts):
        size = last - first
        sent = windows[chunk * ring : (chunk + 1) * ring]
        got = [sent[0]] + [
            lax.ppermute(sent[d], "gx", rotation(ring, d)) for d in range(1, ring)
        ]
        final = last == p.groups
        smooth, hidden, slope, *score = call(
            functools.partial(forward_body, p, first, size, final),
            [
                shape(size, p.xs, rows, LANES),
                shape(size, p.xs, p.reach_rows, LANES, kind=F32),
                shape(size, p.xs, p.reach_rows, LANES, kind=F32),
                shape(classes, p.xs, p.reach_rows, LANES, kind=F32),
                shape(p.groups if final else size, p.xs // 2, 16, LANES),
            ],
            (table, near, *got, *score[:1], *(rims if final else [])),
            [column],
            micros=0.001,
        )
        rims.append(score[1])
        smooths, pieces = smooths + [smooth], pieces + got
        hiddens, slopes = hiddens + [hidden], slopes + [slope]
    score = score[0]
    rim = lax.ppermute(rims[-1], "col", rotation(2, 1))

    sizes = [last - first for first, last in cuts]
    early = sizes[:-1]
    solved = call(
        functools.partial(backward_body, p, cuts, packs[0]),
        [shape(packs[0], cells_x, rows, LANES)] * ring
        + [
            shape(classes, p.xs, p.reach_rows, LANES, kind=F32),
            shape(classes, p.xs, rows, LANES, kind=F32),
            shape(p.groups, p.xs, 8, LANES, kind=F32),
            shape(p.groups, p.xs, 8, LANES, kind=F32),
        ]
        + [shape(size, p.xs, rows, LANES) for size in early] * 2,
        (table, near, score, rim, *smooths, *slopes[:-1]),
        [wall, pltpu.VMEM((sum(early), p.xs, rows, LANES), F32), column],
        micros=5,
    )
    sent, solved = solved[:ring], solved[ring:]
    score, errors, hidden_near, slope_near, *grads = solved
    back = [sent[0]] + [
        lax.ppermute(sent[d], "gx", rotation(ring, -d)) for d in range(1, ring)
    ]
    *sent, sums = call(
        functools.partial(finish_body, p, cuts, packs[1]),
        [shape(packs[1], cells_x, rows, LANES)] * ring + [shape(p.table_rows, LANES, kind=F32)],
        (
            *(table, near, score, errors, hidden_near, slope_near, rim, slopes[-1]),
            *hiddens, *smooths, *pieces, *grads,
        ),
        [
            wall,
            pltpu.VMEM((sizes[-1], p.xs, rows, LANES), F32),
            pltpu.VMEM((sizes[-1], p.xs, rows, LANES), BF16),
            pltpu.VMEM((sizes[-1], p.xs, rows, LANES), BF16),
            column,
            pltpu.VMEM((p.groups, p.table_rows, LANES), F32),
        ],
        micros=0.01,
    )
    (sums,) = call(
        pass_body,
        [shape(p.table_rows, LANES, kind=F32)],
        (sums, *back[1:]),
        micros=0.1,
        unread=ring - 1,
    )
    back += [sent[0]] + [
        lax.ppermute(sent[d], "gx", rotation(ring, -d)) for d in range(1, ring)
    ]
    sums = sum_over(sums, "gx")
    (sums,) = call(
        pass_body,
        [shape(p.table_rows, LANES, kind=F32)],
        (sums, *back[ring + 1 :]),
        micros=0.1,
        unread=ring - 1,
    )
    sums = sum_near(sums)
    sums = sums / volume
    (grad_field,) = call(
        functools.partial(unpack_body, p),
        [jax.ShapeDtypeStruct((chans, tall, cells_z), BF16)],
        back,
        [pltpu.VMEM((ring, tall, LANES), F32)],
    )
    return (
        grad_field.reshape(features.shape),
        sums[:ROW_WALL, :chans].T,
        sums[ROW_WALL:ROW_CLASS, :chans].T,
        sums[ROW_CLASS : ROW_CLASS + classes, :chans],
    )


def with_halo(value, sides, width):
    for axis, dim in sides:
        size, length = (lax.axis_size(axis), value.shape[dim])
        up = [(i, (i + 1) % size) for i in range(size)]
        down = [(j, i) for i, j in up]
        last = lax.slice_in_dim(value, length - width, length, axis=dim)
        leading = lax.slice_in_dim(value, 0, width, axis=dim)
        before = lax.ppermute(last, axis, up)
        after = lax.ppermute(leading, axis, down)
        value = jnp.concatenate([before, value, after], axis=dim)
    return value


def rim_tiles(field):
    return with_halo(field, (("gx", 2), ("gz", 3)), 2)


def wall_forward(smooth_ext, wall_rows, band_rows):
    rows = band_rows.shape[0]
    total = jnp.zeros((smooth_ext.shape[0], rows) + smooth_ext.shape[2:], jnp.float32)
    for k in range(9):
        tap = wall_rows[:, k][:, None] * band_rows[:, k][None, :]
        total = total + tap[:, :, None, None] * smooth_ext[:, k : k + rows].astype(jnp.float32)
    return total


def wall_backward(grad_ext, wall_rows, band_ext, rows):
    total = jnp.zeros((grad_ext.shape[0], rows) + grad_ext.shape[2:], jnp.float32)
    for k in range(9):
        first = 8 - k
        tap = wall_rows[:, k][:, None] * band_ext[first : first + rows, k][None, :]
        total = total + tap[:, :, None, None] * grad_ext[:, first : first + rows].astype(
            jnp.float32
        )
    return total


def by_halos(features, labels, grid_index, stretch, tile_filter, wall_filter, class_weight):
    chans, half_rows, cells_x, cells_z = features.shape
    all_rows = labels.shape[0]
    classes = class_weight.shape[0]
    volume = all_rows * cells_x * lax.axis_size("gx") * cells_z * lax.axis_size("gz")
    widened = rim_tiles(features)
    smooth = jnp.zeros(features.shape, jnp.float32)
    for i in range(5):
        for j in range(5):
            weight = tile_filter[:, 5 * i + j][:, None, None, None]
            smooth = smooth + weight * widened[:, :, i : i + cells_x, j : j + cells_z].astype(
                jnp.float32
            )
    smoothed = smooth.astype(jnp.bfloat16)
    bands = band_rows(grid_index, stretch)
    bands_pad = jnp.pad(bands, ((4, 4), (0, 0)))
    place = lax.axis_index("col")
    share = chans // lax.axis_size("col")
    first_chan = place * share
    pencil = lax.all_to_all(smoothed, "col", split_axis=0, concat_axis=1, tiled=True)
    smooth_ext = jnp.pad(pencil, ((0, 0), (4, 4), (0, 0), (0, 0)))
    wall_rows = lax.dynamic_slice_in_dim(wall_filter, first_chan, share, 0)
    class_rows = lax.dynamic_slice_in_dim(class_weight, first_chan, share, 1)
    wall_out = wall_forward(smooth_ext, wall_rows, bands)
    sig = jax.nn.sigmoid(wall_out)
    hidden = wall_out * sig
    partial_scores = jnp.einsum(
        "kc,cyxz->kyxz", class_rows, hidden, precision=lax.Precision.HIGHEST
    )
    scores = lax.psum(partial_scores, "col")
    targets = (labels[None] == jnp.arange(classes, dtype=jnp.int32)[:, None, None, None]).astype(
        jnp.float32
    )
    errors = scores - targets
    grad_hidden = jnp.einsum("kc,kyxz->cyxz", class_rows, errors, precision=lax.Precision.HIGHEST)
    grad_wall = (grad_hidden * sig * (1.0 + wall_out * (1.0 - sig))).astype(jnp.bfloat16)
    class_part = jnp.einsum("kyxz,cyxz->kc", errors, hidden, precision=lax.Precision.HIGHEST)
    grad_vals = grad_wall.astype(jnp.float32)
    wall_part = jnp.stack(
        [
            jnp.sum(
                grad_vals
                * bands[:, k][None, :, None, None]
                * smooth_ext[:, k : k + all_rows].astype(jnp.float32),
                axis=(1, 2, 3),
            )
            for k in range(9)
        ],
        axis=1,
    )
    grad_ext = jnp.pad(grad_wall, ((0, 0), (4, 4), (0, 0), (0, 0)))
    grad_smooth = wall_backward(grad_ext, wall_rows, bands_pad, all_rows).astype(jnp.bfloat16)
    grad_tile = lax.all_to_all(grad_smooth, "col", split_axis=1, concat_axis=0, tiled=True)
    wall_full = lax.dynamic_update_slice_in_dim(
        jnp.zeros((chans, 9), jnp.float32), wall_part, first_chan, 0
    )
    class_full = lax.dynamic_update_slice_in_dim(
        jnp.zeros((classes, chans), jnp.float32), class_part, first_chan, 1
    )
    grad_widened = rim_tiles(grad_tile)
    grad_tile_vals = grad_tile.astype(jnp.float32)
    grad_field = jnp.zeros(features.shape, jnp.float32)
    tile_terms = []
    for i in range(5):
        for j in range(5):
            weight = tile_filter[:, 5 * i + j][:, None, None, None]
            grad_field = grad_field + weight * grad_widened[
                :, :, 4 - i : 4 - i + cells_x, 4 - j : 4 - j + cells_z
            ].astype(jnp.float32)
            shifted = widened[:, :, i : i + cells_x, j : j + cells_z].astype(jnp.float32)
            tile_terms.append(jnp.sum(shifted * grad_tile_vals, axis=(1, 2, 3)))
    tile_part = jnp.stack(tile_terms, axis=1)
    totals = lax.psum((tile_part, wall_full, class_full), ("gx", "gz", "col"))
    return (
        grad_field.astype(jnp.bfloat16),
        totals[0] / volume,
        totals[1] / volume,
        totals[2] / volume,
    )


def shards(features, labels, grid_index, stretch, tile_filter, wall_filter, class_weight):
    sizes = [lax.axis_size(axis) for axis in ("gx", "gz", "col")]
    plan = by_windows if fits(*sizes, *features.shape, class_weight.shape[0]) else by_halos
    return plan(features, labels, grid_index, stretch, tile_filter, wall_filter, class_weight)


def solution(mesh):
    return jax.shard_map(
        shards,
        mesh=mesh,
        in_specs=(
            P(None, "col", ("group", "gx"), "gz"),
            P(None, ("group", "gx"), "gz"),
            P(),
            P(),
            P(),
            P(),
            P(),
        ),
        out_specs=(
            P(None, "col", ("group", "gx"), "gz"),
            P("group", None),
            P("group", None),
            P("group", None),
        ),
        check_vma=False,
    )
```

```python
import functools

import jax
import jax.numpy as jnp
from jax import lax
from jax.experimental import pallas as pl
from jax.experimental.pallas import tpu as pltpu
from jax.sharding import PartitionSpec as P

LANES = 128
TAPS = 5
REACH = 2
EDGE = 4
WALL = 9
WALL_HALO = 8
ROW_WALL = TAPS * TAPS
ROW_CLASS = ROW_WALL + WALL
CENTRE = ROW_WALL // 2
F32, BF16 = jnp.float32, jnp.bfloat16


class Plan:
    def __init__(self, ring, chans, rows, cells_x, cells_z, classes):
        self.ring, self.chans, self.rows, self.cells_x = ring, chans, rows, cells_x
        self.classes = classes
        self.window = cells_z // ring
        self.block = self.window + 2 * EDGE
        self.per = LANES // self.block
        self.slots = chans + 1
        self.groups = self.slots // self.per
        self.xs = ring * cells_x
        self.packs = chans // ring
        self.reach_rows = rows + 2 * (WALL_HALO // 2)
        self.edge_slots = LANES // (2 * EDGE)
        self.edge_groups = -(-self.slots // self.edge_slots)
        self.table_rows = -(-(ROW_CLASS + classes) // 8) * 8


    def cuts(self):
        tail = -(-self.groups // 4)
        return ((0, self.groups - tail), (self.groups - tail, self.groups))


def fits(ring, gz, col, chans, rows, cells_x, cells_z, classes):
    if cells_z != LANES or cells_x != 2 or col != 2 or ring < 2 or ring > 4 or LANES % ring:
        return False
    block = LANES // ring + 2 * EDGE
    per = LANES // block
    return (chans + 1) % per == 0 and chans % ring == 0 and rows % 16 == 0 and ring * cells_x >= TAPS


def vmem(count):
    return [pl.BlockSpec(memory_space=pltpu.VMEM)] * count


def call(body, outs, args, scratch=(), micros=1.0, unread=0, scalars={}):
    return pl.pallas_call(
        body,
        out_shape=outs,
        in_specs=[
            *(scalars.get(i, spec) for i, spec in enumerate(vmem(len(args) - unread))),
            *[pl.BlockSpec(memory_space=pl.ANY)] * unread,
        ],
        cost_estimate=pl.CostEstimate(
            flops=0, bytes_accessed=int(3.0e6 * micros), transcendentals=0
        ),
        out_specs=vmem(len(outs)),
        scratch_shapes=list(scratch),
        compiler_params=pltpu.CompilerParams(vmem_limit_bytes=40 * 2**20),
    )(*args)


def lane_of(rows):
    return lax.broadcasted_iota(jnp.int32, (rows, LANES), 1)


def edge_body(p, field, labels, out):
    core = lax.axis_index("col")
    tall = p.rows * p.cells_x
    lane = lane_of(tall)

    def group(g, count, fetch):
        total = jnp.zeros((tall, LANES), F32)
        for e in range(count):
            moved = pltpu.roll(fetch(g * p.edge_slots + e), (2 * EDGE * e + EDGE) % LANES, 1)
            total = jnp.where(lane // (2 * EDGE) == e, moved, total)
        out[g] = total.astype(BF16)

    def step(g, carry):
        group(g, p.edge_slots, lambda c: field[c].astype(F32))
        return carry

    full = p.chans // p.edge_slots
    lax.fori_loop(0, full, step, 0)
    own = labels[pl.ds(pl.multiple_of(core * tall, 8), tall), :].astype(F32)
    group(full, p.slots - full * p.edge_slots, lambda c: own)


def pack_body(p, cuts, field, labels, left, right, *refs):
    outs, stage = refs[:-1], refs[-1]
    ring = p.ring
    me, core = lax.axis_index("gx"), lax.axis_index("col")
    tall = p.rows * p.cells_x
    lane = lane_of(tall)
    takes = [lax.rem(me + d, ring) for d in range(ring)]
    fixes = [
        ((lane >= LANES - EDGE) & (k == 0)) | ((lane < EDGE) & (k == ring - 1)) for k in takes
    ]
    older = lane % (2 * EDGE) < EDGE

    def edges(c):
        g, e = c // p.edge_slots, c % p.edge_slots
        both = jnp.where(older, left[g].astype(F32), right[g].astype(F32))
        return pltpu.roll(both, LANES - EDGE - 2 * EDGE * e, 1)

    def group(cg, fetch, chunk, first):
        values = [fetch(cg * p.per + b) for b in range(p.per)]
        rims = [edges(cg * p.per + b) for b in range(p.per)]
        for d in range(ring):
            total = jnp.zeros((tall, LANES), F32)
            for b in range(p.per):
                shift = lax.rem(2 * LANES + p.block * b + EDGE - p.window * takes[d], LANES)
                moved = pltpu.roll(jnp.where(fixes[d], rims[b], values[b]), shift, 1)
                total = jnp.where(lane // p.block == b, moved, total)
            stage[d] = total
            for xp in range(p.cells_x):
                outs[chunk * ring + d][cg - first, xp] = stage[
                    d, pl.ds(xp, p.rows, stride=p.cells_x), :
                ].astype(BF16)

    own = labels[pl.ds(pl.multiple_of(core * tall, 8), tall), :].astype(F32)
    for chunk, (first, last) in enumerate(cuts):
        tail = last == p.groups

        def step(cg, carry, chunk=chunk, first=first):
            group(cg, lambda c: field[c].astype(F32), chunk, first)
            return carry

        lax.fori_loop(first, last - 1 if tail else last, step, 0)
        if tail:
            group(last - 1, lambda c: field[c].astype(F32) if c < p.chans else own, chunk, first)


def cell_of(p, d, xp):
    return (xp - p.cells_x * d) % p.xs


def smooth_group(p, table, cg, pieces, g, store):
    weights = [table[cg, pl.ds(t, 1), :] for t in range(ROW_WALL)]
    for part in range(p.rows // 16):
        cells = {}
        for d in range(p.ring):
            for xp in range(p.cells_x):
                cells[cell_of(p, d, xp)] = pieces[d][g, xp, pl.ds(16 * part, 16), :].astype(F32)
        for x in range(p.xs):
            total = None
            for j in range(TAPS):
                line = None
                for i in range(TAPS):
                    term = weights[TAPS * i + j] * cells[(x + i - REACH) % p.xs]
                    line = term if line is None else line + term
                if j != REACH:
                    line = pltpu.roll(line, (REACH - j) % LANES, 1)
                total = line if total is None else total + line
            store(x, 16 * part, total.astype(BF16))


def activate(value):
    sig = 0.5 * jnp.tanh(0.5 * value) + 0.5
    act = value * sig
    return act, sig + act * (1.0 - sig)


def forward_body(p, first, count, last, table, bands, *refs):
    refs = list(refs)

    def take(number):
        taken = refs[:number]
        del refs[:number]
        return taken

    pieces = take(p.ring)
    before = take(1 if first else 0)
    rims = take(len(refs) - 6 if last else 0)
    smooth, hidden, slope, score, rim, column = refs
    core = lax.axis_index("col")
    blocks = p.reach_rows // 8
    score[...] = before[0][...] if first else jnp.zeros_like(score)
    for x in range(p.xs):
        column[x, pl.ds(0, WALL_HALO), :] = jnp.zeros((WALL_HALO, LANES), F32)
        column[x, pl.ds(WALL_HALO + p.rows, WALL_HALO), :] = jnp.zeros((WALL_HALO, LANES), F32)
    base = 0
    for other in rims:
        rim[pl.ds(base, other.shape[0])] = other[...]
        base += other.shape[0]

    def step(g, carry):
        cg = first + g

        def store(x, row, value):
            smooth[g, x, pl.ds(row, 16), :] = value
            column[x, pl.ds(WALL_HALO + row, 16), :] = value.astype(F32)

        smooth_group(p, table, cg, pieces, g, store)
        for pair in range(p.xs // 2):
            cells = (2 * pair, 2 * pair + 1)
            tops = [column[x, pl.ds(WALL_HALO, 8), :] for x in cells]
            lows = [column[x, pl.ds(p.rows, 8), :] for x in cells]
            rim[base + g, pair] = jnp.where(
                core == 0, jnp.concatenate(lows, axis=0), jnp.concatenate(tops, axis=0)
            ).astype(BF16)
        taps = [table[cg, pl.ds(ROW_WALL + k, 1), :] for k in range(WALL)]
        classes = [table[cg, pl.ds(ROW_CLASS + k, 1), :] for k in range(p.classes)]
        for blk in range(blocks):
            rows = pl.ds(8 * blk, 8)
            sums = [None] * p.xs
            for k in range(WALL):
                tap = taps[k] * bands[k, rows, :]
                for x in range(p.xs):
                    term = tap * column[x, pl.ds(8 * blk + k, 8), :]
                    sums[x] = term if k == 0 else sums[x] + term
            for x in range(p.xs):
                hidden[g, x, rows, :], slope[g, x, rows, :] = act, _ = activate(sums[x])
                for k in range(p.classes):
                    score[k, x, rows, :] += classes[k] * act
        return carry

    lax.fori_loop(0, count, step, 0)


def fill_column(p, core, smooth, rim, g, cg, x, store):
    store(WALL_HALO, p.rows, smooth[g, x].astype(F32))
    near = rim[cg, x // 2].astype(F32)[8 * (x % 2) : 8 * (x % 2) + 8]
    store(0, WALL_HALO, jnp.where(core == 0, 0.0, near))
    store(WALL_HALO + p.rows, WALL_HALO, jnp.where(core == 0, near, 0.0))


def own_lanes(p, rows):
    lane = lane_of(rows)
    place = lane % p.block
    return (place >= EDGE) & (place < EDGE + p.window) & (lane < p.per * p.block)


def spread(p, value, lane):
    total = value
    for b in range(p.per - 1):
        moved = pltpu.roll(value, LANES - p.block * (p.per - 1 - b), 1)
        total = jnp.where(lane // p.block == b, moved, total)
    return total


def near_block(p, core):
    return pl.multiple_of(jnp.where(core == 0, p.reach_rows - 8, 0), 8)


def edge_rows(p, core, cuts, table, bands, smooths, rim, score, hidden_near, slope_near):
    base = near_block(p, core)
    rows = pl.ds(base, 8)
    for k in range(p.classes):
        for x in range(p.xs):
            score[k, x, rows, :] = jnp.zeros((8, LANES), F32)

    for chunk, (first, last) in enumerate(cuts):

        def step(g, carry, chunk=chunk, first=first):
            cg = first + g
            taps = [
                table[cg, pl.ds(ROW_WALL + k, 1), :] * bands[k, rows, :] for k in range(WALL)
            ]
            classes = [table[cg, pl.ds(ROW_CLASS + k, 1), :] for k in range(p.classes)]
            for x in range(p.xs):
                near = rim[cg, x // 2].astype(F32)[8 * (x % 2) : 8 * (x % 2) + 8]
                low = smooths[chunk][g, x, pl.ds(p.rows - 16, 16), :].astype(F32)[8:]
                top = smooths[chunk][g, x, pl.ds(0, 16), :].astype(F32)[:8]
                hidden_near[cg, x] = jnp.where(core == 0, low, near)
                slope_near[cg, x] = jnp.where(core == 0, near, top)
            sums = []
            for x in range(p.xs):
                both = jnp.concatenate([hidden_near[cg, x], slope_near[cg, x]], axis=0)
                total = taps[0] * both[:8]
                for k in range(1, WALL):
                    total = total + taps[k] * both[k : k + 8]
                sums.append(total)
            for x in range(p.xs):
                act, bend = activate(sums[x])
                hidden_near[cg, x], slope_near[cg, x] = act, bend
                for k in range(p.classes):
                    score[k, x, rows, :] += classes[k] * act
            return carry

        lax.fori_loop(0, last - first, step, 0)


def judge(p, core, smooth, rim, score, errors, column):
    lane = lane_of(8)
    half = WALL // 2
    for x in range(p.xs):

        def store(start, length, value, x=x):
            column[x, pl.ds(start, length), :] = value

        fill_column(p, core, smooth, rim, smooth.shape[0] - 1, p.groups - 1, x, store)

    def step(blk, carry):
        rows = pl.ds(pl.multiple_of(8 * blk, 8), 8)
        place = core * p.rows - half + 8 * blk + lax.broadcasted_iota(jnp.int32, (8, LANES), 0)
        inside = (place >= 0) & (place < 2 * p.rows)
        for x in range(p.xs):
            label = spread(p, column[x, pl.ds(8 * blk + half, 8), :], lane)
            for k in range(p.classes):
                value = score[k, x, rows, :]
                total = value
                for b in range(1, p.per):
                    total = total + pltpu.roll(value, p.block * b, 1)
                error = spread(p, total, lane) - jnp.where(label == k, 1.0, 0.0)
                score[k, x, rows, :] = jnp.where(inside, error, 0.0)
        return carry

    lax.fori_loop(0, p.reach_rows // 8, step, 0)
    own = own_lanes(p, p.rows)
    for k in range(p.classes):
        for x in range(p.xs):
            errors[k, x] = jnp.where(own, score[k, x, pl.ds(half, p.rows), :], 0.0)


def with_near(p, core, blk, value, near):
    if blk == 0:
        return jnp.where(core == 0, value, near)
    if blk == p.reach_rows // 8 - 1:
        return jnp.where(core == 0, near, value)
    return value


def backward_groups(
    p, first, count, table, bands, score, slope, slope_near, grad_smooth, grad_wall, wall, field
):
    core = lax.axis_index("col")
    half = WALL // 2
    own = own_lanes(p, p.rows)

    def step(g, carry):
        cg = first + g
        taps = [table[cg, pl.ds(ROW_WALL + k, 1), :] for k in range(WALL)]
        classes = [table[cg, pl.ds(ROW_CLASS + k, 1), :] for k in range(p.classes)]
        for blk in range(p.reach_rows // 8):
            rows = pl.ds(8 * blk, 8)
            for x in range(p.xs):
                grad = classes[0] * score[0, x, rows, :]
                for k in range(1, p.classes):
                    grad = grad + classes[k] * score[k, x, rows, :]
                bend = with_near(p, core, blk, slope[g, x, rows, :], slope_near[cg, x])
                wall[x, rows, :] = (grad * bend).astype(BF16).astype(F32)
        for x in range(p.xs):
            grad_wall[g, x] = jnp.where(own, wall[x, pl.ds(half, p.rows), :], 0.0).astype(BF16)
        for part in range(p.rows // 16):
            sums = [None] * p.xs
            for k in range(WALL):
                rows = pl.ds(16 * part + WALL - 1 - k, 16)
                tap = taps[k] * bands[k, rows, :]
                for x in range(p.xs):
                    term = tap * wall[x, rows, :]
                    sums[x] = term if k == 0 else sums[x] + term
            for x in range(p.xs):
                grad_smooth[g, x, pl.ds(16 * part, 16), :] = sums[x].astype(BF16)
        weights = [table[cg, pl.ds(t, 1), :] for t in range(ROW_WALL)]
        for part in range(p.rows // 16):
            rows = pl.ds(16 * part, 16)
            cells = [grad_smooth[g, x, rows, :].astype(F32) for x in range(p.xs)]
            for x in range(p.xs):
                total = None
                for j in range(TAPS):
                    line = None
                    for i in range(TAPS):
                        term = weights[TAPS * i + j] * cells[(x - i + REACH) % p.xs]
                        line = term if line is None else line + term
                    if j != REACH:
                        line = pltpu.roll(line, (j - REACH) % LANES, 1)
                    total = line if total is None else total + line
                field[g, x, rows, :] = total
        return carry

    lax.fori_loop(0, count, step, 0)


def ship(p, packs, field, results):
    me = lax.axis_index("gx")
    wide = lane_of(p.rows) // p.window

    def step(pack, carry):
        totals = [jnp.zeros((p.rows, LANES), F32)] * p.xs
        for b in range(p.ring):
            c = pack * p.ring + b
            spot = lax.rem(b + me, p.ring)
            shift = lax.rem(2 * LANES + p.window * spot - p.block * (c % p.per) - EDGE, LANES)
            for x in range(p.xs):
                moved = pltpu.roll(field[c // p.per, x], shift, 1)
                totals[x] = jnp.where(wide == spot, moved, totals[x])
        for d in range(p.ring):
            for xp in range(p.cells_x):
                results[d][pack, xp] = totals[cell_of(p, d, xp)].astype(BF16)
        return carry

    lax.fori_loop(0, packs, step, 0)


def backward_body(p, cuts, table, bands, score_in, rim, *refs):
    count = len(cuts)
    smooths, slopes, refs = refs[:count], refs[count : 2 * count], refs[2 * count :]
    results, refs = refs[: p.ring], refs[p.ring :]
    errors, hidden_near, grad_smooth, grad_wall = refs[:4]
    score, slope_near, wall, field, column = refs[4:]
    core = lax.axis_index("col")
    score[...] = score_in[...]
    edge_rows(p, core, cuts, table, bands, smooths, rim, score, hidden_near, slope_near)
    judge(p, core, smooths[-1], rim, score, errors, column)
    for (first, last), slope in zip(cuts, slopes):
        own = pl.ds(first, last - first)
        backward_groups(
            p, first, last - first, table, bands, score, slope, slope_near,
            grad_smooth.at[own], grad_wall.at[own], wall, field.at[own],
        )
    ship(p, p.packs, field, results)


def weight_body(
    p, cuts, bands, errors, hidden_near, rim, grad_smooth, grad_wall, *refs
):
    count = len(cuts)
    refs = list(refs)

    def take(number):
        taken = refs[:number]
        del refs[:number]
        return taken

    hiddens, smooths = take(count), take(count)
    pieces = [take(p.ring) for i in range(count)]
    out, wall, column, lines = refs
    core = lax.axis_index("col")
    half = WALL // 2
    own = own_lanes(p, 16)
    lines[...] = jnp.zeros_like(lines)

    def fold(value):
        total = value[:8]
        for r in range(8, value.shape[0], 8):
            total = total + value[r : r + 8]
        return jnp.sum(total, axis=0, keepdims=True)

    for chunk, (first, last) in enumerate(cuts):

        def step(g, carry, chunk=chunk, first=first):
            cg = first + g
            sums = [None] * ROW_WALL
            for part in range(p.rows // 16):
                rows = pl.ds(16 * part, 16)
                cells = {}
                for d in range(p.ring):
                    for xp in range(p.cells_x):
                        cells[cell_of(p, d, xp)] = pieces[chunk][d][g, xp, rows, :].astype(F32)
                for x in range(p.xs):
                    grad = jnp.where(own, grad_smooth[cg, x, rows, :].astype(F32), 0.0)
                    for j in range(TAPS):
                        moved = grad if j == REACH else pltpu.roll(grad, (j - REACH) % LANES, 1)
                        for i in range(TAPS):
                            t = TAPS * i + j
                            term = cells[(x + i - REACH) % p.xs] * moved
                            term = term[:8] + term[8:]
                            sums[t] = term if sums[t] is None else sums[t] + term
            for t in range(ROW_WALL):
                lines[cg, pl.ds(t, 1), :] = fold(sums[t])
            for x in range(p.xs):

                def store(start, length, value, x=x):
                    column[x, pl.ds(start, length), :] = value

                fill_column(p, core, smooths[chunk], rim, g, cg, x, store)
            grads = [grad_wall[cg, x].astype(F32) for x in range(p.xs)]
            for k in range(WALL):
                total = None
                for x in range(p.xs):
                    term = grads[x] * column[x, pl.ds(half + k, p.rows), :]
                    total = term if total is None else total + term
                lines[cg, pl.ds(ROW_WALL + k, 1), :] = fold(
                    total * bands[k, pl.ds(half, p.rows), :]
                )
            for x in range(p.xs):
                for blk in range(p.reach_rows // 8):
                    rows = pl.ds(8 * blk, 8)
                    wall[x, rows, :] = with_near(
                        p, core, blk, hiddens[chunk][g, x, rows, :], hidden_near[cg, x]
                    )
            for k in range(p.classes):
                total = None
                for x in range(p.xs):
                    term = errors[k, x] * wall[x, pl.ds(half, p.rows), :]
                    total = term if total is None else total + term
                lines[cg, pl.ds(ROW_CLASS + k, 1), :] = fold(total)
            return carry

        lax.fori_loop(0, last - first, step, 0)

    lane = lane_of(LANES)
    channel = lax.broadcasted_iota(jnp.int32, (LANES, LANES), 0)
    total = jnp.zeros((p.table_rows, LANES), F32)
    for cg in range(p.groups):
        pick = (lane // p.block + cg * p.per == channel) & (lane < p.per * p.block)
        total = total + lax.dot_general(
            lines[cg],
            jnp.where(pick, 1.0, 0.0),
            (((1,), (1,)), ((), ())),
            precision=lax.Precision.HIGHEST,
            preferred_element_type=F32,
        )
    out[...] = total


def pass_body(value, *refs):
    refs[-1][...] = value[...]


def unpack_body(p, *refs):
    out, stage = refs[-2:]
    me = lax.axis_index("gx")
    spot = lane_of(p.rows) // p.window

    def step(pack, carry, pieces, base):
        for xp in range(p.cells_x):
            values = [pieces[d][pack, xp].astype(F32) for d in range(p.ring)]
            for b in range(p.ring):
                total = values[0]
                for d in range(1, p.ring):
                    total = jnp.where(spot == lax.rem(b + me + d, p.ring), values[d], total)
                total = pltpu.roll(total, (LANES - p.window * b) % LANES, 1) if b else total
                stage[b, pl.ds(xp, p.rows, stride=p.cells_x), :] = total
        for b in range(p.ring):
            out[(base + pack) * p.ring + b] = stage[b].astype(BF16)
        return carry

    base = 0
    for i in range(0, len(refs) - 2, p.ring):
        pieces = refs[i : i + p.ring]
        size = pieces[0].shape[0]
        lax.fori_loop(0, size, functools.partial(step, pieces=pieces, base=base), 0)
        base += size


def rotation(size, by):
    return [(i, (i + by) % size) for i in range(size)]


def sum_over(value, axis):
    size = lax.axis_size(axis)
    return sum((lax.ppermute(value, axis, rotation(size, d)) for d in range(1, size)), value)


def near_parts(value):
    col, gz = lax.axis_size("col"), lax.axis_size("gz")
    parts = [value]
    for d in range(1, col * gz):
        pairs = [
            (i * col + j, (i + d // col) % gz * col + (j + d) % col)
            for i in range(gz)
            for j in range(col)
        ]
        parts.append(lax.ppermute(value, ("gz", "col"), pairs))
    return parts


def table_body(p, tile, wall, classes, levels, stretch, *refs):
    table, near = refs[-2:]
    core = lax.axis_index("col")
    lane = lax.broadcasted_iota(jnp.int32, (p.chans, LANES), 1)
    channel = lax.broadcasted_iota(jnp.int32, (p.chans, LANES), 0)

    def spread_rows(value, pick, dim):
        return lax.dot_general(
            value, pick, (((dim,), (0,)), ((), ())),
            precision=lax.Precision.HIGHEST, preferred_element_type=F32,
        )

    for cg in range(p.groups):
        pick = (lane // p.block + cg * p.per == channel) & (lane < p.per * p.block)
        pick = jnp.where(pick, 1.0, 0.0)
        table[cg, pl.ds(0, ROW_WALL), :] = spread_rows(tile[...], pick, 0)
        table[cg, pl.ds(ROW_WALL, WALL), :] = spread_rows(wall[...], pick, 1)
        table[cg, pl.ds(ROW_CLASS, p.classes), :] = spread_rows(classes[...], pick, 1)
    marks = lane_of(1)
    marks = (marks // p.block == p.per - 1) & (marks < p.per * p.block)
    last = table[p.groups - 1, pl.ds(CENTRE, 1), :]
    table[p.groups - 1, pl.ds(CENTRE, 1), :] = jnp.where(marks, 1.0, last)

    def step(q, carry):
        y = jnp.clip(core * p.rows - WALL // 2 + q, 0, 2 * p.rows - 1)
        level = levels[y]
        for k in range(WALL):
            near[k, pl.ds(q, 1), :] = jnp.full((1, LANES), stretch[level, k], F32)
        return carry

    lax.fori_loop(0, p.reach_rows, step, 0)


def sums_body(p, volume, *refs):
    tile, wall, classes = refs[-3:]
    total = refs[0][...]
    for ref in refs[1:-3]:
        total = total + ref[...]
    total = total * (1.0 / volume)
    rows = jnp.zeros((LANES - p.table_rows, LANES), F32)
    turned = jnp.concatenate([total, rows], axis=0).T
    tile[...] = turned[: p.chans, :ROW_WALL]
    wall[...] = total[ROW_WALL:ROW_CLASS, : p.chans]
    classes[...] = total[ROW_CLASS : ROW_CLASS + p.classes, : p.chans]


def band_rows(grid_index, stretch):
    levels = stretch.shape[0]
    onehot = (grid_index[:, None] == jnp.arange(levels, dtype=jnp.int32)[None, :]).astype(F32)
    return jnp.dot(onehot, stretch, precision=lax.Precision.HIGHEST)


def by_windows(features, labels, grid_index, stretch, tile_filter, wall_filter, class_weight):
    chans, rows, cells_x, cells_z = features.shape
    classes = class_weight.shape[0]
    ring, gz = lax.axis_size("gx"), lax.axis_size("gz")
    p = Plan(ring, chans, rows, cells_x, cells_z, classes)
    volume = labels.shape[0] * cells_x * ring * cells_z * gz
    tall = rows * cells_x
    cuts = p.cuts()

    field = features.reshape(chans, tall, cells_z)
    marks = labels.reshape(labels.shape[0] * cells_x, cells_z)
    (edge,) = call(
        functools.partial(edge_body, p),
        [jax.ShapeDtypeStruct((p.edge_groups, tall, LANES), BF16)],
        (field, marks),
    )
    left = lax.ppermute(edge, "gz", rotation(gz, 1))
    right = left if gz == 2 else lax.ppermute(edge, "gz", rotation(gz, -1))

    windows = call(
        functools.partial(pack_body, p, cuts),
        [
            jax.ShapeDtypeStruct((last - first, cells_x, rows, LANES), BF16)
            for first, last in cuts
            for d in range(ring)
        ],
        (field, marks, left, right),
        [pltpu.VMEM((ring, tall, LANES), F32)],
    )

    def shape(*sizes, kind=BF16):
        return jax.ShapeDtypeStruct(sizes, kind)

    smem = pl.BlockSpec(memory_space=pltpu.SMEM)
    table, near = call(
        functools.partial(table_body, p),
        [
            shape(p.groups, p.table_rows, LANES, kind=F32),
            shape(WALL, p.reach_rows, LANES, kind=F32),
        ],
        (tile_filter, wall_filter.T, class_weight, grid_index, stretch, windows[0]),
        micros=0.1,
        unread=1,
        scalars={3: smem, 4: smem},
    )
    column = pltpu.VMEM((p.xs, rows + 2 * WALL_HALO, LANES), F32)
    wall = pltpu.VMEM((p.xs, p.reach_rows, LANES), F32)
    smooths, rims, pieces, hiddens, slopes, score = [], [], [], [], [], ()
    for chunk, (first, last) in enumerate(cuts):
        size = last - first
        sent = windows[chunk * ring : (chunk + 1) * ring]
        got = [sent[0]] + [
            lax.ppermute(sent[d], "gx", rotation(ring, d)) for d in range(1, ring)
        ]
        final = last == p.groups
        smooth, hidden, slope, *score = call(
            functools.partial(forward_body, p, first, size, final),
            [
                shape(size, p.xs, rows, LANES),
                shape(size, p.xs, p.reach_rows, LANES, kind=F32),
                shape(size, p.xs, p.reach_rows, LANES, kind=F32),
                shape(classes, p.xs, p.reach_rows, LANES, kind=F32),
                shape(p.groups if final else size, p.xs // 2, 16, LANES),
            ],
            (table, near, *got, *score[:1], *(rims if final else [])),
            [column],
            micros=0.001,
        )
        rims.append(score[1])
        smooths, pieces = smooths + [smooth], pieces + got
        hiddens, slopes = hiddens + [hidden], slopes + [slope]
    score = score[0]
    rim = lax.ppermute(rims[-1], "col", rotation(2, 1))

    near_shape = (p.groups, p.xs, 8, LANES)
    *sent, errors, hidden_near, grad_smooth, grad_wall = call(
        functools.partial(backward_body, p, cuts),
        [shape(p.packs, cells_x, rows, LANES)] * ring
        + [
            shape(classes, p.xs, rows, LANES, kind=F32),
            shape(*near_shape, kind=F32),
            shape(p.groups, p.xs, rows, LANES),
            shape(p.groups, p.xs, rows, LANES),
        ],
        (table, near, score, rim, *smooths, *slopes),
        [
            pltpu.VMEM((classes, p.xs, p.reach_rows, LANES), F32),
            pltpu.VMEM(near_shape, F32),
            wall,
            pltpu.VMEM((p.groups, p.xs, rows, LANES), F32),
            column,
        ],
        micros=5,
    )
    back = [sent[0]] + [
        lax.ppermute(sent[d], "gx", rotation(ring, -d)) for d in range(1, ring)
    ]
    (sums,) = call(
        functools.partial(weight_body, p, cuts),
        [shape(p.table_rows, LANES, kind=F32)],
        (
            *(near, errors, hidden_near, rim, grad_smooth, grad_wall),
            *hiddens, *smooths, *pieces,
        ),
        [wall, column, pltpu.VMEM((p.groups, p.table_rows, LANES), F32)],
        micros=0.01,
    )
    (sums,) = call(
        pass_body,
        [shape(p.table_rows, LANES, kind=F32)],
        (sums, *back[1:]),
        micros=0.1,
        unread=ring - 1,
    )
    sums = sum_over(sums, "gx")
    (grad_field,) = call(
        functools.partial(unpack_body, p),
        [shape(chans, tall, cells_z)],
        back,
        [pltpu.VMEM((ring, tall, LANES), F32)],
    )
    grad_tile, grad_wall, grad_class = call(
        functools.partial(sums_body, p, volume),
        [
            shape(chans, ROW_WALL, kind=F32),
            shape(WALL, chans, kind=F32),
            shape(classes, chans, kind=F32),
        ],
        near_parts(sums),
        micros=0.1,
    )
    return grad_field.reshape(features.shape), grad_tile, grad_wall.T, grad_class


def with_halo(value, sides, width):
    for axis, dim in sides:
        size, length = (lax.axis_size(axis), value.shape[dim])
        up = [(i, (i + 1) % size) for i in range(size)]
        down = [(j, i) for i, j in up]
        last = lax.slice_in_dim(value, length - width, length, axis=dim)
        leading = lax.slice_in_dim(value, 0, width, axis=dim)
        before = lax.ppermute(last, axis, up)
        after = lax.ppermute(leading, axis, down)
        value = jnp.concatenate([before, value, after], axis=dim)
    return value


def rim_tiles(field):
    return with_halo(field, (("gx", 2), ("gz", 3)), 2)


def wall_forward(smooth_ext, wall_rows, band_rows):
    rows = band_rows.shape[0]
    total = jnp.zeros((smooth_ext.shape[0], rows) + smooth_ext.shape[2:], jnp.float32)
    for k in range(9):
        tap = wall_rows[:, k][:, None] * band_rows[:, k][None, :]
        total = total + tap[:, :, None, None] * smooth_ext[:, k : k + rows].astype(jnp.float32)
    return total


def wall_backward(grad_ext, wall_rows, band_ext, rows):
    total = jnp.zeros((grad_ext.shape[0], rows) + grad_ext.shape[2:], jnp.float32)
    for k in range(9):
        first = 8 - k
        tap = wall_rows[:, k][:, None] * band_ext[first : first + rows, k][None, :]
        total = total + tap[:, :, None, None] * grad_ext[:, first : first + rows].astype(
            jnp.float32
        )
    return total


def by_halos(features, labels, grid_index, stretch, tile_filter, wall_filter, class_weight):
    chans, half_rows, cells_x, cells_z = features.shape
    all_rows = labels.shape[0]
    classes = class_weight.shape[0]
    volume = all_rows * cells_x * lax.axis_size("gx") * cells_z * lax.axis_size("gz")
    widened = rim_tiles(features)
    smooth = jnp.zeros(features.shape, jnp.float32)
    for i in range(5):
        for j in range(5):
            weight = tile_filter[:, 5 * i + j][:, None, None, None]
            smooth = smooth + weight * widened[:, :, i : i + cells_x, j : j + cells_z].astype(
                jnp.float32
            )
    smoothed = smooth.astype(jnp.bfloat16)
    bands = band_rows(grid_index, stretch)
    bands_pad = jnp.pad(bands, ((4, 4), (0, 0)))
    place = lax.axis_index("col")
    share = chans // lax.axis_size("col")
    first_chan = place * share
    pencil = lax.all_to_all(smoothed, "col", split_axis=0, concat_axis=1, tiled=True)
    smooth_ext = jnp.pad(pencil, ((0, 0), (4, 4), (0, 0), (0, 0)))
    wall_rows = lax.dynamic_slice_in_dim(wall_filter, first_chan, share, 0)
    class_rows = lax.dynamic_slice_in_dim(class_weight, first_chan, share, 1)
    wall_out = wall_forward(smooth_ext, wall_rows, bands)
    sig = jax.nn.sigmoid(wall_out)
    hidden = wall_out * sig
    partial_scores = jnp.einsum(
        "kc,cyxz->kyxz", class_rows, hidden, precision=lax.Precision.HIGHEST
    )
    scores = lax.psum(partial_scores, "col")
    targets = (labels[None] == jnp.arange(classes, dtype=jnp.int32)[:, None, None, None]).astype(
        jnp.float32
    )
    errors = scores - targets
    grad_hidden = jnp.einsum("kc,kyxz->cyxz", class_rows, errors, precision=lax.Precision.HIGHEST)
    grad_wall = (grad_hidden * sig * (1.0 + wall_out * (1.0 - sig))).astype(jnp.bfloat16)
    class_part = jnp.einsum("kyxz,cyxz->kc", errors, hidden, precision=lax.Precision.HIGHEST)
    grad_vals = grad_wall.astype(jnp.float32)
    wall_part = jnp.stack(
        [
            jnp.sum(
                grad_vals
                * bands[:, k][None, :, None, None]
                * smooth_ext[:, k : k + all_rows].astype(jnp.float32),
                axis=(1, 2, 3),
            )
            for k in range(9)
        ],
        axis=1,
    )
    grad_ext = jnp.pad(grad_wall, ((0, 0), (4, 4), (0, 0), (0, 0)))
    grad_smooth = wall_backward(grad_ext, wall_rows, bands_pad, all_rows).astype(jnp.bfloat16)
    grad_tile = lax.all_to_all(grad_smooth, "col", split_axis=1, concat_axis=0, tiled=True)
    wall_full = lax.dynamic_update_slice_in_dim(
        jnp.zeros((chans, 9), jnp.float32), wall_part, first_chan, 0
    )
    class_full = lax.dynamic_update_slice_in_dim(
        jnp.zeros((classes, chans), jnp.float32), class_part, first_chan, 1
    )
    grad_widened = rim_tiles(grad_tile)
    grad_tile_vals = grad_tile.astype(jnp.float32)
    grad_field = jnp.zeros(features.shape, jnp.float32)
    tile_terms = []
    for i in range(5):
        for j in range(5):
            weight = tile_filter[:, 5 * i + j][:, None, None, None]
            grad_field = grad_field + weight * grad_widened[
                :, :, 4 - i : 4 - i + cells_x, 4 - j : 4 - j + cells_z
            ].astype(jnp.float32)
            shifted = widened[:, :, i : i + cells_x, j : j + cells_z].astype(jnp.float32)
            tile_terms.append(jnp.sum(shifted * grad_tile_vals, axis=(1, 2, 3)))
    tile_part = jnp.stack(tile_terms, axis=1)
    totals = lax.psum((tile_part, wall_full, class_full), ("gx", "gz", "col"))
    return (
        grad_field.astype(jnp.bfloat16),
        totals[0] / volume,
        totals[1] / volume,
        totals[2] / volume,
    )


def shards(features, labels, grid_index, stretch, tile_filter, wall_filter, class_weight):
    sizes = [lax.axis_size(axis) for axis in ("gx", "gz", "col")]
    plan = by_windows if fits(*sizes, *features.shape, class_weight.shape[0]) else by_halos
    return plan(features, labels, grid_index, stretch, tile_filter, wall_filter, class_weight)


def solution(mesh):
    return jax.shard_map(
        shards,
        mesh=mesh,
        in_specs=(
            P(None, "col", ("group", "gx"), "gz"),
            P(None, ("group", "gx"), "gz"),
            P(),
            P(),
            P(),
            P(),
            P(),
        ),
        out_specs=(
            P(None, "col", ("group", "gx"), "gz"),
            P("group", None),
            P("group", None),
            P("group", None),
        ),
        check_vma=False,
    )
```

```python
import functools

import jax
import jax.numpy as jnp
from jax import lax
from jax.experimental import pallas as pl
from jax.experimental.pallas import tpu as pltpu
from jax.sharding import PartitionSpec as P

LANES = 128
TAPS = 5
REACH = 2
EDGE = 4
WALL = 9
WALL_HALO = 8
ROW_WALL = TAPS * TAPS
ROW_CLASS = ROW_WALL + WALL
CENTRE = ROW_WALL // 2
F32, BF16 = jnp.float32, jnp.bfloat16


class Plan:
    def __init__(self, ring, chans, rows, cells_x, cells_z, classes):
        self.ring, self.chans, self.rows, self.cells_x = ring, chans, rows, cells_x
        self.classes = classes
        self.window = cells_z // ring
        self.block = self.window + 2 * EDGE
        self.per = LANES // self.block
        self.slots = chans + 1
        self.groups = self.slots // self.per
        self.xs = ring * cells_x
        self.packs = chans // ring
        self.reach_rows = rows + 2 * (WALL_HALO // 2)
        self.edge_slots = LANES // (2 * EDGE)
        self.edge_groups = -(-self.slots // self.edge_slots)
        self.table_rows = -(-(ROW_CLASS + classes) // 8) * 8


    def cuts(self):
        tail = -(-self.groups // 4)
        return ((0, self.groups - tail), (self.groups - tail, self.groups))


def fits(ring, gz, col, chans, rows, cells_x, cells_z, classes):
    if cells_z != LANES or cells_x != 2 or col != 2 or ring < 2 or ring > 4 or LANES % ring:
        return False
    block = LANES // ring + 2 * EDGE
    per = LANES // block
    return (chans + 1) % per == 0 and chans % ring == 0 and rows % 16 == 0 and ring * cells_x >= TAPS


def vmem(count):
    return [pl.BlockSpec(memory_space=pltpu.VMEM)] * count


def call(body, outs, args, scratch=(), micros=1.0, unread=0, scalars={}):
    return pl.pallas_call(
        body,
        out_shape=outs,
        in_specs=[
            *(scalars.get(i, spec) for i, spec in enumerate(vmem(len(args) - unread))),
            *[pl.BlockSpec(memory_space=pl.ANY)] * unread,
        ],
        cost_estimate=pl.CostEstimate(
            flops=0, bytes_accessed=int(3.0e6 * micros), transcendentals=0
        ),
        out_specs=vmem(len(outs)),
        scratch_shapes=list(scratch),
        compiler_params=pltpu.CompilerParams(vmem_limit_bytes=40 * 2**20),
    )(*args)


def lane_of(rows):
    return lax.broadcasted_iota(jnp.int32, (rows, LANES), 1)


def edge_body(p, field, labels, out):
    core = lax.axis_index("col")
    tall = p.rows * p.cells_x
    lane = lane_of(tall)

    def group(g, count, fetch):
        total = jnp.zeros((tall, LANES), F32)
        for e in range(count):
            moved = pltpu.roll(fetch(g * p.edge_slots + e), (2 * EDGE * e + EDGE) % LANES, 1)
            total = jnp.where(lane // (2 * EDGE) == e, moved, total)
        out[g] = total.astype(BF16)

    def step(g, carry):
        group(g, p.edge_slots, lambda c: field[c].astype(F32))
        return carry

    full = p.chans // p.edge_slots
    lax.fori_loop(0, full, step, 0)
    own = labels[pl.ds(pl.multiple_of(core * tall, 8), tall), :].astype(F32)
    group(full, p.slots - full * p.edge_slots, lambda c: own)


def pack_body(p, cuts, field, labels, left, right, *refs):
    outs, stage = refs[:-1], refs[-1]
    ring = p.ring
    me, core = lax.axis_index("gx"), lax.axis_index("col")
    tall = p.rows * p.cells_x
    lane = lane_of(tall)
    takes = [lax.rem(me + d, ring) for d in range(ring)]
    fixes = [
        ((lane >= LANES - EDGE) & (k == 0)) | ((lane < EDGE) & (k == ring - 1)) for k in takes
    ]
    older = lane % (2 * EDGE) < EDGE

    def edges(c):
        g, e = c // p.edge_slots, c % p.edge_slots
        both = jnp.where(older, left[g], right[g])
        return pltpu.roll(both, LANES - EDGE - 2 * EDGE * e, 1)

    def group(cg, fetch, chunk, first):
        values = [fetch(cg * p.per + b) for b in range(p.per)]
        rims = [edges(cg * p.per + b) for b in range(p.per)]
        for d in range(ring):
            total = jnp.zeros((tall, LANES), BF16)
            for b in range(p.per):
                shift = lax.rem(2 * LANES + p.block * b + EDGE - p.window * takes[d], LANES)
                moved = pltpu.roll(jnp.where(fixes[d], rims[b], values[b]), shift, 1)
                total = jnp.where(lane // p.block == b, moved, total)
            stage[d] = total.astype(F32)
            for xp in range(p.cells_x):
                outs[chunk * ring + d][cg - first, xp] = stage[
                    d, pl.ds(xp, p.rows, stride=p.cells_x), :
                ].astype(BF16)

    own = labels[pl.ds(pl.multiple_of(core * tall, 8), tall), :].astype(F32).astype(BF16)
    for chunk, (first, last) in enumerate(cuts):
        tail = last == p.groups

        def step(cg, carry, chunk=chunk, first=first):
            group(cg, lambda c: field[c], chunk, first)
            return carry

        lax.fori_loop(first, last - 1 if tail else last, step, 0)
        if tail:
            group(last - 1, lambda c: field[c] if c < p.chans else own, chunk, first)


def cell_of(p, d, xp):
    return (xp - p.cells_x * d) % p.xs


def smooth_group(p, table, cg, pieces, g, store):
    weights = [table[cg, pl.ds(t, 1), :] for t in range(ROW_WALL)]
    for part in range(p.rows // 16):
        cells = {}
        for d in range(p.ring):
            for xp in range(p.cells_x):
                cells[cell_of(p, d, xp)] = pieces[d][g, xp, pl.ds(16 * part, 16), :].astype(F32)
        for x in range(p.xs):
            total = None
            for j in range(TAPS):
                line = None
                for i in range(TAPS):
                    term = weights[TAPS * i + j] * cells[(x + i - REACH) % p.xs]
                    line = term if line is None else line + term
                if j != REACH:
                    line = pltpu.roll(line, (REACH - j) % LANES, 1)
                total = line if total is None else total + line
            store(x, 16 * part, total.astype(BF16))


def activate(value):
    sig = 0.5 * jnp.tanh(0.5 * value) + 0.5
    act = value * sig
    return act, sig + act * (1.0 - sig)


def forward_body(p, first, count, last, table, bands, *refs):
    refs = list(refs)

    def take(number):
        taken = refs[:number]
        del refs[:number]
        return taken

    pieces = take(p.ring)
    before = take(1 if first else 0)
    rims = take(len(refs) - 6 if last else 0)
    smooth, hidden, slope, score, rim, column = refs
    core = lax.axis_index("col")
    blocks = p.reach_rows // 8
    score[...] = before[0][...] if first else jnp.zeros_like(score)
    for x in range(p.xs):
        column[x, pl.ds(0, WALL_HALO), :] = jnp.zeros((WALL_HALO, LANES), F32)
        column[x, pl.ds(WALL_HALO + p.rows, WALL_HALO), :] = jnp.zeros((WALL_HALO, LANES), F32)
    base = 0
    for other in rims:
        rim[pl.ds(base, other.shape[0])] = other[...]
        base += other.shape[0]

    def step(g, carry):
        cg = first + g

        def store(x, row, value):
            smooth[g, x, pl.ds(row, 16), :] = value
            column[x, pl.ds(WALL_HALO + row, 16), :] = value.astype(F32)

        smooth_group(p, table, cg, pieces, g, store)
        for pair in range(p.xs // 2):
            cells = (2 * pair, 2 * pair + 1)
            tops = [column[x, pl.ds(WALL_HALO, 8), :] for x in cells]
            lows = [column[x, pl.ds(p.rows, 8), :] for x in cells]
            rim[base + g, pair] = jnp.where(
                core == 0, jnp.concatenate(lows, axis=0), jnp.concatenate(tops, axis=0)
            ).astype(BF16)
        taps = [table[cg, pl.ds(ROW_WALL + k, 1), :] for k in range(WALL)]
        classes = [table[cg, pl.ds(ROW_CLASS + k, 1), :] for k in range(p.classes)]
        for blk in range(blocks):
            rows = pl.ds(8 * blk, 8)
            sums = [None] * p.xs
            for k in range(WALL):
                tap = taps[k] * bands[k, rows, :]
                for x in range(p.xs):
                    term = tap * column[x, pl.ds(8 * blk + k, 8), :]
                    sums[x] = term if k == 0 else sums[x] + term
            for x in range(p.xs):
                hidden[g, x, rows, :], slope[g, x, rows, :] = act, _ = activate(sums[x])
                for k in range(p.classes):
                    score[k, x, rows, :] += classes[k] * act
        return carry

    lax.fori_loop(0, count, step, 0)


def fill_column(p, core, smooth, rim, g, cg, x, store):
    store(WALL_HALO, p.rows, smooth[g, x].astype(F32))
    near = rim[cg, x // 2].astype(F32)[8 * (x % 2) : 8 * (x % 2) + 8]
    store(0, WALL_HALO, jnp.where(core == 0, 0.0, near))
    store(WALL_HALO + p.rows, WALL_HALO, jnp.where(core == 0, near, 0.0))


def own_lanes(p, rows):
    lane = lane_of(rows)
    place = lane % p.block
    return (place >= EDGE) & (place < EDGE + p.window) & (lane < p.per * p.block)


def spread(p, value, lane):
    total = value
    for b in range(p.per - 1):
        moved = pltpu.roll(value, LANES - p.block * (p.per - 1 - b), 1)
        total = jnp.where(lane // p.block == b, moved, total)
    return total


def near_block(p, core):
    return pl.multiple_of(jnp.where(core == 0, p.reach_rows - 8, 0), 8)


def edge_rows(p, core, cuts, table, bands, smooths, rim, score, hidden_near, slope_near):
    base = near_block(p, core)
    rows = pl.ds(base, 8)
    for k in range(p.classes):
        for x in range(p.xs):
            score[k, x, rows, :] = jnp.zeros((8, LANES), F32)

    for chunk, (first, last) in enumerate(cuts):

        def step(g, carry, chunk=chunk, first=first):
            cg = first + g
            taps = [
                table[cg, pl.ds(ROW_WALL + k, 1), :] * bands[k, rows, :] for k in range(WALL)
            ]
            classes = [table[cg, pl.ds(ROW_CLASS + k, 1), :] for k in range(p.classes)]
            for x in range(p.xs):
                near = rim[cg, x // 2].astype(F32)[8 * (x % 2) : 8 * (x % 2) + 8]
                low = smooths[chunk][g, x, pl.ds(p.rows - 16, 16), :].astype(F32)[8:]
                top = smooths[chunk][g, x, pl.ds(0, 16), :].astype(F32)[:8]
                hidden_near[cg, x] = jnp.where(core == 0, low, near)
                slope_near[cg, x] = jnp.where(core == 0, near, top)
            sums = []
            for x in range(p.xs):
                both = jnp.concatenate([hidden_near[cg, x], slope_near[cg, x]], axis=0)
                total = taps[0] * both[:8]
                for k in range(1, WALL):
                    total = total + taps[k] * both[k : k + 8]
                sums.append(total)
            for x in range(p.xs):
                act, bend = activate(sums[x])
                hidden_near[cg, x], slope_near[cg, x] = act, bend
                for k in range(p.classes):
                    score[k, x, rows, :] += classes[k] * act
            return carry

        lax.fori_loop(0, last - first, step, 0)


def judge(p, core, smooth, rim, score, errors, column):
    lane = lane_of(8)
    half = WALL // 2
    for x in range(p.xs):

        def store(start, length, value, x=x):
            column[x, pl.ds(start, length), :] = value

        fill_column(p, core, smooth, rim, smooth.shape[0] - 1, p.groups - 1, x, store)

    def step(blk, carry):
        rows = pl.ds(pl.multiple_of(8 * blk, 8), 8)
        place = core * p.rows - half + 8 * blk + lax.broadcasted_iota(jnp.int32, (8, LANES), 0)
        inside = (place >= 0) & (place < 2 * p.rows)
        for x in range(p.xs):
            label = spread(p, column[x, pl.ds(8 * blk + half, 8), :], lane)
            for k in range(p.classes):
                value = score[k, x, rows, :]
                total = value
                for b in range(1, p.per):
                    total = total + pltpu.roll(value, p.block * b, 1)
                error = spread(p, total, lane) - jnp.where(label == k, 1.0, 0.0)
                score[k, x, rows, :] = jnp.where(inside, error, 0.0)
        return carry

    lax.fori_loop(0, p.reach_rows // 8, step, 0)
    own = own_lanes(p, p.rows)
    for k in range(p.classes):
        for x in range(p.xs):
            errors[k, x] = jnp.where(own, score[k, x, pl.ds(half, p.rows), :], 0.0)


def with_near(p, core, blk, value, near):
    if blk == 0:
        return jnp.where(core == 0, value, near)
    if blk == p.reach_rows // 8 - 1:
        return jnp.where(core == 0, near, value)
    return value


def backward_groups(
    p, first, count, table, bands, score, slope, slope_near, grad_smooth, grad_wall, wall, field
):
    core = lax.axis_index("col")
    half = WALL // 2
    own = own_lanes(p, p.rows)

    def step(g, carry):
        cg = first + g
        taps = [table[cg, pl.ds(ROW_WALL + k, 1), :] for k in range(WALL)]
        classes = [table[cg, pl.ds(ROW_CLASS + k, 1), :] for k in range(p.classes)]
        for blk in range(p.reach_rows // 8):
            rows = pl.ds(8 * blk, 8)
            for x in range(p.xs):
                grad = classes[0] * score[0, x, rows, :]
                for k in range(1, p.classes):
                    grad = grad + classes[k] * score[k, x, rows, :]
                bend = with_near(p, core, blk, slope[g, x, rows, :], slope_near[cg, x])
                wall[x, rows, :] = (grad * bend).astype(BF16).astype(F32)
        for x in range(p.xs):
            grad_wall[g, x] = jnp.where(own, wall[x, pl.ds(half, p.rows), :], 0.0).astype(BF16)
        for part in range(p.rows // 16):
            sums = [None] * p.xs
            for k in range(WALL):
                rows = pl.ds(16 * part + WALL - 1 - k, 16)
                tap = taps[k] * bands[k, rows, :]
                for x in range(p.xs):
                    term = tap * wall[x, rows, :]
                    sums[x] = term if k == 0 else sums[x] + term
            for x in range(p.xs):
                grad_smooth[g, x, pl.ds(16 * part, 16), :] = sums[x].astype(BF16)
        weights = [table[cg, pl.ds(t, 1), :] for t in range(ROW_WALL)]
        for part in range(p.rows // 16):
            rows = pl.ds(16 * part, 16)
            cells = [grad_smooth[g, x, rows, :].astype(F32) for x in range(p.xs)]
            for x in range(p.xs):
                total = None
                for j in range(TAPS):
                    line = None
                    for i in range(TAPS):
                        term = weights[TAPS * i + j] * cells[(x - i + REACH) % p.xs]
                        line = term if line is None else line + term
                    if j != REACH:
                        line = pltpu.roll(line, (j - REACH) % LANES, 1)
                    total = line if total is None else total + line
                field[g, x, rows, :] = total.astype(BF16)
        return carry

    lax.fori_loop(0, count, step, 0)


def ship(p, packs, field, results):
    me = lax.axis_index("gx")
    wide = lane_of(p.rows) // p.window

    def step(pack, carry):
        totals = [jnp.zeros((p.rows, LANES), BF16)] * p.xs
        for b in range(p.ring):
            c = pack * p.ring + b
            spot = lax.rem(b + me, p.ring)
            shift = lax.rem(2 * LANES + p.window * spot - p.block * (c % p.per) - EDGE, LANES)
            for x in range(p.xs):
                moved = pltpu.roll(field[c // p.per, x], shift, 1)
                totals[x] = jnp.where(wide == spot, moved, totals[x])
        for d in range(p.ring):
            for xp in range(p.cells_x):
                results[d][pack, xp] = totals[cell_of(p, d, xp)]
        return carry

    lax.fori_loop(0, packs, step, 0)


def backward_body(p, cuts, table, bands, score_in, rim, *refs):
    count = len(cuts)
    smooths, slopes, refs = refs[:count], refs[count : 2 * count], refs[2 * count :]
    results, refs = refs[: p.ring], refs[p.ring :]
    errors, hidden_near, grad_smooth, grad_wall = refs[:4]
    score, slope_near, wall, field, column = refs[4:]
    core = lax.axis_index("col")
    score[...] = score_in[...]
    edge_rows(p, core, cuts, table, bands, smooths, rim, score, hidden_near, slope_near)
    judge(p, core, smooths[-1], rim, score, errors, column)
    for (first, last), slope in zip(cuts, slopes):
        own = pl.ds(first, last - first)
        backward_groups(
            p, first, last - first, table, bands, score, slope, slope_near,
            grad_smooth.at[own], grad_wall.at[own], wall, field.at[own],
        )
    ship(p, p.packs, field, results)


def weight_body(
    p, cuts, bands, errors, hidden_near, rim, grad_smooth, grad_wall, *refs
):
    count = len(cuts)
    refs = list(refs)

    def take(number):
        taken = refs[:number]
        del refs[:number]
        return taken

    hiddens, smooths = take(count), take(count)
    pieces = [take(p.ring) for i in range(count)]
    out, wall, column, lines = refs
    core = lax.axis_index("col")
    half = WALL // 2
    own = own_lanes(p, 16)
    lines[...] = jnp.zeros_like(lines)

    def fold(value):
        total = value[:8]
        for r in range(8, value.shape[0], 8):
            total = total + value[r : r + 8]
        return jnp.sum(total, axis=0, keepdims=True)

    for chunk, (first, last) in enumerate(cuts):

        def step(g, carry, chunk=chunk, first=first):
            cg = first + g
            sums = [None] * ROW_WALL
            for part in range(p.rows // 16):
                rows = pl.ds(16 * part, 16)
                cells = {}
                for d in range(p.ring):
                    for xp in range(p.cells_x):
                        cells[cell_of(p, d, xp)] = pieces[chunk][d][g, xp, rows, :].astype(F32)
                for x in range(p.xs):
                    grad = jnp.where(own, grad_smooth[cg, x, rows, :].astype(F32), 0.0)
                    for j in range(TAPS):
                        moved = grad if j == REACH else pltpu.roll(grad, (j - REACH) % LANES, 1)
                        for i in range(TAPS):
                            t = TAPS * i + j
                            term = cells[(x + i - REACH) % p.xs] * moved
                            term = term[:8] + term[8:]
                            sums[t] = term if sums[t] is None else sums[t] + term
            for t in range(ROW_WALL):
                lines[cg, pl.ds(t, 1), :] = fold(sums[t])
            for x in range(p.xs):

                def store(start, length, value, x=x):
                    column[x, pl.ds(start, length), :] = value

                fill_column(p, core, smooths[chunk], rim, g, cg, x, store)
            grads = [grad_wall[cg, x].astype(F32) for x in range(p.xs)]
            for k in range(WALL):
                total = None
                for x in range(p.xs):
                    term = grads[x] * column[x, pl.ds(half + k, p.rows), :]
                    total = term if total is None else total + term
                lines[cg, pl.ds(ROW_WALL + k, 1), :] = fold(
                    total * bands[k, pl.ds(half, p.rows), :]
                )
            for x in range(p.xs):
                for blk in range(p.reach_rows // 8):
                    rows = pl.ds(8 * blk, 8)
                    wall[x, rows, :] = with_near(
                        p, core, blk, hiddens[chunk][g, x, rows, :], hidden_near[cg, x]
                    )
            for k in range(p.classes):
                total = None
                for x in range(p.xs):
                    term = errors[k, x] * wall[x, pl.ds(half, p.rows), :]
                    total = term if total is None else total + term
                lines[cg, pl.ds(ROW_CLASS + k, 1), :] = fold(total)
            return carry

        lax.fori_loop(0, last - first, step, 0)

    lane = lane_of(LANES)
    channel = lax.broadcasted_iota(jnp.int32, (LANES, LANES), 0)
    total = jnp.zeros((p.table_rows, LANES), F32)
    for cg in range(p.groups):
        pick = (lane // p.block + cg * p.per == channel) & (lane < p.per * p.block)
        total = total + lax.dot_general(
            lines[cg],
            jnp.where(pick, 1.0, 0.0),
            (((1,), (1,)), ((), ())),
            precision=lax.Precision.HIGHEST,
            preferred_element_type=F32,
        )
    out[...] = total


def pass_body(value, *refs):
    refs[-1][...] = value[...]


def unpack_body(p, *refs):
    out, stage = refs[-2:]
    me = lax.axis_index("gx")
    spot = lane_of(p.rows) // p.window

    def step(pack, carry, pieces, base):
        for xp in range(p.cells_x):
            values = [pieces[d][pack, xp] for d in range(p.ring)]
            for b in range(p.ring):
                total = values[0]
                for d in range(1, p.ring):
                    total = jnp.where(spot == lax.rem(b + me + d, p.ring), values[d], total)
                total = pltpu.roll(total, (LANES - p.window * b) % LANES, 1) if b else total
                stage[b, pl.ds(xp, p.rows, stride=p.cells_x), :] = total.astype(F32)
        for b in range(p.ring):
            out[(base + pack) * p.ring + b] = stage[b].astype(BF16)
        return carry

    base = 0
    for i in range(0, len(refs) - 2, p.ring):
        pieces = refs[i : i + p.ring]
        size = pieces[0].shape[0]
        lax.fori_loop(0, size, functools.partial(step, pieces=pieces, base=base), 0)
        base += size


def rotation(size, by):
    return [(i, (i + by) % size) for i in range(size)]


def sum_over(value, axis):
    size = lax.axis_size(axis)
    return sum((lax.ppermute(value, axis, rotation(size, d)) for d in range(1, size)), value)


def near_parts(value):
    col, gz = lax.axis_size("col"), lax.axis_size("gz")
    parts = [value]
    for d in range(1, col * gz):
        pairs = [
            (i * col + j, (i + d // col) % gz * col + (j + d) % col)
            for i in range(gz)
            for j in range(col)
        ]
        parts.append(lax.ppermute(value, ("gz", "col"), pairs))
    return parts


def table_body(p, tile, wall, classes, levels, stretch, *refs):
    table, near = refs[-2:]
    core = lax.axis_index("col")
    lane = lax.broadcasted_iota(jnp.int32, (p.chans, LANES), 1)
    channel = lax.broadcasted_iota(jnp.int32, (p.chans, LANES), 0)

    def spread_rows(value, pick, dim):
        return lax.dot_general(
            value, pick, (((dim,), (0,)), ((), ())),
            precision=lax.Precision.HIGHEST, preferred_element_type=F32,
        )

    for cg in range(p.groups):
        pick = (lane // p.block + cg * p.per == channel) & (lane < p.per * p.block)
        pick = jnp.where(pick, 1.0, 0.0)
        table[cg, pl.ds(0, ROW_WALL), :] = spread_rows(tile[...], pick, 0)
        table[cg, pl.ds(ROW_WALL, WALL), :] = spread_rows(wall[...], pick, 1)
        table[cg, pl.ds(ROW_CLASS, p.classes), :] = spread_rows(classes[...], pick, 1)
    marks = lane_of(1)
    marks = (marks // p.block == p.per - 1) & (marks < p.per * p.block)
    last = table[p.groups - 1, pl.ds(CENTRE, 1), :]
    table[p.groups - 1, pl.ds(CENTRE, 1), :] = jnp.where(marks, 1.0, last)

    def step(q, carry):
        y = jnp.clip(core * p.rows - WALL // 2 + q, 0, 2 * p.rows - 1)
        level = levels[y]
        for k in range(WALL):
            near[k, pl.ds(q, 1), :] = jnp.full((1, LANES), stretch[level, k], F32)
        return carry

    lax.fori_loop(0, p.reach_rows, step, 0)


def sums_body(p, volume, *refs):
    tile, wall, classes = refs[-3:]
    total = refs[0][...]
    for ref in refs[1:-3]:
        total = total + ref[...]
    total = total * (1.0 / volume)
    rows = jnp.zeros((LANES - p.table_rows, LANES), F32)
    turned = jnp.concatenate([total, rows], axis=0).T
    tile[...] = turned[: p.chans, :ROW_WALL]
    wall[...] = total[ROW_WALL:ROW_CLASS, : p.chans]
    classes[...] = total[ROW_CLASS : ROW_CLASS + p.classes, : p.chans]


def band_rows(grid_index, stretch):
    levels = stretch.shape[0]
    onehot = (grid_index[:, None] == jnp.arange(levels, dtype=jnp.int32)[None, :]).astype(F32)
    return jnp.dot(onehot, stretch, precision=lax.Precision.HIGHEST)


def by_windows(features, labels, grid_index, stretch, tile_filter, wall_filter, class_weight):
    chans, rows, cells_x, cells_z = features.shape
    classes = class_weight.shape[0]
    ring, gz = lax.axis_size("gx"), lax.axis_size("gz")
    p = Plan(ring, chans, rows, cells_x, cells_z, classes)
    volume = labels.shape[0] * cells_x * ring * cells_z * gz
    tall = rows * cells_x
    cuts = p.cuts()

    field = features.reshape(chans, tall, cells_z)
    marks = labels.reshape(labels.shape[0] * cells_x, cells_z)
    (edge,) = call(
        functools.partial(edge_body, p),
        [jax.ShapeDtypeStruct((p.edge_groups, tall, LANES), BF16)],
        (field, marks),
    )
    left = lax.ppermute(edge, "gz", rotation(gz, 1))
    right = left if gz == 2 else lax.ppermute(edge, "gz", rotation(gz, -1))

    windows = call(
        functools.partial(pack_body, p, cuts),
        [
            jax.ShapeDtypeStruct((last - first, cells_x, rows, LANES), BF16)
            for first, last in cuts
            for d in range(ring)
        ],
        (field, marks, left, right),
        [pltpu.VMEM((ring, tall, LANES), F32)],
    )

    def shape(*sizes, kind=BF16):
        return jax.ShapeDtypeStruct(sizes, kind)

    smem = pl.BlockSpec(memory_space=pltpu.SMEM)
    table, near = call(
        functools.partial(table_body, p),
        [
            shape(p.groups, p.table_rows, LANES, kind=F32),
            shape(WALL, p.reach_rows, LANES, kind=F32),
        ],
        (tile_filter, wall_filter.T, class_weight, grid_index, stretch, windows[0]),
        micros=0.1,
        unread=1,
        scalars={3: smem, 4: smem},
    )
    column = pltpu.VMEM((p.xs, rows + 2 * WALL_HALO, LANES), F32)
    wall = pltpu.VMEM((p.xs, p.reach_rows, LANES), F32)
    smooths, rims, pieces, hiddens, slopes, score = [], [], [], [], [], ()
    for chunk, (first, last) in enumerate(cuts):
        size = last - first
        sent = windows[chunk * ring : (chunk + 1) * ring]
        got = [sent[0]] + [
            lax.ppermute(sent[d], "gx", rotation(ring, d)) for d in range(1, ring)
        ]
        final = last == p.groups
        smooth, hidden, slope, *score = call(
            functools.partial(forward_body, p, first, size, final),
            [
                shape(size, p.xs, rows, LANES),
                shape(size, p.xs, p.reach_rows, LANES, kind=F32),
                shape(size, p.xs, p.reach_rows, LANES, kind=F32),
                shape(classes, p.xs, p.reach_rows, LANES, kind=F32),
                shape(p.groups if final else size, p.xs // 2, 16, LANES),
            ],
            (table, near, *got, *score[:1], *(rims if final else [])),
            [column],
            micros=0.001,
        )
        rims.append(score[1])
        smooths, pieces = smooths + [smooth], pieces + got
        hiddens, slopes = hiddens + [hidden], slopes + [slope]
    score = score[0]
    rim = lax.ppermute(rims[-1], "col", rotation(2, 1))

    near_shape = (p.groups, p.xs, 8, LANES)
    *sent, errors, hidden_near, grad_smooth, grad_wall = call(
        functools.partial(backward_body, p, cuts),
        [shape(p.packs, cells_x, rows, LANES)] * ring
        + [
            shape(classes, p.xs, rows, LANES, kind=F32),
            shape(*near_shape, kind=F32),
            shape(p.groups, p.xs, rows, LANES),
            shape(p.groups, p.xs, rows, LANES),
        ],
        (table, near, score, rim, *smooths, *slopes),
        [
            pltpu.VMEM((classes, p.xs, p.reach_rows, LANES), F32),
            pltpu.VMEM(near_shape, F32),
            wall,
            pltpu.VMEM((p.groups, p.xs, rows, LANES), BF16),
            column,
        ],
        micros=5,
    )
    back = [sent[0]] + [
        lax.ppermute(sent[d], "gx", rotation(ring, -d)) for d in range(1, ring)
    ]
    (sums,) = call(
        functools.partial(weight_body, p, cuts),
        [shape(p.table_rows, LANES, kind=F32)],
        (
            *(near, errors, hidden_near, rim, grad_smooth, grad_wall),
            *hiddens, *smooths, *pieces,
        ),
        [wall, column, pltpu.VMEM((p.groups, p.table_rows, LANES), F32)],
        micros=0.01,
    )
    (sums,) = call(
        pass_body,
        [shape(p.table_rows, LANES, kind=F32)],
        (sums, *back[1:]),
        micros=0.1,
        unread=ring - 1,
    )
    sums = sum_over(sums, "gx")
    (grad_field,) = call(
        functools.partial(unpack_body, p),
        [shape(chans, tall, cells_z)],
        back,
        [pltpu.VMEM((ring, tall, LANES), F32)],
    )
    grad_tile, grad_wall, grad_class = call(
        functools.partial(sums_body, p, volume),
        [
            shape(chans, ROW_WALL, kind=F32),
            shape(WALL, chans, kind=F32),
            shape(classes, chans, kind=F32),
        ],
        near_parts(sums),
        micros=0.1,
    )
    return grad_field.reshape(features.shape), grad_tile, grad_wall.T, grad_class


def with_halo(value, sides, width):
    for axis, dim in sides:
        size, length = (lax.axis_size(axis), value.shape[dim])
        up = [(i, (i + 1) % size) for i in range(size)]
        down = [(j, i) for i, j in up]
        last = lax.slice_in_dim(value, length - width, length, axis=dim)
        leading = lax.slice_in_dim(value, 0, width, axis=dim)
        before = lax.ppermute(last, axis, up)
        after = lax.ppermute(leading, axis, down)
        value = jnp.concatenate([before, value, after], axis=dim)
    return value


def rim_tiles(field):
    return with_halo(field, (("gx", 2), ("gz", 3)), 2)


def wall_forward(smooth_ext, wall_rows, band_rows):
    rows = band_rows.shape[0]
    total = jnp.zeros((smooth_ext.shape[0], rows) + smooth_ext.shape[2:], jnp.float32)
    for k in range(9):
        tap = wall_rows[:, k][:, None] * band_rows[:, k][None, :]
        total = total + tap[:, :, None, None] * smooth_ext[:, k : k + rows].astype(jnp.float32)
    return total


def wall_backward(grad_ext, wall_rows, band_ext, rows):
    total = jnp.zeros((grad_ext.shape[0], rows) + grad_ext.shape[2:], jnp.float32)
    for k in range(9):
        first = 8 - k
        tap = wall_rows[:, k][:, None] * band_ext[first : first + rows, k][None, :]
        total = total + tap[:, :, None, None] * grad_ext[:, first : first + rows].astype(
            jnp.float32
        )
    return total


def by_halos(features, labels, grid_index, stretch, tile_filter, wall_filter, class_weight):
    chans, half_rows, cells_x, cells_z = features.shape
    all_rows = labels.shape[0]
    classes = class_weight.shape[0]
    volume = all_rows * cells_x * lax.axis_size("gx") * cells_z * lax.axis_size("gz")
    widened = rim_tiles(features)
    smooth = jnp.zeros(features.shape, jnp.float32)
    for i in range(5):
        for j in range(5):
            weight = tile_filter[:, 5 * i + j][:, None, None, None]
            smooth = smooth + weight * widened[:, :, i : i + cells_x, j : j + cells_z].astype(
                jnp.float32
            )
    smoothed = smooth.astype(jnp.bfloat16)
    bands = band_rows(grid_index, stretch)
    bands_pad = jnp.pad(bands, ((4, 4), (0, 0)))
    place = lax.axis_index("col")
    share = chans // lax.axis_size("col")
    first_chan = place * share
    pencil = lax.all_to_all(smoothed, "col", split_axis=0, concat_axis=1, tiled=True)
    smooth_ext = jnp.pad(pencil, ((0, 0), (4, 4), (0, 0), (0, 0)))
    wall_rows = lax.dynamic_slice_in_dim(wall_filter, first_chan, share, 0)
    class_rows = lax.dynamic_slice_in_dim(class_weight, first_chan, share, 1)
    wall_out = wall_forward(smooth_ext, wall_rows, bands)
    sig = jax.nn.sigmoid(wall_out)
    hidden = wall_out * sig
    partial_scores = jnp.einsum(
        "kc,cyxz->kyxz", class_rows, hidden, precision=lax.Precision.HIGHEST
    )
    scores = lax.psum(partial_scores, "col")
    targets = (labels[None] == jnp.arange(classes, dtype=jnp.int32)[:, None, None, None]).astype(
        jnp.float32
    )
    errors = scores - targets
    grad_hidden = jnp.einsum("kc,kyxz->cyxz", class_rows, errors, precision=lax.Precision.HIGHEST)
    grad_wall = (grad_hidden * sig * (1.0 + wall_out * (1.0 - sig))).astype(jnp.bfloat16)
    class_part = jnp.einsum("kyxz,cyxz->kc", errors, hidden, precision=lax.Precision.HIGHEST)
    grad_vals = grad_wall.astype(jnp.float32)
    wall_part = jnp.stack(
        [
            jnp.sum(
                grad_vals
                * bands[:, k][None, :, None, None]
                * smooth_ext[:, k : k + all_rows].astype(jnp.float32),
                axis=(1, 2, 3),
            )
            for k in range(9)
        ],
        axis=1,
    )
    grad_ext = jnp.pad(grad_wall, ((0, 0), (4, 4), (0, 0), (0, 0)))
    grad_smooth = wall_backward(grad_ext, wall_rows, bands_pad, all_rows).astype(jnp.bfloat16)
    grad_tile = lax.all_to_all(grad_smooth, "col", split_axis=1, concat_axis=0, tiled=True)
    wall_full = lax.dynamic_update_slice_in_dim(
        jnp.zeros((chans, 9), jnp.float32), wall_part, first_chan, 0
    )
    class_full = lax.dynamic_update_slice_in_dim(
        jnp.zeros((classes, chans), jnp.float32), class_part, first_chan, 1
    )
    grad_widened = rim_tiles(grad_tile)
    grad_tile_vals = grad_tile.astype(jnp.float32)
    grad_field = jnp.zeros(features.shape, jnp.float32)
    tile_terms = []
    for i in range(5):
        for j in range(5):
            weight = tile_filter[:, 5 * i + j][:, None, None, None]
            grad_field = grad_field + weight * grad_widened[
                :, :, 4 - i : 4 - i + cells_x, 4 - j : 4 - j + cells_z
            ].astype(jnp.float32)
            shifted = widened[:, :, i : i + cells_x, j : j + cells_z].astype(jnp.float32)
            tile_terms.append(jnp.sum(shifted * grad_tile_vals, axis=(1, 2, 3)))
    tile_part = jnp.stack(tile_terms, axis=1)
    totals = lax.psum((tile_part, wall_full, class_full), ("gx", "gz", "col"))
    return (
        grad_field.astype(jnp.bfloat16),
        totals[0] / volume,
        totals[1] / volume,
        totals[2] / volume,
    )


def shards(features, labels, grid_index, stretch, tile_filter, wall_filter, class_weight):
    sizes = [lax.axis_size(axis) for axis in ("gx", "gz", "col")]
    plan = by_windows if fits(*sizes, *features.shape, class_weight.shape[0]) else by_halos
    return plan(features, labels, grid_index, stretch, tile_filter, wall_filter, class_weight)


def solution(mesh):
    return jax.shard_map(
        shards,
        mesh=mesh,
        in_specs=(
            P(None, "col", ("group", "gx"), "gz"),
            P(None, ("group", "gx"), "gz"),
            P(),
            P(),
            P(),
            P(),
            P(),
        ),
        out_specs=(
            P(None, "col", ("group", "gx"), "gz"),
            P("group", None),
            P("group", None),
            P("group", None),
        ),
        check_vma=False,
    )
```

```python
import functools

import jax
import jax.numpy as jnp
from jax import lax
from jax.experimental import pallas as pl
from jax.experimental.pallas import tpu as pltpu
from jax.sharding import PartitionSpec as P

LANES = 128
TAPS = 5
REACH = 2
EDGE = 4
WALL = 9
WALL_HALO = 8
ROW_WALL = TAPS * TAPS
ROW_CLASS = ROW_WALL + WALL
CENTRE = ROW_WALL // 2
F32, BF16 = jnp.float32, jnp.bfloat16


class Plan:
    def __init__(self, ring, chans, rows, cells_x, cells_z, classes):
        self.ring, self.chans, self.rows, self.cells_x = ring, chans, rows, cells_x
        self.classes = classes
        self.window = cells_z // ring
        self.block = self.window + 2 * EDGE
        self.per = LANES // self.block
        self.slots = chans + 1
        self.groups = self.slots // self.per
        self.xs = ring * cells_x
        self.packs = chans // ring
        self.reach_rows = rows + 2 * (WALL_HALO // 2)
        self.edge_slots = LANES // (2 * EDGE)
        self.edge_groups = -(-self.slots // self.edge_slots)
        self.table_rows = -(-(ROW_CLASS + classes) // 8) * 8


    def cuts(self):
        tail = -(-self.groups // 4)
        return ((0, self.groups - tail), (self.groups - tail, self.groups))


def fits(ring, gz, col, chans, rows, cells_x, cells_z, classes):
    if cells_z != LANES or cells_x != 2 or col != 2 or ring < 2 or ring > 4 or LANES % ring:
        return False
    block = LANES // ring + 2 * EDGE
    per = LANES // block
    return (chans + 1) % per == 0 and chans % ring == 0 and rows % 16 == 0 and ring * cells_x >= TAPS


def vmem(count):
    return [pl.BlockSpec(memory_space=pltpu.VMEM)] * count


def call(body, outs, args, scratch=(), micros=1.0, unread=0, scalars={}):
    return pl.pallas_call(
        body,
        out_shape=outs,
        in_specs=[
            *(scalars.get(i, spec) for i, spec in enumerate(vmem(len(args) - unread))),
            *[pl.BlockSpec(memory_space=pl.ANY)] * unread,
        ],
        cost_estimate=pl.CostEstimate(
            flops=0, bytes_accessed=int(3.0e6 * micros), transcendentals=0
        ),
        out_specs=vmem(len(outs)),
        scratch_shapes=list(scratch),
        compiler_params=pltpu.CompilerParams(vmem_limit_bytes=40 * 2**20),
    )(*args)


def lane_of(rows):
    return lax.broadcasted_iota(jnp.int32, (rows, LANES), 1)


def edge_body(p, field, labels, out):
    core = lax.axis_index("col")
    tall = p.rows * p.cells_x
    lane = lane_of(tall)

    def group(g, count, fetch):
        total = jnp.zeros((tall, LANES), F32)
        for e in range(count):
            moved = pltpu.roll(fetch(g * p.edge_slots + e), (2 * EDGE * e + EDGE) % LANES, 1)
            total = jnp.where(lane // (2 * EDGE) == e, moved, total)
        out[g] = total.astype(BF16)

    def step(g, carry):
        group(g, p.edge_slots, lambda c: field[c].astype(F32))
        return carry

    full = p.chans // p.edge_slots
    lax.fori_loop(0, full, step, 0)
    own = labels[pl.ds(pl.multiple_of(core * tall, 8), tall), :].astype(F32)
    group(full, p.slots - full * p.edge_slots, lambda c: own)


def pack_body(p, cuts, field, labels, left, right, *refs):
    outs, stage = refs[:-1], refs[-1]
    ring = p.ring
    me, core = lax.axis_index("gx"), lax.axis_index("col")
    tall = p.rows * p.cells_x
    lane = lane_of(tall)
    takes = [lax.rem(me + d, ring) for d in range(ring)]
    fixes = [
        ((lane >= LANES - EDGE) & (k == 0)) | ((lane < EDGE) & (k == ring - 1)) for k in takes
    ]
    older = lane % (2 * EDGE) < EDGE

    def edges(c):
        g, e = c // p.edge_slots, c % p.edge_slots
        both = jnp.where(older, left[g].astype(F32), right[g].astype(F32))
        return pltpu.roll(both, LANES - EDGE - 2 * EDGE * e, 1)

    def group(cg, fetch, chunk, first):
        values = [fetch(cg * p.per + b) for b in range(p.per)]
        rims = [edges(cg * p.per + b) for b in range(p.per)]
        for d in range(ring):
            total = jnp.zeros((tall, LANES), F32)
            for b in range(p.per):
                shift = lax.rem(2 * LANES + p.block * b + EDGE - p.window * takes[d], LANES)
                moved = pltpu.roll(jnp.where(fixes[d], rims[b], values[b]), shift, 1)
                total = jnp.where(lane // p.block == b, moved, total)
            stage[d] = total
            for xp in range(p.cells_x):
                outs[chunk * ring + d][cg - first, xp] = stage[
                    d, pl.ds(xp, p.rows, stride=p.cells_x), :
                ].astype(BF16)

    own = labels[pl.ds(pl.multiple_of(core * tall, 8), tall), :].astype(F32)
    for chunk, (first, last) in enumerate(cuts):
        tail = last == p.groups

        def step(cg, carry, chunk=chunk, first=first):
            group(cg, lambda c: field[c].astype(F32), chunk, first)
            return carry

        lax.fori_loop(first, last - 1 if tail else last, step, 0)
        if tail:
            group(last - 1, lambda c: field[c].astype(F32) if c < p.chans else own, chunk, first)


def cell_of(p, d, xp):
    return (xp - p.cells_x * d) % p.xs


def smooth_group(p, table, cg, pieces, g, store):
    weights = [table[cg, pl.ds(t, 1), :] for t in range(ROW_WALL)]
    for part in range(p.rows // 16):
        cells = {}
        for d in range(p.ring):
            for xp in range(p.cells_x):
                cells[cell_of(p, d, xp)] = pieces[d][g, xp, pl.ds(16 * part, 16), :].astype(F32)
        for x in range(p.xs):
            total = None
            for j in range(TAPS):
                line = None
                for i in range(TAPS):
                    term = weights[TAPS * i + j] * cells[(x + i - REACH) % p.xs]
                    line = term if line is None else line + term
                if j != REACH:
                    line = pltpu.roll(line, (REACH - j) % LANES, 1)
                total = line if total is None else total + line
            store(x, 16 * part, total.astype(BF16))


def activate(value):
    sig = 0.5 * jnp.tanh(0.5 * value) + 0.5
    act = value * sig
    return act, sig + act * (1.0 - sig)


def forward_body(p, first, count, last, table, bands, *refs):
    refs = list(refs)

    def take(number):
        taken = refs[:number]
        del refs[:number]
        return taken

    pieces = take(p.ring)
    before = take(1 if first else 0)
    rims = take(len(refs) - 6 if last else 0)
    smooth, hidden, slope, score, rim, column = refs
    core = lax.axis_index("col")
    blocks = p.reach_rows // 8
    score[...] = before[0][...] if first else jnp.zeros_like(score)
    for x in range(p.xs):
        column[x, pl.ds(0, WALL_HALO), :] = jnp.zeros((WALL_HALO, LANES), F32)
        column[x, pl.ds(WALL_HALO + p.rows, WALL_HALO), :] = jnp.zeros((WALL_HALO, LANES), F32)
    base = 0
    for other in rims:
        rim[pl.ds(base, other.shape[0])] = other[...]
        base += other.shape[0]

    def step(g, carry):
        cg = first + g

        def store(x, row, value):
            smooth[g, x, pl.ds(row, 16), :] = value
            column[x, pl.ds(WALL_HALO + row, 16), :] = value.astype(F32)

        smooth_group(p, table, cg, pieces, g, store)
        for pair in range(p.xs // 2):
            cells = (2 * pair, 2 * pair + 1)
            tops = [column[x, pl.ds(WALL_HALO, 8), :] for x in cells]
            lows = [column[x, pl.ds(p.rows, 8), :] for x in cells]
            rim[base + g, pair] = jnp.where(
                core == 0, jnp.concatenate(lows, axis=0), jnp.concatenate(tops, axis=0)
            ).astype(BF16)
        taps = [table[cg, pl.ds(ROW_WALL + k, 1), :] for k in range(WALL)]
        classes = [table[cg, pl.ds(ROW_CLASS + k, 1), :] for k in range(p.classes)]
        for blk in range(blocks):
            rows = pl.ds(8 * blk, 8)
            sums = [None] * p.xs
            for k in range(WALL):
                tap = taps[k] * bands[k, rows, :]
                for x in range(p.xs):
                    term = tap * column[x, pl.ds(8 * blk + k, 8), :]
                    sums[x] = term if k == 0 else sums[x] + term
            for x in range(p.xs):
                hidden[g, x, rows, :], slope[g, x, rows, :] = act, _ = activate(sums[x])
                for k in range(p.classes):
                    score[k, x, rows, :] += classes[k] * act
        return carry

    lax.fori_loop(0, count, step, 0)


def fill_column(p, core, smooth, rim, g, cg, x, store):
    store(WALL_HALO, p.rows, smooth[g, x].astype(F32))
    near = rim[cg, x // 2].astype(F32)[8 * (x % 2) : 8 * (x % 2) + 8]
    store(0, WALL_HALO, jnp.where(core == 0, 0.0, near))
    store(WALL_HALO + p.rows, WALL_HALO, jnp.where(core == 0, near, 0.0))


def own_lanes(p, rows):
    lane = lane_of(rows)
    place = lane % p.block
    return (place >= EDGE) & (place < EDGE + p.window) & (lane < p.per * p.block)


def spread(p, value, lane):
    total = value
    for b in range(p.per - 1):
        moved = pltpu.roll(value, LANES - p.block * (p.per - 1 - b), 1)
        total = jnp.where(lane // p.block == b, moved, total)
    return total


def near_block(p, core):
    return pl.multiple_of(jnp.where(core == 0, p.reach_rows - 8, 0), 8)


def edge_rows(p, core, cuts, table, bands, smooths, rim, score, hidden_near, slope_near):
    base = near_block(p, core)
    rows = pl.ds(base, 8)
    for k in range(p.classes):
        for x in range(p.xs):
            score[k, x, rows, :] = jnp.zeros((8, LANES), F32)

    for chunk, (first, last) in enumerate(cuts):

        def step(g, carry, chunk=chunk, first=first):
            cg = first + g
            taps = [
                table[cg, pl.ds(ROW_WALL + k, 1), :] * bands[k, rows, :] for k in range(WALL)
            ]
            classes = [table[cg, pl.ds(ROW_CLASS + k, 1), :] for k in range(p.classes)]
            for x in range(p.xs):
                near = rim[cg, x // 2].astype(F32)[8 * (x % 2) : 8 * (x % 2) + 8]
                low = smooths[chunk][g, x, pl.ds(p.rows - 16, 16), :].astype(F32)[8:]
                top = smooths[chunk][g, x, pl.ds(0, 16), :].astype(F32)[:8]
                hidden_near[cg, x] = jnp.where(core == 0, low, near)
                slope_near[cg, x] = jnp.where(core == 0, near, top)
            sums = []
            for x in range(p.xs):
                both = jnp.concatenate([hidden_near[cg, x], slope_near[cg, x]], axis=0)
                total = taps[0] * both[:8]
                for k in range(1, WALL):
                    total = total + taps[k] * both[k : k + 8]
                sums.append(total)
            for x in range(p.xs):
                act, bend = activate(sums[x])
                hidden_near[cg, x], slope_near[cg, x] = act, bend
                for k in range(p.classes):
                    score[k, x, rows, :] += classes[k] * act
            return carry

        lax.fori_loop(0, last - first, step, 0)


def judge(p, core, smooth, rim, score, errors, column):
    lane = lane_of(8)
    half = WALL // 2
    for x in range(p.xs):

        def store(start, length, value, x=x):
            column[x, pl.ds(start, length), :] = value

        fill_column(p, core, smooth, rim, smooth.shape[0] - 1, p.groups - 1, x, store)

    def step(blk, carry):
        rows = pl.ds(pl.multiple_of(8 * blk, 8), 8)
        place = core * p.rows - half + 8 * blk + lax.broadcasted_iota(jnp.int32, (8, LANES), 0)
        inside = (place >= 0) & (place < 2 * p.rows)
        for x in range(p.xs):
            label = spread(p, column[x, pl.ds(8 * blk + half, 8), :], lane)
            for k in range(p.classes):
                value = score[k, x, rows, :]
                total = value
                for b in range(1, p.per):
                    total = total + pltpu.roll(value, p.block * b, 1)
                error = spread(p, total, lane) - jnp.where(label == k, 1.0, 0.0)
                score[k, x, rows, :] = jnp.where(inside, error, 0.0)
        return carry

    lax.fori_loop(0, p.reach_rows // 8, step, 0)
    own = own_lanes(p, p.rows)
    for k in range(p.classes):
        for x in range(p.xs):
            errors[k, x] = jnp.where(own, score[k, x, pl.ds(half, p.rows), :], 0.0)


def with_near(p, core, blk, value, near):
    if blk == 0:
        return jnp.where(core == 0, value, near)
    if blk == p.reach_rows // 8 - 1:
        return jnp.where(core == 0, near, value)
    return value


def backward_groups(
    p, first, count, table, bands, score, slope, slope_near, grad_smooth, grad_wall, wall, field
):
    core = lax.axis_index("col")
    half = WALL // 2
    own = own_lanes(p, p.rows)

    def step(g, carry):
        cg = first + g
        taps = [table[cg, pl.ds(ROW_WALL + k, 1), :] for k in range(WALL)]
        classes = [table[cg, pl.ds(ROW_CLASS + k, 1), :] for k in range(p.classes)]
        for blk in range(p.reach_rows // 8):
            rows = pl.ds(8 * blk, 8)
            for x in range(p.xs):
                grad = classes[0] * score[0, x, rows, :]
                for k in range(1, p.classes):
                    grad = grad + classes[k] * score[k, x, rows, :]
                bend = with_near(p, core, blk, slope[g, x, rows, :], slope_near[cg, x])
                wall[x, rows, :] = (grad * bend).astype(BF16).astype(F32)
        for x in range(p.xs):
            grad_wall[g, x] = jnp.where(own, wall[x, pl.ds(half, p.rows), :], 0.0).astype(BF16)
        for part in range(p.rows // 16):
            sums = [None] * p.xs
            for k in range(WALL):
                rows = pl.ds(16 * part + WALL - 1 - k, 16)
                tap = taps[k] * bands[k, rows, :]
                for x in range(p.xs):
                    term = tap * wall[x, rows, :]
                    sums[x] = term if k == 0 else sums[x] + term
            for x in range(p.xs):
                grad_smooth[g, x, pl.ds(16 * part, 16), :] = sums[x].astype(BF16)
        weights = [table[cg, pl.ds(t, 1), :] for t in range(ROW_WALL)]
        for part in range(p.rows // 16):
            rows = pl.ds(16 * part, 16)
            cells = [grad_smooth[g, x, rows, :].astype(F32) for x in range(p.xs)]
            for x in range(p.xs):
                total = None
                for j in range(TAPS):
                    line = None
                    for i in range(TAPS):
                        term = weights[TAPS * i + j] * cells[(x - i + REACH) % p.xs]
                        line = term if line is None else line + term
                    if j != REACH:
                        line = pltpu.roll(line, (j - REACH) % LANES, 1)
                    total = line if total is None else total + line
                field[g, x, rows, :] = total
        return carry

    lax.fori_loop(0, count, step, 0)


def ship(p, packs, field, results):
    me = lax.axis_index("gx")
    wide = lane_of(p.rows) // p.window

    def step(pack, carry):
        totals = [jnp.zeros((p.rows, LANES), F32)] * p.xs
        for b in range(p.ring):
            c = pack * p.ring + b
            spot = lax.rem(b + me, p.ring)
            shift = lax.rem(2 * LANES + p.window * spot - p.block * (c % p.per) - EDGE, LANES)
            for x in range(p.xs):
                moved = pltpu.roll(field[c // p.per, x], shift, 1)
                totals[x] = jnp.where(wide == spot, moved, totals[x])
        for d in range(p.ring):
            for xp in range(p.cells_x):
                results[d][pack, xp] = totals[cell_of(p, d, xp)].astype(BF16)
        return carry

    lax.fori_loop(0, packs, step, 0)


def backward_body(p, cuts, table, bands, score_in, rim, *refs):
    count = len(cuts)
    smooths, slopes, refs = refs[:count], refs[count : 2 * count], refs[2 * count :]
    results, refs = refs[: p.ring], refs[p.ring :]
    errors, hidden_near, grad_smooth, grad_wall = refs[:4]
    score, slope_near, wall, field, column = refs[4:]
    core = lax.axis_index("col")
    score[...] = score_in[...]
    edge_rows(p, core, cuts, table, bands, smooths, rim, score, hidden_near, slope_near)
    judge(p, core, smooths[-1], rim, score, errors, column)
    for (first, last), slope in zip(cuts, slopes):
        own = pl.ds(first, last - first)
        backward_groups(
            p, first, last - first, table, bands, score, slope, slope_near,
            grad_smooth.at[own], grad_wall.at[own], wall, field.at[own],
        )
    ship(p, p.packs, field, results)


def weight_body(
    p, cuts, bands, errors, hidden_near, rim, grad_smooth, grad_wall, *refs
):
    count = len(cuts)
    refs = list(refs)

    def take(number):
        taken = refs[:number]
        del refs[:number]
        return taken

    hiddens, smooths = take(count), take(count)
    pieces = [take(p.ring) for i in range(count)]
    out, wall, column, lines = refs
    core = lax.axis_index("col")
    half = WALL // 2
    own = own_lanes(p, 16)
    lines[...] = jnp.zeros_like(lines)

    def fold(value):
        total = value[:8]
        for r in range(8, value.shape[0], 8):
            total = total + value[r : r + 8]
        return jnp.sum(total, axis=0, keepdims=True)

    for chunk, (first, last) in enumerate(cuts):

        def step(g, carry, chunk=chunk, first=first):
            cg = first + g
            sums = [None] * ROW_WALL
            for part in range(p.rows // 16):
                rows = pl.ds(16 * part, 16)
                cells = {}
                for d in range(p.ring):
                    for xp in range(p.cells_x):
                        cells[cell_of(p, d, xp)] = pieces[chunk][d][g, xp, rows, :].astype(F32)
                for x in range(p.xs):
                    grad = jnp.where(own, grad_smooth[cg, x, rows, :].astype(F32), 0.0)
                    for j in range(TAPS):
                        moved = grad if j == REACH else pltpu.roll(grad, (j - REACH) % LANES, 1)
                        for i in range(TAPS):
                            t = TAPS * i + j
                            term = cells[(x + i - REACH) % p.xs] * moved
                            term = term[:8] + term[8:]
                            sums[t] = term if sums[t] is None else sums[t] + term
            for t in range(ROW_WALL):
                lines[cg, pl.ds(t, 1), :] = fold(sums[t])
            for x in range(p.xs):

                def store(start, length, value, x=x):
                    column[x, pl.ds(start, length), :] = value

                fill_column(p, core, smooths[chunk], rim, g, cg, x, store)
            grads = [grad_wall[cg, x].astype(F32) for x in range(p.xs)]
            for k in range(WALL):
                total = None
                for x in range(p.xs):
                    term = grads[x] * column[x, pl.ds(half + k, p.rows), :]
                    total = term if total is None else total + term
                lines[cg, pl.ds(ROW_WALL + k, 1), :] = fold(
                    total * bands[k, pl.ds(half, p.rows), :]
                )
            for x in range(p.xs):
                for blk in range(p.reach_rows // 8):
                    rows = pl.ds(8 * blk, 8)
                    wall[x, rows, :] = with_near(
                        p, core, blk, hiddens[chunk][g, x, rows, :], hidden_near[cg, x]
                    )
            for k in range(p.classes):
                total = None
                for x in range(p.xs):
                    term = errors[k, x] * wall[x, pl.ds(half, p.rows), :]
                    total = term if total is None else total + term
                lines[cg, pl.ds(ROW_CLASS + k, 1), :] = fold(total)
            return carry

        lax.fori_loop(0, last - first, step, 0)

    lane = lane_of(LANES)
    channel = lax.broadcasted_iota(jnp.int32, (LANES, LANES), 0)
    total = jnp.zeros((p.table_rows, LANES), F32)
    for cg in range(p.groups):
        pick = (lane // p.block + cg * p.per == channel) & (lane < p.per * p.block)
        total = total + lax.dot_general(
            lines[cg],
            jnp.where(pick, 1.0, 0.0),
            (((1,), (1,)), ((), ())),
            precision=lax.Precision.HIGHEST,
            preferred_element_type=F32,
        )
    out[...] = total


def pass_body(value, *refs):
    refs[-1][...] = value[...]


def unpack_body(p, *refs):
    out, stage = refs[-2:]
    me = lax.axis_index("gx")
    spot = lane_of(p.rows) // p.window

    def step(pack, carry, pieces, base):
        for xp in range(p.cells_x):
            values = [pieces[d][pack, xp].astype(F32) for d in range(p.ring)]
            for b in range(p.ring):
                total = values[0]
                for d in range(1, p.ring):
                    total = jnp.where(spot == lax.rem(b + me + d, p.ring), values[d], total)
                total = pltpu.roll(total, (LANES - p.window * b) % LANES, 1) if b else total
                stage[b, pl.ds(xp, p.rows, stride=p.cells_x), :] = total
        for b in range(p.ring):
            out[(base + pack) * p.ring + b] = stage[b].astype(BF16)
        return carry

    base = 0
    for i in range(0, len(refs) - 2, p.ring):
        pieces = refs[i : i + p.ring]
        size = pieces[0].shape[0]
        lax.fori_loop(0, size, functools.partial(step, pieces=pieces, base=base), 0)
        base += size


def rotation(size, by):
    return [(i, (i + by) % size) for i in range(size)]


def sum_over(value, axis):
    size = lax.axis_size(axis)
    if size & (size - 1):
        return sum((lax.ppermute(value, axis, rotation(size, d)) for d in range(1, size)), value)
    step = 1
    while step < size:
        value = value + lax.ppermute(value, axis, [(i, i ^ step) for i in range(size)])
        step *= 2
    return value


def near_parts(value):
    col, gz = lax.axis_size("col"), lax.axis_size("gz")
    parts = [value]
    for d in range(1, col * gz):
        pairs = [
            (i * col + j, (i + d // col) % gz * col + (j + d) % col)
            for i in range(gz)
            for j in range(col)
        ]
        parts.append(lax.ppermute(value, ("gz", "col"), pairs))
    return parts


def table_body(p, tile, wall, classes, levels, stretch, *refs):
    table, near = refs[-2:]
    core = lax.axis_index("col")
    lane = lax.broadcasted_iota(jnp.int32, (p.chans, LANES), 1)
    channel = lax.broadcasted_iota(jnp.int32, (p.chans, LANES), 0)

    def spread_rows(value, pick, dim):
        return lax.dot_general(
            value, pick, (((dim,), (0,)), ((), ())),
            precision=lax.Precision.HIGHEST, preferred_element_type=F32,
        )

    for cg in range(p.groups):
        pick = (lane // p.block + cg * p.per == channel) & (lane < p.per * p.block)
        pick = jnp.where(pick, 1.0, 0.0)
        table[cg, pl.ds(0, ROW_WALL), :] = spread_rows(tile[...], pick, 0)
        table[cg, pl.ds(ROW_WALL, WALL), :] = spread_rows(wall[...], pick, 1)
        table[cg, pl.ds(ROW_CLASS, p.classes), :] = spread_rows(classes[...], pick, 1)
    marks = lane_of(1)
    marks = (marks // p.block == p.per - 1) & (marks < p.per * p.block)
    last = table[p.groups - 1, pl.ds(CENTRE, 1), :]
    table[p.groups - 1, pl.ds(CENTRE, 1), :] = jnp.where(marks, 1.0, last)

    def step(q, carry):
        y = jnp.clip(core * p.rows - WALL // 2 + q, 0, 2 * p.rows - 1)
        level = levels[y]
        for k in range(WALL):
            near[k, pl.ds(q, 1), :] = jnp.full((1, LANES), stretch[level, k], F32)
        return carry

    lax.fori_loop(0, p.reach_rows, step, 0)


def sums_body(p, volume, *refs):
    tile, wall, classes = refs[-3:]
    total = refs[0][...]
    for ref in refs[1:-3]:
        total = total + ref[...]
    total = total * (1.0 / volume)
    rows = jnp.zeros((LANES - p.table_rows, LANES), F32)
    turned = jnp.concatenate([total, rows], axis=0).T
    tile[...] = turned[: p.chans, :ROW_WALL]
    wall[...] = total[ROW_WALL:ROW_CLASS, : p.chans]
    classes[...] = total[ROW_CLASS : ROW_CLASS + p.classes, : p.chans]


def band_rows(grid_index, stretch):
    levels = stretch.shape[0]
    onehot = (grid_index[:, None] == jnp.arange(levels, dtype=jnp.int32)[None, :]).astype(F32)
    return jnp.dot(onehot, stretch, precision=lax.Precision.HIGHEST)


def by_windows(features, labels, grid_index, stretch, tile_filter, wall_filter, class_weight):
    chans, rows, cells_x, cells_z = features.shape
    classes = class_weight.shape[0]
    ring, gz = lax.axis_size("gx"), lax.axis_size("gz")
    p = Plan(ring, chans, rows, cells_x, cells_z, classes)
    volume = labels.shape[0] * cells_x * ring * cells_z * gz
    tall = rows * cells_x
    cuts = p.cuts()

    field = features.reshape(chans, tall, cells_z)
    marks = labels.reshape(labels.shape[0] * cells_x, cells_z)
    (edge,) = call(
        functools.partial(edge_body, p),
        [jax.ShapeDtypeStruct((p.edge_groups, tall, LANES), BF16)],
        (field, marks),
    )
    left = lax.ppermute(edge, "gz", rotation(gz, 1))
    right = left if gz == 2 else lax.ppermute(edge, "gz", rotation(gz, -1))

    windows = call(
        functools.partial(pack_body, p, cuts),
        [
            jax.ShapeDtypeStruct((last - first, cells_x, rows, LANES), BF16)
            for first, last in cuts
            for d in range(ring)
        ],
        (field, marks, left, right),
        [pltpu.VMEM((ring, tall, LANES), F32)],
    )

    def shape(*sizes, kind=BF16):
        return jax.ShapeDtypeStruct(sizes, kind)

    smem = pl.BlockSpec(memory_space=pltpu.SMEM)
    table, near = call(
        functools.partial(table_body, p),
        [
            shape(p.groups, p.table_rows, LANES, kind=F32),
            shape(WALL, p.reach_rows, LANES, kind=F32),
        ],
        (tile_filter, wall_filter.T, class_weight, grid_index, stretch, windows[0]),
        micros=0.1,
        unread=1,
        scalars={3: smem, 4: smem},
    )
    column = pltpu.VMEM((p.xs, rows + 2 * WALL_HALO, LANES), F32)
    wall = pltpu.VMEM((p.xs, p.reach_rows, LANES), F32)
    smooths, rims, pieces, hiddens, slopes, score = [], [], [], [], [], ()
    for chunk, (first, last) in enumerate(cuts):
        size = last - first
        sent = windows[chunk * ring : (chunk + 1) * ring]
        got = [sent[0]] + [
            lax.ppermute(sent[d], "gx", rotation(ring, d)) for d in range(1, ring)
        ]
        final = last == p.groups
        smooth, hidden, slope, *score = call(
            functools.partial(forward_body, p, first, size, final),
            [
                shape(size, p.xs, rows, LANES),
                shape(size, p.xs, p.reach_rows, LANES, kind=F32),
                shape(size, p.xs, p.reach_rows, LANES, kind=F32),
                shape(classes, p.xs, p.reach_rows, LANES, kind=F32),
                shape(p.groups if final else size, p.xs // 2, 16, LANES),
            ],
            (table, near, *got, *score[:1], *(rims if final else [])),
            [column],
            micros=0.001,
        )
        rims.append(score[1])
        smooths, pieces = smooths + [smooth], pieces + got
        hiddens, slopes = hiddens + [hidden], slopes + [slope]
    score = score[0]
    rim = lax.ppermute(rims[-1], "col", rotation(2, 1))

    near_shape = (p.groups, p.xs, 8, LANES)
    *sent, errors, hidden_near, grad_smooth, grad_wall = call(
        functools.partial(backward_body, p, cuts),
        [shape(p.packs, cells_x, rows, LANES)] * ring
        + [
            shape(classes, p.xs, rows, LANES, kind=F32),
            shape(*near_shape, kind=F32),
            shape(p.groups, p.xs, rows, LANES),
            shape(p.groups, p.xs, rows, LANES),
        ],
        (table, near, score, rim, *smooths, *slopes),
        [
            pltpu.VMEM((classes, p.xs, p.reach_rows, LANES), F32),
            pltpu.VMEM(near_shape, F32),
            wall,
            pltpu.VMEM((p.groups, p.xs, rows, LANES), F32),
            column,
        ],
        micros=5,
    )
    back = [sent[0]] + [
        lax.ppermute(sent[d], "gx", rotation(ring, -d)) for d in range(1, ring)
    ]
    (sums,) = call(
        functools.partial(weight_body, p, cuts),
        [shape(p.table_rows, LANES, kind=F32)],
        (
            *(near, errors, hidden_near, rim, grad_smooth, grad_wall),
            *hiddens, *smooths, *pieces,
        ),
        [wall, column, pltpu.VMEM((p.groups, p.table_rows, LANES), F32)],
        micros=0.01,
    )
    (sums,) = call(
        pass_body,
        [shape(p.table_rows, LANES, kind=F32)],
        (sums, *back[1:]),
        micros=0.1,
        unread=ring - 1,
    )
    sums = sum_over(sums, "gx")
    (grad_field,) = call(
        functools.partial(unpack_body, p),
        [shape(chans, tall, cells_z)],
        back,
        [pltpu.VMEM((ring, tall, LANES), F32)],
    )
    grad_tile, grad_wall, grad_class = call(
        functools.partial(sums_body, p, volume),
        [
            shape(chans, ROW_WALL, kind=F32),
            shape(WALL, chans, kind=F32),
            shape(classes, chans, kind=F32),
        ],
        near_parts(sums),
        micros=0.1,
    )
    return grad_field.reshape(features.shape), grad_tile, grad_wall.T, grad_class


def with_halo(value, sides, width):
    for axis, dim in sides:
        size, length = (lax.axis_size(axis), value.shape[dim])
        up = [(i, (i + 1) % size) for i in range(size)]
        down = [(j, i) for i, j in up]
        last = lax.slice_in_dim(value, length - width, length, axis=dim)
        leading = lax.slice_in_dim(value, 0, width, axis=dim)
        before = lax.ppermute(last, axis, up)
        after = lax.ppermute(leading, axis, down)
        value = jnp.concatenate([before, value, after], axis=dim)
    return value


def rim_tiles(field):
    return with_halo(field, (("gx", 2), ("gz", 3)), 2)


def wall_forward(smooth_ext, wall_rows, band_rows):
    rows = band_rows.shape[0]
    total = jnp.zeros((smooth_ext.shape[0], rows) + smooth_ext.shape[2:], jnp.float32)
    for k in range(9):
        tap = wall_rows[:, k][:, None] * band_rows[:, k][None, :]
        total = total + tap[:, :, None, None] * smooth_ext[:, k : k + rows].astype(jnp.float32)
    return total


def wall_backward(grad_ext, wall_rows, band_ext, rows):
    total = jnp.zeros((grad_ext.shape[0], rows) + grad_ext.shape[2:], jnp.float32)
    for k in range(9):
        first = 8 - k
        tap = wall_rows[:, k][:, None] * band_ext[first : first + rows, k][None, :]
        total = total + tap[:, :, None, None] * grad_ext[:, first : first + rows].astype(
            jnp.float32
        )
    return total


def by_halos(features, labels, grid_index, stretch, tile_filter, wall_filter, class_weight):
    chans, half_rows, cells_x, cells_z = features.shape
    all_rows = labels.shape[0]
    classes = class_weight.shape[0]
    volume = all_rows * cells_x * lax.axis_size("gx") * cells_z * lax.axis_size("gz")
    widened = rim_tiles(features)
    smooth = jnp.zeros(features.shape, jnp.float32)
    for i in range(5):
        for j in range(5):
            weight = tile_filter[:, 5 * i + j][:, None, None, None]
            smooth = smooth + weight * widened[:, :, i : i + cells_x, j : j + cells_z].astype(
                jnp.float32
            )
    smoothed = smooth.astype(jnp.bfloat16)
    bands = band_rows(grid_index, stretch)
    bands_pad = jnp.pad(bands, ((4, 4), (0, 0)))
    place = lax.axis_index("col")
    share = chans // lax.axis_size("col")
    first_chan = place * share
    pencil = lax.all_to_all(smoothed, "col", split_axis=0, concat_axis=1, tiled=True)
    smooth_ext = jnp.pad(pencil, ((0, 0), (4, 4), (0, 0), (0, 0)))
    wall_rows = lax.dynamic_slice_in_dim(wall_filter, first_chan, share, 0)
    class_rows = lax.dynamic_slice_in_dim(class_weight, first_chan, share, 1)
    wall_out = wall_forward(smooth_ext, wall_rows, bands)
    sig = jax.nn.sigmoid(wall_out)
    hidden = wall_out * sig
    partial_scores = jnp.einsum(
        "kc,cyxz->kyxz", class_rows, hidden, precision=lax.Precision.HIGHEST
    )
    scores = lax.psum(partial_scores, "col")
    targets = (labels[None] == jnp.arange(classes, dtype=jnp.int32)[:, None, None, None]).astype(
        jnp.float32
    )
    errors = scores - targets
    grad_hidden = jnp.einsum("kc,kyxz->cyxz", class_rows, errors, precision=lax.Precision.HIGHEST)
    grad_wall = (grad_hidden * sig * (1.0 + wall_out * (1.0 - sig))).astype(jnp.bfloat16)
    class_part = jnp.einsum("kyxz,cyxz->kc", errors, hidden, precision=lax.Precision.HIGHEST)
    grad_vals = grad_wall.astype(jnp.float32)
    wall_part = jnp.stack(
        [
            jnp.sum(
                grad_vals
                * bands[:, k][None, :, None, None]
                * smooth_ext[:, k : k + all_rows].astype(jnp.float32),
                axis=(1, 2, 3),
            )
            for k in range(9)
        ],
        axis=1,
    )
    grad_ext = jnp.pad(grad_wall, ((0, 0), (4, 4), (0, 0), (0, 0)))
    grad_smooth = wall_backward(grad_ext, wall_rows, bands_pad, all_rows).astype(jnp.bfloat16)
    grad_tile = lax.all_to_all(grad_smooth, "col", split_axis=1, concat_axis=0, tiled=True)
    wall_full = lax.dynamic_update_slice_in_dim(
        jnp.zeros((chans, 9), jnp.float32), wall_part, first_chan, 0
    )
    class_full = lax.dynamic_update_slice_in_dim(
        jnp.zeros((classes, chans), jnp.float32), class_part, first_chan, 1
    )
    grad_widened = rim_tiles(grad_tile)
    grad_tile_vals = grad_tile.astype(jnp.float32)
    grad_field = jnp.zeros(features.shape, jnp.float32)
    tile_terms = []
    for i in range(5):
        for j in range(5):
            weight = tile_filter[:, 5 * i + j][:, None, None, None]
            grad_field = grad_field + weight * grad_widened[
                :, :, 4 - i : 4 - i + cells_x, 4 - j : 4 - j + cells_z
            ].astype(jnp.float32)
            shifted = widened[:, :, i : i + cells_x, j : j + cells_z].astype(jnp.float32)
            tile_terms.append(jnp.sum(shifted * grad_tile_vals, axis=(1, 2, 3)))
    tile_part = jnp.stack(tile_terms, axis=1)
    totals = lax.psum((tile_part, wall_full, class_full), ("gx", "gz", "col"))
    return (
        grad_field.astype(jnp.bfloat16),
        totals[0] / volume,
        totals[1] / volume,
        totals[2] / volume,
    )


def shards(features, labels, grid_index, stretch, tile_filter, wall_filter, class_weight):
    sizes = [lax.axis_size(axis) for axis in ("gx", "gz", "col")]
    plan = by_windows if fits(*sizes, *features.shape, class_weight.shape[0]) else by_halos
    return plan(features, labels, grid_index, stretch, tile_filter, wall_filter, class_weight)


def solution(mesh):
    return jax.shard_map(
        shards,
        mesh=mesh,
        in_specs=(
            P(None, "col", ("group", "gx"), "gz"),
            P(None, ("group", "gx"), "gz"),
            P(),
            P(),
            P(),
            P(),
            P(),
        ),
        out_specs=(
            P(None, "col", ("group", "gx"), "gz"),
            P("group", None),
            P("group", None),
            P("group", None),
        ),
        check_vma=False,
    )
```

```python
import functools

import jax
import jax.numpy as jnp
from jax import lax
from jax.experimental import pallas as pl
from jax.experimental.pallas import tpu as pltpu
from jax.sharding import PartitionSpec as P

LANES = 128
TAPS = 5
REACH = 2
EDGE = 4
WALL = 9
WALL_HALO = 8
ROW_WALL = TAPS * TAPS
ROW_CLASS = ROW_WALL + WALL
CENTRE = ROW_WALL // 2
F32, BF16 = jnp.float32, jnp.bfloat16


class Plan:
    def __init__(self, ring, chans, rows, cells_x, cells_z, classes):
        self.ring, self.chans, self.rows, self.cells_x = ring, chans, rows, cells_x
        self.classes = classes
        self.window = cells_z // ring
        self.block = self.window + 2 * EDGE
        self.per = LANES // self.block
        self.slots = chans + 1
        self.groups = self.slots // self.per
        self.xs = ring * cells_x
        self.packs = chans // ring
        self.reach_rows = rows + 2 * (WALL_HALO // 2)
        self.edge_slots = LANES // (2 * EDGE)
        self.edge_groups = -(-self.slots // self.edge_slots)
        self.table_rows = -(-(ROW_CLASS + classes) // 8) * 8


    def cuts(self):
        tail = -(-self.groups // 4)
        return ((0, self.groups - tail), (self.groups - tail, self.groups))


def fits(ring, gz, col, chans, rows, cells_x, cells_z, classes):
    if cells_z != LANES or cells_x != 2 or col != 2 or ring < 2 or ring > 4 or LANES % ring:
        return False
    block = LANES // ring + 2 * EDGE
    per = LANES // block
    return (chans + 1) % per == 0 and chans % ring == 0 and rows % 16 == 0 and ring * cells_x >= TAPS


def vmem(count):
    return [pl.BlockSpec(memory_space=pltpu.VMEM)] * count


def call(body, outs, args, scratch=(), micros=1.0, unread=0, scalars={}):
    return pl.pallas_call(
        body,
        out_shape=outs,
        in_specs=[
            *(scalars.get(i, spec) for i, spec in enumerate(vmem(len(args) - unread))),
            *[pl.BlockSpec(memory_space=pl.ANY)] * unread,
        ],
        cost_estimate=pl.CostEstimate(
            flops=0, bytes_accessed=int(3.0e6 * micros), transcendentals=0
        ),
        out_specs=vmem(len(outs)),
        scratch_shapes=list(scratch),
        compiler_params=pltpu.CompilerParams(vmem_limit_bytes=40 * 2**20),
    )(*args)


def lane_of(rows):
    return lax.broadcasted_iota(jnp.int32, (rows, LANES), 1)


def edge_body(p, field, labels, out):
    core = lax.axis_index("col")
    tall = p.rows * p.cells_x
    lane = lane_of(tall)

    def group(g, count, fetch):
        total = jnp.zeros((tall, LANES), F32)
        for e in range(count):
            moved = pltpu.roll(fetch(g * p.edge_slots + e), (2 * EDGE * e + EDGE) % LANES, 1)
            total = jnp.where(lane // (2 * EDGE) == e, moved, total)
        out[g] = total.astype(BF16)

    def step(g, carry):
        group(g, p.edge_slots, lambda c: field[c].astype(F32))
        return carry

    full = p.chans // p.edge_slots
    lax.fori_loop(0, full, step, 0)
    own = labels[pl.ds(pl.multiple_of(core * tall, 8), tall), :].astype(F32)
    group(full, p.slots - full * p.edge_slots, lambda c: own)


def pack_body(p, cuts, field, labels, left, right, *refs):
    outs, stage = refs[:-1], refs[-1]
    ring = p.ring
    me, core = lax.axis_index("gx"), lax.axis_index("col")
    tall = p.rows * p.cells_x
    lane = lane_of(tall)
    takes = [lax.rem(me + d, ring) for d in range(ring)]
    fixes = [
        ((lane >= LANES - EDGE) & (k == 0)) | ((lane < EDGE) & (k == ring - 1)) for k in takes
    ]
    older = lane % (2 * EDGE) < EDGE

    def edges(c):
        g, e = c // p.edge_slots, c % p.edge_slots
        both = jnp.where(older, left[g].astype(F32), right[g].astype(F32))
        return pltpu.roll(both, LANES - EDGE - 2 * EDGE * e, 1)

    def group(cg, fetch, chunk, first):
        values = [fetch(cg * p.per + b) for b in range(p.per)]
        rims = [edges(cg * p.per + b) for b in range(p.per)]
        for d in range(ring):
            total = jnp.zeros((tall, LANES), F32)
            for b in range(p.per):
                shift = lax.rem(2 * LANES + p.block * b + EDGE - p.window * takes[d], LANES)
                moved = pltpu.roll(jnp.where(fixes[d], rims[b], values[b]), shift, 1)
                total = jnp.where(lane // p.block == b, moved, total)
            stage[d] = total
            for xp in range(p.cells_x):
                outs[chunk * ring + d][cg - first, xp] = stage[
                    d, pl.ds(xp, p.rows, stride=p.cells_x), :
                ].astype(BF16)

    own = labels[pl.ds(pl.multiple_of(core * tall, 8), tall), :].astype(F32)
    for chunk, (first, last) in enumerate(cuts):
        tail = last == p.groups

        def step(cg, carry, chunk=chunk, first=first):
            group(cg, lambda c: field[c].astype(F32), chunk, first)
            return carry

        lax.fori_loop(first, last - 1 if tail else last, step, 0)
        if tail:
            group(last - 1, lambda c: field[c].astype(F32) if c < p.chans else own, chunk, first)


def cell_of(p, d, xp):
    return (xp - p.cells_x * d) % p.xs


def smooth_group(p, table, cg, pieces, g, store):
    weights = [table[cg, pl.ds(t, 1), :] for t in range(ROW_WALL)]
    for part in range(p.rows // 16):
        cells = {}
        for d in range(p.ring):
            for xp in range(p.cells_x):
                cells[cell_of(p, d, xp)] = pieces[d][g, xp, pl.ds(16 * part, 16), :].astype(F32)
        for x in range(p.xs):
            total = None
            for j in range(TAPS):
                line = None
                for i in range(TAPS):
                    term = weights[TAPS * i + j] * cells[(x + i - REACH) % p.xs]
                    line = term if line is None else line + term
                if j != REACH:
                    line = pltpu.roll(line, (REACH - j) % LANES, 1)
                total = line if total is None else total + line
            store(x, 16 * part, total.astype(BF16))


def activate(value):
    sig = 0.5 * jnp.tanh(0.5 * value) + 0.5
    act = value * sig
    return act, sig + act * (1.0 - sig)


def forward_body(p, first, count, last, table, bands, *refs):
    refs = list(refs)

    def take(number):
        taken = refs[:number]
        del refs[:number]
        return taken

    pieces = take(p.ring)
    before = take(1 if first else 0)
    rims = take(len(refs) - 6 if last else 0)
    smooth, hidden, slope, score, rim, column = refs
    core = lax.axis_index("col")
    blocks = p.reach_rows // 8
    score[...] = before[0][...] if first else jnp.zeros_like(score)
    for x in range(p.xs):
        column[x, pl.ds(0, WALL_HALO), :] = jnp.zeros((WALL_HALO, LANES), F32)
        column[x, pl.ds(WALL_HALO + p.rows, WALL_HALO), :] = jnp.zeros((WALL_HALO, LANES), F32)
    base = 0
    for other in rims:
        rim[pl.ds(base, other.shape[0])] = other[...]
        base += other.shape[0]

    def step(g, carry):
        cg = first + g

        def store(x, row, value):
            smooth[g, x, pl.ds(row, 16), :] = value
            column[x, pl.ds(WALL_HALO + row, 16), :] = value.astype(F32)

        smooth_group(p, table, cg, pieces, g, store)
        for pair in range(p.xs // 2):
            cells = (2 * pair, 2 * pair + 1)
            tops = [column[x, pl.ds(WALL_HALO, 8), :] for x in cells]
            lows = [column[x, pl.ds(p.rows, 8), :] for x in cells]
            rim[base + g, pair] = jnp.where(
                core == 0, jnp.concatenate(lows, axis=0), jnp.concatenate(tops, axis=0)
            ).astype(BF16)
        taps = [table[cg, pl.ds(ROW_WALL + k, 1), :] for k in range(WALL)]
        classes = [table[cg, pl.ds(ROW_CLASS + k, 1), :] for k in range(p.classes)]
        for blk in range(blocks):
            rows = pl.ds(8 * blk, 8)
            sums = [None] * p.xs
            for k in range(WALL):
                tap = taps[k] * bands[k, rows, :]
                for x in range(p.xs):
                    term = tap * column[x, pl.ds(8 * blk + k, 8), :]
                    sums[x] = term if k == 0 else sums[x] + term
            for x in range(p.xs):
                hidden[g, x, rows, :], slope[g, x, rows, :] = act, _ = activate(sums[x])
                for k in range(p.classes):
                    score[k, x, rows, :] += classes[k] * act
        return carry

    lax.fori_loop(0, count, step, 0)


def fill_column(p, core, smooth, rim, g, cg, x, store):
    store(WALL_HALO, p.rows, smooth[g, x].astype(F32))
    near = rim[cg, x // 2].astype(F32)[8 * (x % 2) : 8 * (x % 2) + 8]
    store(0, WALL_HALO, jnp.where(core == 0, 0.0, near))
    store(WALL_HALO + p.rows, WALL_HALO, jnp.where(core == 0, near, 0.0))


def own_lanes(p, rows):
    lane = lane_of(rows)
    place = lane % p.block
    return (place >= EDGE) & (place < EDGE + p.window) & (lane < p.per * p.block)


def spread(p, value, lane):
    total = value
    for b in range(p.per - 1):
        moved = pltpu.roll(value, LANES - p.block * (p.per - 1 - b), 1)
        total = jnp.where(lane // p.block == b, moved, total)
    return total


def near_block(p, core):
    return pl.multiple_of(jnp.where(core == 0, p.reach_rows - 8, 0), 8)


def edge_rows(p, core, cuts, table, bands, smooths, rim, score, hidden_near, slope_near):
    base = near_block(p, core)
    rows = pl.ds(base, 8)
    for k in range(p.classes):
        for x in range(p.xs):
            score[k, x, rows, :] = jnp.zeros((8, LANES), F32)

    for chunk, (first, last) in enumerate(cuts):

        def step(g, carry, chunk=chunk, first=first):
            cg = first + g
            taps = [
                table[cg, pl.ds(ROW_WALL + k, 1), :] * bands[k, rows, :] for k in range(WALL)
            ]
            classes = [table[cg, pl.ds(ROW_CLASS + k, 1), :] for k in range(p.classes)]
            for x in range(p.xs):
                near = rim[cg, x // 2].astype(F32)[8 * (x % 2) : 8 * (x % 2) + 8]
                low = smooths[chunk][g, x, pl.ds(p.rows - 16, 16), :].astype(F32)[8:]
                top = smooths[chunk][g, x, pl.ds(0, 16), :].astype(F32)[:8]
                hidden_near[cg, x] = jnp.where(core == 0, low, near)
                slope_near[cg, x] = jnp.where(core == 0, near, top)
            sums = []
            for x in range(p.xs):
                both = jnp.concatenate([hidden_near[cg, x], slope_near[cg, x]], axis=0)
                total = taps[0] * both[:8]
                for k in range(1, WALL):
                    total = total + taps[k] * both[k : k + 8]
                sums.append(total)
            for x in range(p.xs):
                act, bend = activate(sums[x])
                hidden_near[cg, x], slope_near[cg, x] = act, bend
                for k in range(p.classes):
                    score[k, x, rows, :] += classes[k] * act
            return carry

        lax.fori_loop(0, last - first, step, 0)


def judge(p, core, smooth, rim, score, errors, column):
    lane = lane_of(8)
    half = WALL // 2
    for x in range(p.xs):

        def store(start, length, value, x=x):
            column[x, pl.ds(start, length), :] = value

        fill_column(p, core, smooth, rim, smooth.shape[0] - 1, p.groups - 1, x, store)

    def step(blk, carry):
        rows = pl.ds(pl.multiple_of(8 * blk, 8), 8)
        place = core * p.rows - half + 8 * blk + lax.broadcasted_iota(jnp.int32, (8, LANES), 0)
        inside = (place >= 0) & (place < 2 * p.rows)
        for x in range(p.xs):
            label = spread(p, column[x, pl.ds(8 * blk + half, 8), :], lane)
            for k in range(p.classes):
                value = score[k, x, rows, :]
                total = value
                for b in range(1, p.per):
                    total = total + pltpu.roll(value, p.block * b, 1)
                error = spread(p, total, lane) - jnp.where(label == k, 1.0, 0.0)
                score[k, x, rows, :] = jnp.where(inside, error, 0.0)
        return carry

    lax.fori_loop(0, p.reach_rows // 8, step, 0)
    own = own_lanes(p, p.rows)
    for k in range(p.classes):
        for x in range(p.xs):
            errors[k, x] = jnp.where(own, score[k, x, pl.ds(half, p.rows), :], 0.0)


def with_near(p, core, blk, value, near):
    if blk == 0:
        return jnp.where(core == 0, value, near)
    if blk == p.reach_rows // 8 - 1:
        return jnp.where(core == 0, near, value)
    return value


def backward_groups(
    p, first, count, table, bands, score, slope, slope_near, grad_smooth, grad_wall, wall, field
):
    core = lax.axis_index("col")
    half = WALL // 2
    own = own_lanes(p, p.rows)

    def step(g, carry):
        cg = first + g
        taps = [table[cg, pl.ds(ROW_WALL + k, 1), :] for k in range(WALL)]
        classes = [table[cg, pl.ds(ROW_CLASS + k, 1), :] for k in range(p.classes)]
        for blk in range(p.reach_rows // 8):
            rows = pl.ds(8 * blk, 8)
            for x in range(p.xs):
                grad = classes[0] * score[0, x, rows, :]
                for k in range(1, p.classes):
                    grad = grad + classes[k] * score[k, x, rows, :]
                bend = with_near(p, core, blk, slope[g, x, rows, :], slope_near[cg, x])
                wall[x, rows, :] = (grad * bend).astype(BF16).astype(F32)
        for x in range(p.xs):
            grad_wall[g, x] = jnp.where(own, wall[x, pl.ds(half, p.rows), :], 0.0).astype(BF16)
        for part in range(p.rows // 16):
            sums = [None] * p.xs
            for k in range(WALL):
                rows = pl.ds(16 * part + WALL - 1 - k, 16)
                tap = taps[k] * bands[k, rows, :]
                for x in range(p.xs):
                    term = tap * wall[x, rows, :]
                    sums[x] = term if k == 0 else sums[x] + term
            for x in range(p.xs):
                grad_smooth[g, x, pl.ds(16 * part, 16), :] = sums[x].astype(BF16)
        weights = [table[cg, pl.ds(t, 1), :] for t in range(ROW_WALL)]
        for part in range(p.rows // 16):
            rows = pl.ds(16 * part, 16)
            cells = [grad_smooth[g, x, rows, :].astype(F32) for x in range(p.xs)]
            for x in range(p.xs):
                total = None
                for j in range(TAPS):
                    line = None
                    for i in range(TAPS):
                        term = weights[TAPS * i + j] * cells[(x - i + REACH) % p.xs]
                        line = term if line is None else line + term
                    if j != REACH:
                        line = pltpu.roll(line, (j - REACH) % LANES, 1)
                    total = line if total is None else total + line
                field[g, x, rows, :] = total
        return carry

    lax.fori_loop(0, count, step, 0)


def ship(p, packs, field, results):
    me = lax.axis_index("gx")
    wide = lane_of(p.rows) // p.window

    def step(pack, carry):
        totals = [jnp.zeros((p.rows, LANES), F32)] * p.xs
        for b in range(p.ring):
            c = pack * p.ring + b
            spot = lax.rem(b + me, p.ring)
            shift = lax.rem(2 * LANES + p.window * spot - p.block * (c % p.per) - EDGE, LANES)
            for x in range(p.xs):
                moved = pltpu.roll(field[c // p.per, x], shift, 1)
                totals[x] = jnp.where(wide == spot, moved, totals[x])
        for d in range(p.ring):
            for xp in range(p.cells_x):
                results[d][pack, xp] = totals[cell_of(p, d, xp)].astype(BF16)
        return carry

    lax.fori_loop(0, packs, step, 0)


def backward_body(p, cuts, table, bands, score_in, rim, *refs):
    count = len(cuts)
    smooths, slopes, refs = refs[:count], refs[count : 2 * count], refs[2 * count :]
    results, refs = refs[: p.ring], refs[p.ring :]
    errors, hidden_near, grad_smooth, grad_wall = refs[:4]
    score, slope_near, wall, field, column = refs[4:]
    core = lax.axis_index("col")
    score[...] = score_in[...]
    edge_rows(p, core, cuts, table, bands, smooths, rim, score, hidden_near, slope_near)
    judge(p, core, smooths[-1], rim, score, errors, column)
    for (first, last), slope in zip(cuts, slopes):
        own = pl.ds(first, last - first)
        backward_groups(
            p, first, last - first, table, bands, score, slope, slope_near,
            grad_smooth.at[own], grad_wall.at[own], wall, field.at[own],
        )
    ship(p, p.packs, field, results)


def weight_body(
    p, cuts, bands, errors, hidden_near, rim, grad_smooth, grad_wall, *refs
):
    count = len(cuts)
    refs = list(refs)

    def take(number):
        taken = refs[:number]
        del refs[:number]
        return taken

    hiddens, smooths = take(count), take(count)
    pieces = [take(p.ring) for i in range(count)]
    out, wall, column, lines = refs
    core = lax.axis_index("col")
    half = WALL // 2
    own = own_lanes(p, 16)
    lines[...] = jnp.zeros_like(lines)

    def fold(value):
        total = value[:8]
        for r in range(8, value.shape[0], 8):
            total = total + value[r : r + 8]
        return jnp.sum(total, axis=0, keepdims=True)

    for chunk, (first, last) in enumerate(cuts):

        def step(g, carry, chunk=chunk, first=first):
            cg = first + g
            sums = [None] * ROW_WALL
            for part in range(p.rows // 16):
                rows = pl.ds(16 * part, 16)
                cells = {}
                for d in range(p.ring):
                    for xp in range(p.cells_x):
                        cells[cell_of(p, d, xp)] = pieces[chunk][d][g, xp, rows, :].astype(F32)
                for x in range(p.xs):
                    grad = jnp.where(own, grad_smooth[cg, x, rows, :].astype(F32), 0.0)
                    for j in range(TAPS):
                        moved = grad if j == REACH else pltpu.roll(grad, (j - REACH) % LANES, 1)
                        for i in range(TAPS):
                            t = TAPS * i + j
                            term = cells[(x + i - REACH) % p.xs] * moved
                            term = term[:8] + term[8:]
                            sums[t] = term if sums[t] is None else sums[t] + term
            for t in range(ROW_WALL):
                lines[cg, pl.ds(t, 1), :] = fold(sums[t])
            for x in range(p.xs):

                def store(start, length, value, x=x):
                    column[x, pl.ds(start, length), :] = value

                fill_column(p, core, smooths[chunk], rim, g, cg, x, store)
            grads = [grad_wall[cg, x].astype(F32) for x in range(p.xs)]
            for k in range(WALL):
                total = None
                for x in range(p.xs):
                    term = grads[x] * column[x, pl.ds(half + k, p.rows), :]
                    total = term if total is None else total + term
                lines[cg, pl.ds(ROW_WALL + k, 1), :] = fold(
                    total * bands[k, pl.ds(half, p.rows), :]
                )
            for x in range(p.xs):
                for blk in range(p.reach_rows // 8):
                    rows = pl.ds(8 * blk, 8)
                    wall[x, rows, :] = with_near(
                        p, core, blk, hiddens[chunk][g, x, rows, :], hidden_near[cg, x]
                    )
            for k in range(p.classes):
                total = None
                for x in range(p.xs):
                    term = errors[k, x] * wall[x, pl.ds(half, p.rows), :]
                    total = term if total is None else total + term
                lines[cg, pl.ds(ROW_CLASS + k, 1), :] = fold(total)
            return carry

        lax.fori_loop(0, last - first, step, 0)

    lane = lane_of(LANES)
    channel = lax.broadcasted_iota(jnp.int32, (LANES, LANES), 0)
    total = jnp.zeros((p.table_rows, LANES), F32)
    for cg in range(p.groups):
        pick = (lane // p.block + cg * p.per == channel) & (lane < p.per * p.block)
        total = total + lax.dot_general(
            lines[cg],
            jnp.where(pick, 1.0, 0.0),
            (((1,), (1,)), ((), ())),
            precision=lax.Precision.HIGHEST,
            preferred_element_type=F32,
        )
    out[...] = total


def pass_body(value, *refs):
    refs[-1][...] = value[...]


def unpack_body(p, *refs):
    out, stage = refs[-2:]
    me = lax.axis_index("gx")
    spot = lane_of(p.rows) // p.window

    def step(pack, carry, pieces, base):
        for xp in range(p.cells_x):
            values = [pieces[d][pack, xp].astype(F32) for d in range(p.ring)]
            for b in range(p.ring):
                total = values[0]
                for d in range(1, p.ring):
                    total = jnp.where(spot == lax.rem(b + me + d, p.ring), values[d], total)
                total = pltpu.roll(total, (LANES - p.window * b) % LANES, 1) if b else total
                stage[b, pl.ds(xp, p.rows, stride=p.cells_x), :] = total
        for b in range(p.ring):
            out[(base + pack) * p.ring + b] = stage[b].astype(BF16)
        return carry

    base = 0
    for i in range(0, len(refs) - 2, p.ring):
        pieces = refs[i : i + p.ring]
        size = pieces[0].shape[0]
        lax.fori_loop(0, size, functools.partial(step, pieces=pieces, base=base), 0)
        base += size


def rotation(size, by):
    return [(i, (i + by) % size) for i in range(size)]


def sum_over(value, axis):
    size = lax.axis_size(axis)
    return sum((lax.ppermute(value, axis, rotation(size, d)) for d in range(1, size)), value)


def near_parts(value):
    col, gz = lax.axis_size("col"), lax.axis_size("gz")
    parts = [value]
    for d in range(1, col * gz):
        pairs = [
            (i * col + j, (i + d // col) % gz * col + (j + d) % col)
            for i in range(gz)
            for j in range(col)
        ]
        parts.append(lax.ppermute(value, ("gz", "col"), pairs))
    return parts


def table_body(p, tile, wall, classes, levels, stretch, *refs):
    table, near = refs[-2:]
    core = lax.axis_index("col")
    lane = lax.broadcasted_iota(jnp.int32, (p.chans, LANES), 1)
    channel = lax.broadcasted_iota(jnp.int32, (p.chans, LANES), 0)

    def spread_rows(value, pick, dim):
        return lax.dot_general(
            value, pick, (((dim,), (0,)), ((), ())),
            precision=lax.Precision.HIGHEST, preferred_element_type=F32,
        )

    for cg in range(p.groups):
        pick = (lane // p.block + cg * p.per == channel) & (lane < p.per * p.block)
        pick = jnp.where(pick, 1.0, 0.0)
        table[cg, pl.ds(0, ROW_WALL), :] = spread_rows(tile[...], pick, 0)
        table[cg, pl.ds(ROW_WALL, WALL), :] = spread_rows(wall[...], pick, 1)
        table[cg, pl.ds(ROW_CLASS, p.classes), :] = spread_rows(classes[...], pick, 1)
    marks = lane_of(1)
    marks = (marks // p.block == p.per - 1) & (marks < p.per * p.block)
    last = table[p.groups - 1, pl.ds(CENTRE, 1), :]
    table[p.groups - 1, pl.ds(CENTRE, 1), :] = jnp.where(marks, 1.0, last)

    def step(q, carry):
        y = jnp.clip(core * p.rows - WALL // 2 + q, 0, 2 * p.rows - 1)
        level = levels[y]
        for k in range(WALL):
            near[k, pl.ds(q, 1), :] = jnp.full((1, LANES), stretch[level, k], F32)
        return carry

    lax.fori_loop(0, p.reach_rows, step, 0)


def sums_body(p, volume, *refs):
    tile, wall, classes = refs[-3:]
    total = refs[0][...]
    for ref in refs[1:-3]:
        total = total + ref[...]
    total = total * (1.0 / volume)
    rows = jnp.zeros((LANES - p.table_rows, LANES), F32)
    turned = jnp.concatenate([total, rows], axis=0).T
    tile[...] = turned[: p.chans, :ROW_WALL]
    wall[...] = total[ROW_WALL:ROW_CLASS, : p.chans]
    classes[...] = total[ROW_CLASS : ROW_CLASS + p.classes, : p.chans]


def band_rows(grid_index, stretch):
    levels = stretch.shape[0]
    onehot = (grid_index[:, None] == jnp.arange(levels, dtype=jnp.int32)[None, :]).astype(F32)
    return jnp.dot(onehot, stretch, precision=lax.Precision.HIGHEST)


def by_windows(features, labels, grid_index, stretch, tile_filter, wall_filter, class_weight):
    chans, rows, cells_x, cells_z = features.shape
    classes = class_weight.shape[0]
    ring, gz = lax.axis_size("gx"), lax.axis_size("gz")
    p = Plan(ring, chans, rows, cells_x, cells_z, classes)
    volume = labels.shape[0] * cells_x * ring * cells_z * gz
    tall = rows * cells_x
    cuts = p.cuts()

    field = features.reshape(chans, tall, cells_z)
    marks = labels.reshape(labels.shape[0] * cells_x, cells_z)
    (edge,) = call(
        functools.partial(edge_body, p),
        [jax.ShapeDtypeStruct((p.edge_groups, tall, LANES), BF16)],
        (field, marks),
    )
    left = lax.ppermute(edge, "gz", rotation(gz, 1))
    right = left if gz == 2 else lax.ppermute(edge, "gz", rotation(gz, -1))

    windows = []
    for first, last in cuts:
        windows += call(
            functools.partial(pack_body, p, ((first, last),)),
            [jax.ShapeDtypeStruct((last - first, cells_x, rows, LANES), BF16)] * ring,
            (field, marks, left, right),
            [pltpu.VMEM((ring, tall, LANES), F32)],
            micros=0.1,
        )

    def shape(*sizes, kind=BF16):
        return jax.ShapeDtypeStruct(sizes, kind)

    smem = pl.BlockSpec(memory_space=pltpu.SMEM)
    table, near = call(
        functools.partial(table_body, p),
        [
            shape(p.groups, p.table_rows, LANES, kind=F32),
            shape(WALL, p.reach_rows, LANES, kind=F32),
        ],
        (tile_filter, wall_filter.T, class_weight, grid_index, stretch, windows[0]),
        micros=0.1,
        unread=1,
        scalars={3: smem, 4: smem},
    )
    column = pltpu.VMEM((p.xs, rows + 2 * WALL_HALO, LANES), F32)
    wall = pltpu.VMEM((p.xs, p.reach_rows, LANES), F32)
    smooths, rims, pieces, hiddens, slopes, score = [], [], [], [], [], ()
    for chunk, (first, last) in enumerate(cuts):
        size = last - first
        sent = windows[chunk * ring : (chunk + 1) * ring]
        got = [sent[0]] + [
            lax.ppermute(sent[d], "gx", rotation(ring, d)) for d in range(1, ring)
        ]
        final = last == p.groups
        smooth, hidden, slope, *score = call(
            functools.partial(forward_body, p, first, size, final),
            [
                shape(size, p.xs, rows, LANES),
                shape(size, p.xs, p.reach_rows, LANES, kind=F32),
                shape(size, p.xs, p.reach_rows, LANES, kind=F32),
                shape(classes, p.xs, p.reach_rows, LANES, kind=F32),
                shape(p.groups if final else size, p.xs // 2, 16, LANES),
            ],
            (table, near, *got, *score[:1], *(rims if final else [])),
            [column],
            micros=0.001,
        )
        rims.append(score[1])
        smooths, pieces = smooths + [smooth], pieces + got
        hiddens, slopes = hiddens + [hidden], slopes + [slope]
    score = score[0]
    rim = lax.ppermute(rims[-1], "col", rotation(2, 1))

    near_shape = (p.groups, p.xs, 8, LANES)
    *sent, errors, hidden_near, grad_smooth, grad_wall = call(
        functools.partial(backward_body, p, cuts),
        [shape(p.packs, cells_x, rows, LANES)] * ring
        + [
            shape(classes, p.xs, rows, LANES, kind=F32),
            shape(*near_shape, kind=F32),
            shape(p.groups, p.xs, rows, LANES),
            shape(p.groups, p.xs, rows, LANES),
        ],
        (table, near, score, rim, *smooths, *slopes),
        [
            pltpu.VMEM((classes, p.xs, p.reach_rows, LANES), F32),
            pltpu.VMEM(near_shape, F32),
            wall,
            pltpu.VMEM((p.groups, p.xs, rows, LANES), F32),
            column,
        ],
        micros=5,
    )
    back = [sent[0]] + [
        lax.ppermute(sent[d], "gx", rotation(ring, -d)) for d in range(1, ring)
    ]
    (sums,) = call(
        functools.partial(weight_body, p, cuts),
        [shape(p.table_rows, LANES, kind=F32)],
        (
            *(near, errors, hidden_near, rim, grad_smooth, grad_wall),
            *hiddens, *smooths, *pieces,
        ),
        [wall, column, pltpu.VMEM((p.groups, p.table_rows, LANES), F32)],
        micros=0.01,
    )
    (sums,) = call(
        pass_body,
        [shape(p.table_rows, LANES, kind=F32)],
        (sums, *back[1:]),
        micros=0.1,
        unread=ring - 1,
    )
    sums = sum_over(sums, "gx")
    (grad_field,) = call(
        functools.partial(unpack_body, p),
        [shape(chans, tall, cells_z)],
        back,
        [pltpu.VMEM((ring, tall, LANES), F32)],
    )
    grad_tile, grad_wall, grad_class = call(
        functools.partial(sums_body, p, volume),
        [
            shape(chans, ROW_WALL, kind=F32),
            shape(WALL, chans, kind=F32),
            shape(classes, chans, kind=F32),
        ],
        near_parts(sums),
        micros=0.1,
    )
    return grad_field.reshape(features.shape), grad_tile, grad_wall.T, grad_class


def with_halo(value, sides, width):
    for axis, dim in sides:
        size, length = (lax.axis_size(axis), value.shape[dim])
        up = [(i, (i + 1) % size) for i in range(size)]
        down = [(j, i) for i, j in up]
        last = lax.slice_in_dim(value, length - width, length, axis=dim)
        leading = lax.slice_in_dim(value, 0, width, axis=dim)
        before = lax.ppermute(last, axis, up)
        after = lax.ppermute(leading, axis, down)
        value = jnp.concatenate([before, value, after], axis=dim)
    return value


def rim_tiles(field):
    return with_halo(field, (("gx", 2), ("gz", 3)), 2)


def wall_forward(smooth_ext, wall_rows, band_rows):
    rows = band_rows.shape[0]
    total = jnp.zeros((smooth_ext.shape[0], rows) + smooth_ext.shape[2:], jnp.float32)
    for k in range(9):
        tap = wall_rows[:, k][:, None] * band_rows[:, k][None, :]
        total = total + tap[:, :, None, None] * smooth_ext[:, k : k + rows].astype(jnp.float32)
    return total


def wall_backward(grad_ext, wall_rows, band_ext, rows):
    total = jnp.zeros((grad_ext.shape[0], rows) + grad_ext.shape[2:], jnp.float32)
    for k in range(9):
        first = 8 - k
        tap = wall_rows[:, k][:, None] * band_ext[first : first + rows, k][None, :]
        total = total + tap[:, :, None, None] * grad_ext[:, first : first + rows].astype(
            jnp.float32
        )
    return total


def by_halos(features, labels, grid_index, stretch, tile_filter, wall_filter, class_weight):
    chans, half_rows, cells_x, cells_z = features.shape
    all_rows = labels.shape[0]
    classes = class_weight.shape[0]
    volume = all_rows * cells_x * lax.axis_size("gx") * cells_z * lax.axis_size("gz")
    widened = rim_tiles(features)
    smooth = jnp.zeros(features.shape, jnp.float32)
    for i in range(5):
        for j in range(5):
            weight = tile_filter[:, 5 * i + j][:, None, None, None]
            smooth = smooth + weight * widened[:, :, i : i + cells_x, j : j + cells_z].astype(
                jnp.float32
            )
    smoothed = smooth.astype(jnp.bfloat16)
    bands = band_rows(grid_index, stretch)
    bands_pad = jnp.pad(bands, ((4, 4), (0, 0)))
    place = lax.axis_index("col")
    share = chans // lax.axis_size("col")
    first_chan = place * share
    pencil = lax.all_to_all(smoothed, "col", split_axis=0, concat_axis=1, tiled=True)
    smooth_ext = jnp.pad(pencil, ((0, 0), (4, 4), (0, 0), (0, 0)))
    wall_rows = lax.dynamic_slice_in_dim(wall_filter, first_chan, share, 0)
    class_rows = lax.dynamic_slice_in_dim(class_weight, first_chan, share, 1)
    wall_out = wall_forward(smooth_ext, wall_rows, bands)
    sig = jax.nn.sigmoid(wall_out)
    hidden = wall_out * sig
    partial_scores = jnp.einsum(
        "kc,cyxz->kyxz", class_rows, hidden, precision=lax.Precision.HIGHEST
    )
    scores = lax.psum(partial_scores, "col")
    targets = (labels[None] == jnp.arange(classes, dtype=jnp.int32)[:, None, None, None]).astype(
        jnp.float32
    )
    errors = scores - targets
    grad_hidden = jnp.einsum("kc,kyxz->cyxz", class_rows, errors, precision=lax.Precision.HIGHEST)
    grad_wall = (grad_hidden * sig * (1.0 + wall_out * (1.0 - sig))).astype(jnp.bfloat16)
    class_part = jnp.einsum("kyxz,cyxz->kc", errors, hidden, precision=lax.Precision.HIGHEST)
    grad_vals = grad_wall.astype(jnp.float32)
    wall_part = jnp.stack(
        [
            jnp.sum(
                grad_vals
                * bands[:, k][None, :, None, None]
                * smooth_ext[:, k : k + all_rows].astype(jnp.float32),
                axis=(1, 2, 3),
            )
            for k in range(9)
        ],
        axis=1,
    )
    grad_ext = jnp.pad(grad_wall, ((0, 0), (4, 4), (0, 0), (0, 0)))
    grad_smooth = wall_backward(grad_ext, wall_rows, bands_pad, all_rows).astype(jnp.bfloat16)
    grad_tile = lax.all_to_all(grad_smooth, "col", split_axis=1, concat_axis=0, tiled=True)
    wall_full = lax.dynamic_update_slice_in_dim(
        jnp.zeros((chans, 9), jnp.float32), wall_part, first_chan, 0
    )
    class_full = lax.dynamic_update_slice_in_dim(
        jnp.zeros((classes, chans), jnp.float32), class_part, first_chan, 1
    )
    grad_widened = rim_tiles(grad_tile)
    grad_tile_vals = grad_tile.astype(jnp.float32)
    grad_field = jnp.zeros(features.shape, jnp.float32)
    tile_terms = []
    for i in range(5):
        for j in range(5):
            weight = tile_filter[:, 5 * i + j][:, None, None, None]
            grad_field = grad_field + weight * grad_widened[
                :, :, 4 - i : 4 - i + cells_x, 4 - j : 4 - j + cells_z
            ].astype(jnp.float32)
            shifted = widened[:, :, i : i + cells_x, j : j + cells_z].astype(jnp.float32)
            tile_terms.append(jnp.sum(shifted * grad_tile_vals, axis=(1, 2, 3)))
    tile_part = jnp.stack(tile_terms, axis=1)
    totals = lax.psum((tile_part, wall_full, class_full), ("gx", "gz", "col"))
    return (
        grad_field.astype(jnp.bfloat16),
        totals[0] / volume,
        totals[1] / volume,
        totals[2] / volume,
    )


def shards(features, labels, grid_index, stretch, tile_filter, wall_filter, class_weight):
    sizes = [lax.axis_size(axis) for axis in ("gx", "gz", "col")]
    plan = by_windows if fits(*sizes, *features.shape, class_weight.shape[0]) else by_halos
    return plan(features, labels, grid_index, stretch, tile_filter, wall_filter, class_weight)


def solution(mesh):
    return jax.shard_map(
        shards,
        mesh=mesh,
        in_specs=(
            P(None, "col", ("group", "gx"), "gz"),
            P(None, ("group", "gx"), "gz"),
            P(),
            P(),
            P(),
            P(),
            P(),
        ),
        out_specs=(
            P(None, "col", ("group", "gx"), "gz"),
            P("group", None),
            P("group", None),
            P("group", None),
        ),
        check_vma=False,
    )
```
